256 devices in a mesh: grp: 32 (over y, z_hi, core), tp: 8 (over x, z_lo).
Axes of the slice: x: 4, y: 4, z: 8 (z_hi: 4, z_lo: 2; z = z_hi * 2 + z_lo), core: 2. Of those that a mesh axis runs over, the one named last changes fastest.
Arguments:
- pool_pages: bfloat16 [32, 48, 128, 576], P('grp', 'tp'), may hold values from -6 to 6
- page_table: int32 [32, 48], replicated, may hold values from 0 to 47, each once within a row
- read_list: int32 [32, 4], replicated, may hold values from 0 to 31, as said below
- context: int32 [384], P('grp'), may hold values from 1 to 6144, as said below
- queries: bfloat16 [384, 4, 64, 576], P('grp', None, 'tp')
- tail_keys: bfloat16 [384, 4, 576], P('grp')
- residual: bfloat16 [384, 4, 3584], P('grp')
- w_uv: bfloat16 [64, 512, 128], P('tp'), may hold values from -0.25 to 0.25
- w_out: bfloat16 [8192, 3584], P('tp'), may hold values from -0.0625 to 0.0625
- norm_gain: float32 [3584], replicated, may hold values from 0.1 to 1.9
- w_gate: bfloat16 [3584, 1024], P(None, 'tp'), may hold values from -0.09375 to 0.09375
- w_up: bfloat16 [3584, 1024], P(None, 'tp'), may hold values from -0.09375 to 0.09375
- w_down: bfloat16 [1024, 3584], P('tp'), may hold values from -0.1875 to 0.1875
Outputs:
- layer_out: bfloat16 [384, 4, 3584], P('grp', None, 'tp')
The draws below stay inside these ranges and needn't reach their ends.
Inputs may be any that keep to these rules, and one draw needn't show every extreme that they name: `read_list`: row g names 4 different prefixes; each column names every prefix once. `page_table`: each row names every logical page once. `context`: some request has the full length 6144.
All inputs are finite; a program needn't handle non-finite values.
Results may differ from the reference program's by a relative error of at most 0.02.
Values may be sent and summed in bfloat16 or wider, within the bound.
A program may use at most 128 MiB of HBM per device.

```python
import jax
import jax.numpy as jnp
from jax import lax

D = 3584
HEADS = 64
LATENT = 512
ROPE = 64
KVW = 576
VDIM = 128
FF = 1024
PAGE = 128
PAGES = 48
READS = 4
ROWS_SLOT = 3
DRAFT = 4
ROWS = 12
PREFIXES = 32
REQUESTS = 384


def shared_latents(key):
    key_width = LATENT + ROPE
    key_one = jax.random.fold_in(key, 0)
    array_shape = (REQUESTS, DRAFT, key_width)
    gaussian = jax.random.normal(key_one, array_shape, jnp.float32)
    tail_rows = gaussian
    prior_rope = tail_rows[:, DRAFT - 2, LATENT:]
    tail_rows = tail_rows.at[:, DRAFT - 2, LATENT:].set(prior_rope)
    return tail_rows


def draw_tail_keys(key, part):
    tail_rows = shared_latents(key)
    return tail_rows.astype(jnp.bfloat16)


def draw_queries(key, part):
    tie_share = 0.0
    tail_rows = shared_latents(key)
    key = jax.random.fold_in(key, 11)
    key_one = jax.random.fold_in(key, 0)
    key_three = jax.random.fold_in(key, 2)
    key_width = LATENT + ROPE
    array_shape = (REQUESTS, DRAFT, HEADS, key_width)
    gaussian = jax.random.normal(key_one, array_shape, jnp.float32)
    base_rows = 1.15 * gaussian + 0.2 * tail_rows[:, :, None, :]
    picked = jax.random.randint(key_three, (REQUESTS, HEADS), 0, 4) == 0
    chosen = tie_share * picked.astype(jnp.float32)
    last_rows = base_rows[:, DRAFT - 1] * (1.0 - chosen[:, :, None])
    base_rows = base_rows.at[:, DRAFT - 1].set(last_rows)
    return base_rows.astype(jnp.bfloat16)


def draw_residual(key, part):
    key = jax.random.fold_in(key, 5)
    key_two = jax.random.fold_in(key, 1)
    column_ramp = 3.0 ** (jnp.arange(D, dtype=jnp.float32) / D)
    array_shape = (REQUESTS, DRAFT, D)
    base_rows = jax.random.normal(key_two, array_shape, jnp.float32)
    return (0.4 * base_rows * column_ramp).astype(jnp.bfloat16)


def draw_read_list(key, part):
    key = jax.random.fold_in(key, 3)
    key_one, key_two, key_three = jax.random.split(key, 3)
    relabel = jax.random.permutation(key_one, PREFIXES)
    row_offsets = jax.random.permutation(key_two, PREFIXES)
    slot_steps = jax.random.permutation(key_three, PREFIXES)[:READS]
    table_index = (row_offsets[:, None] + slot_steps[None, :]) % PREFIXES
    return relabel[table_index].astype(jnp.int32)


def draw_context(key, part):
    key = jax.random.fold_in(key, 7)
    key_one, key_two, key_three, key_four = jax.random.split(key, 4)
    full_length = PAGES * PAGE
    group_high = jax.random.randint(key_one, (PREFIXES,), full_length // 8, full_length + 1)
    full_group = jax.random.randint(key_two, (), 0, PREFIXES)
    group_high = jnp.where(jnp.arange(PREFIXES) == full_group, full_length, group_high)
    lengths = jax.random.randint(key_three, (PREFIXES, ROWS), 1, group_high[:, None] + 1)
    longest = jax.random.randint(key_four, (PREFIXES,), 0, ROWS)
    lengths = jnp.where(jnp.arange(ROWS)[None, :] == longest[:, None], group_high[:, None], lengths)
    return lengths.reshape(PREFIXES * ROWS).astype(jnp.int32)


def steps_of(key, shape, cuts, least, largest):
    factor_of, own = 1.0, jax.random.fold_in(key, 6)
    for dim, parts in cuts:
        draws = jnp.exp(jax.random.uniform(jax.random.fold_in(own, dim), (parts,), jnp.float32, least / len(cuts), largest / len(cuts)))
        factor_of = factor_of * jnp.repeat(draws, shape[dim] // parts).reshape([-1 if axis == dim else 1 for axis in range(len(shape))])
    return factor_of


def scatter_about(own_key, dims, scale, limit, shards=(), kind=jnp.bfloat16):
    gain = steps_of(own_key, dims, shards, -0.22, 0.18) if shards else 1.0
    drawn = jax.random.normal(own_key, dims, jnp.float32) * scale * gain
    return jnp.minimum(jnp.maximum(drawn, -limit), limit).astype(kind)


def setup_inputs(seed: int = 0) -> dict:
    arg_keys = jax.random.split(jax.random.key(seed), 14)
    pool_pages = scatter_about(arg_keys[0], (PREFIXES, PAGES, PAGE, KVW), 1.0, 6.0, ((0, 32), (1, 8)))
    page_table = jax.vmap(lambda own: jax.random.permutation(own, PAGES))(jax.random.split(arg_keys[1], PREFIXES)).reshape((PREFIXES, PAGES)).astype(jnp.int32)
    read_list = draw_read_list(jax.random.fold_in(arg_keys[13], 71), 0)
    context = draw_context(jax.random.fold_in(arg_keys[13], 71), 0)
    queries = draw_queries(jax.random.fold_in(arg_keys[13], 71), 0)
    tail_keys = draw_tail_keys(jax.random.fold_in(arg_keys[13], 71), 0)
    residual = draw_residual(jax.random.fold_in(arg_keys[13], 71), 0)
    w_uv = scatter_about(arg_keys[7], (HEADS, LATENT, VDIM), LATENT ** -0.5, 0.25, ((0, 8),))
    w_out = scatter_about(arg_keys[8], (HEADS * VDIM, D), (HEADS * VDIM) ** -0.5, 0.0625, ((0, 8),))
    norm_gain = jnp.clip(1.0 + 0.18 * jax.random.normal(arg_keys[9], (D,), jnp.float32), 0.1, 1.9)
    w_gate = scatter_about(arg_keys[10], (D, FF), D ** -0.5, 0.09375, ((1, 8),))
    w_up = scatter_about(arg_keys[11], (D, FF), D ** -0.5, 0.09375, ((1, 8),))
    w_down = scatter_about(arg_keys[12], (FF, D), FF ** -0.5, 0.1875, ((0, 8),))
    return dict(pool_pages=pool_pages, page_table=page_table, read_list=read_list, context=context, queries=queries, tail_keys=tail_keys, residual=residual, w_uv=w_uv, w_out=w_out, norm_gain=norm_gain, w_gate=w_gate, w_up=w_up, w_down=w_down)


SCALE = 192.0 ** (-0.5)
NEGATIVE = -1e+30
EPSILON = 1e-06

def reference(pool_pages, page_table, read_list, context, queries, tail_keys, residual, w_uv, w_out, norm_gain, w_gate, w_up, w_down):
    key_width = LATENT + ROPE
    row_count = READS * ROWS_SLOT
    query_all = queries.reshape(PREFIXES, READS, ROWS_SLOT, DRAFT, HEADS, key_width)
    tail_all = tail_keys.reshape(PREFIXES, READS, ROWS_SLOT, DRAFT, key_width)
    length_all = context.reshape(PREFIXES, READS, ROWS_SLOT)
    resid_all = residual.reshape(PREFIXES, row_count * DRAFT, D)
    causal = jnp.arange(DRAFT)[None, :] <= jnp.arange(DRAFT)[:, None]
    offsets = jnp.arange(PAGE, dtype=jnp.int32)
    uv_wide = w_uv.astype(jnp.float32)

    def one_group(packed):
        prefix_ids, query_block, tail_block, length_block, resid_block = packed
        key_block = jnp.take(pool_pages, prefix_ids, axis=0).astype(jnp.float32)
        logical = jnp.take(page_table, prefix_ids, axis=0)
        position = logical[:, :, None] * PAGE + offsets[None, None, :]
        visible = position[:, None] < length_block[:, :, None, None]
        query_wide = query_block.astype(jnp.float32)
        tail_wide = tail_block.astype(jnp.float32)
        scores = jnp.einsum('krshc,kjtc->krshjt', query_wide, key_block) * SCALE
        scores = jnp.where(visible[:, :, None, None], scores, NEGATIVE)
        tail_scores = jnp.einsum('krshc,krzc->krshz', query_wide, tail_wide) * SCALE
        tail_scores = jnp.where(causal[None, None, :, None, :], tail_scores, NEGATIVE)
        row_top = jnp.maximum(lax.optimization_barrier(jnp.max(scores, axis=(4, 5))), lax.optimization_barrier(jnp.max(tail_scores, axis=4)))
        weights = lax.optimization_barrier(jnp.exp(scores - row_top[..., None, None]).astype(jnp.bfloat16)).astype(jnp.float32)
        tail_weights = lax.optimization_barrier(jnp.exp(tail_scores - row_top[..., None]).astype(jnp.bfloat16)).astype(jnp.float32)
        denominator = lax.optimization_barrier(jnp.sum(weights, axis=(4, 5))) + lax.optimization_barrier(jnp.sum(tail_weights, axis=4))
        numerator = jnp.einsum('krshjt,kjtc->krshc', weights, key_block[..., :LATENT])
        numerator = numerator + jnp.einsum('krshz,krzc->krshc', tail_weights, tail_wide[..., :LATENT])
        latent_out = (numerator / denominator[..., None]).astype(jnp.bfloat16)
        head_out = jnp.einsum('krshl,hlv->krshv', latent_out.astype(jnp.float32), uv_wide).astype(jnp.bfloat16)
        flat_heads = head_out.reshape(row_count * DRAFT, HEADS * VDIM)
        mixed = jnp.dot(flat_heads, w_out, preferred_element_type=jnp.float32)
        hidden = resid_block.astype(jnp.float32) + mixed
        mean_square = lax.optimization_barrier(jnp.mean(hidden * hidden, axis=-1, keepdims=True))
        normed = (hidden * lax.rsqrt(mean_square + EPSILON) * norm_gain).astype(jnp.bfloat16)
        gate_value = jnp.dot(normed, w_gate, preferred_element_type=jnp.float32)
        up_value = jnp.dot(normed, w_up, preferred_element_type=jnp.float32)
        activated = (jax.nn.silu(gate_value) * up_value).astype(jnp.bfloat16)
        return (hidden + jnp.dot(activated, w_down, preferred_element_type=jnp.float32)).astype(jnp.bfloat16)
    layer_rows = lax.map(one_group, (read_list, query_all, tail_all, length_all, resid_all))
    return layer_rows.reshape(PREFIXES * row_count, DRAFT, D)
```

```python
import functools

import jax
import jax.numpy as jnp
import numpy as np
from jax import lax
from jax.experimental import pallas as pl
from jax.experimental.pallas import tpu as pltpu
from jax.sharding import PartitionSpec as P

LATENT = 512
SCALE = 192.0 ** (-0.5)
SCALE2 = SCALE * 1.4426950408889634
NEGATIVE = -1e30
EPSILON = 1e-06
MESH = pl.DeviceIdType.MESH
F32 = jnp.float32
BF16 = jnp.bfloat16

GROUPS = 32
QP = 24
EP = 6
NP = QP + EP
WIDE = 640
SLAB = 448
SLABW = 512
ROWS = 48
NT = (((1,), (1,)), ((), ()))


def drain(ref, sem):
    pltpu.make_async_copy(ref, ref, sem).wait()


def iota(shape, dim):
    return lax.broadcasted_iota(jnp.int32, shape, dim)


def kernel(
    inv_ref,
    retk_ref,
    reads_ref,
    send_ref,
    pos_ref,
    gain_ref,
    pool_ref,
    wuv_hbm,
    wout_hbm,
    wgate_hbm,
    wup_hbm,
    wdown_hbm,
    out_ref,
    h1,
    s2,
    q1,
    q2,
    kbuf,
    acc_own,
    acc_peer,
    top,
    den,
    numer_out,
    numer_in,
    lse_out,
    lse_in,
    latent,
    flatm,
    wuv,
    wout,
    wgate,
    wup,
    wdown,
    mix,
    rs1,
    agout,
    ag,
    rs2,
    fin,
    sback,
    rback,
    wsem,
    ksend,
    krecv,
    hsend,
    hrecv,
    zsend,
    zrecv,
    tsend,
    trecv,
):
    g = lax.axis_index("grp")
    t = lax.axis_index("tp")
    x, z = t // 2, t % 2
    right = lax.rem(x + 1, 4)
    left = lax.rem(x + 3, 4)
    across = lax.rem(x + 2, 4)
    right_t = right * 2 + z
    left_t = left * 2 + z
    peer_t = x * 2 + (1 - z)

    barrier = pltpu.get_barrier_semaphore()

    @pl.loop(1, GROUPS)
    def _(d):
        pl.semaphore_signal(
            barrier, inc=1, device_id={"grp": lax.rem(g + d, GROUPS)}, device_id_type=MESH
        )

    @pl.loop(1, 8)
    def _(d):
        pl.semaphore_signal(
            barrier, inc=1, device_id={"tp": lax.rem(t + d, 8)}, device_id_type=MESH
        )

    own_keys = pltpu.make_async_copy(pool_ref, kbuf.at[x], wsem.at[0])
    own_keys.start()
    weights = [
        pltpu.make_async_copy(wuv_hbm, wuv, wsem.at[1]),
        pltpu.make_async_copy(wout_hbm, wout, wsem.at[2]),
        pltpu.make_async_copy(wgate_hbm, wgate, wsem.at[3]),
        pltpu.make_async_copy(wup_hbm, wup, wsem.at[4]),
        pltpu.make_async_copy(wdown_hbm, wdown, wsem.at[5]),
    ]
    for copy in weights:
        copy.start()

    @pl.when(g < NP)
    def _():
        h1[g] = send_ref[g]

    pl.semaphore_wait(barrier, GROUPS - 1 + 7)

    @pl.loop(1, GROUPS)
    def _(d):
        to = lax.rem(g + d, GROUPS)

        @pl.when(to < NP)
        def _():
            pltpu.make_async_remote_copy(
                src_ref=send_ref.at[to],
                dst_ref=h1.at[g],
                send_sem=hsend.at[0],
                recv_sem=hrecv.at[0],
                device_id={"grp": to},
                device_id_type=MESH,
            ).start()

    to_right = pltpu.make_async_remote_copy(
        src_ref=pool_ref,
        dst_ref=kbuf.at[x],
        send_sem=ksend.at[0],
        recv_sem=krecv.at[0],
        device_id={"tp": right_t},
        device_id_type=MESH,
    )
    to_left = pltpu.make_async_remote_copy(
        src_ref=pool_ref,
        dst_ref=kbuf.at[x],
        send_sem=ksend.at[1],
        recv_sem=krecv.at[1],
        device_id={"tp": left_t},
        device_id_type=MESH,
    )
    to_right.start()
    to_left.start()

    @pl.when(g < NP)
    def _():
        drain(h1.at[pl.ds(0, GROUPS - 1)], hrecv.at[0])
        kp = lax.rem(g, 2)
        upper = iota((16, WIDE), 0) < 8

        def picked(to):
            first = h1[inv_ref[2 * kp, to]]
            second = h1[inv_ref[2 * kp + 1, to]]
            return jnp.where(upper, first, second)

        @pl.loop(1, GROUPS)
        def _(d):
            to = lax.rem(g + d, GROUPS)
            s2[to] = picked(to)
            pltpu.make_async_remote_copy(
                src_ref=s2.at[to],
                dst_ref=q1.at[g],
                send_sem=hsend.at[1],
                recv_sem=hrecv.at[1],
                device_id={"grp": to},
                device_id_type=MESH,
            ).start()

        q1[g] = picked(g)

    to_right.wait_recv()
    on_right = pltpu.make_async_remote_copy(
        src_ref=kbuf.at[left, pl.ds(0, 3)],
        dst_ref=kbuf.at[left, pl.ds(0, 3)],
        send_sem=ksend.at[2],
        recv_sem=krecv.at[2],
        device_id={"tp": right_t},
        device_id_type=MESH,
    )
    on_right.start()
    to_left.wait_recv()
    on_left = pltpu.make_async_remote_copy(
        src_ref=kbuf.at[right, pl.ds(3, 3)],
        dst_ref=kbuf.at[right, pl.ds(3, 3)],
        send_sem=ksend.at[3],
        recv_sem=krecv.at[3],
        device_id={"tp": left_t},
        device_id_type=MESH,
    )
    on_left.start()

    @pl.when(g < NP)
    def _():
        drain(q1.at[pl.ds(0, NP - 1)], hrecv.at[1])

    @pl.when(g >= NP)
    def _():
        drain(q1.at[pl.ds(0, NP)], hrecv.at[1])

    swap = pltpu.make_async_remote_copy(
        src_ref=q1.at[pl.ds(0, QP)],
        dst_ref=q2,
        send_sem=zsend.at[0],
        recv_sem=zrecv.at[0],
        device_id={"tp": peer_t},
        device_id_type=MESH,
    )
    swap.start()

    own_keys.wait()
    on_right.wait_recv()
    on_left.wait_recv()

    nq = QP * 16

    def prefix_part(asked, acc):
        def block(b, carry):
            rows = asked[pl.ds(0, QP)].reshape(nq, WIDE)
            lengths = rows[:, 576:577].astype(F32) * 64.0 + rows[:, 608:609].astype(F32)
            keys = kbuf[b].reshape(768, 576)
            scores = lax.dot_general(rows[:, :576], keys, NT, preferred_element_type=F32)
            position = pos_ref[b * 2 + z]
            scores = jnp.where(position < lengths, scores * SCALE2, NEGATIVE)
            old = top[...]
            new = jnp.maximum(old, jnp.max(scores, axis=1, keepdims=True))
            weight = jnp.exp2(scores - new).astype(BF16)
            keep = jnp.exp2(old - new)
            top[...] = new
            den[...] = den[...] * keep + jnp.sum(weight.astype(F32), axis=1, keepdims=True)
            acc[...] = acc[...] * keep + jnp.dot(
                weight, keys[:, :LATENT], preferred_element_type=F32
            )
            return carry

        lax.fori_loop(0, 4, block, 0)

    rows = q1[pl.ds(0, QP)].reshape(nq, WIDE)
    extra = q1[pl.ds(QP, EP)].reshape(EP * 16, WIDE)
    nt = EP * 16
    scores = lax.dot_general(
        rows[:, :576], extra[:, :576], NT, preferred_element_type=F32
    )
    n, m = iota((nq, nt), 0), iota((nq, nt), 1)
    line = (m // 32) * 8 + m % 8
    seen = (line < 12) & (line // 4 == n // 128) & ((m // 8) % 4 == (n // 8) % 4)
    seen = seen & (line % 4 <= (n // 32) % 4)
    scores = jnp.where(seen, scores * SCALE2, NEGATIVE)
    first = jnp.max(scores, axis=1, keepdims=True)
    weight = jnp.where(seen, jnp.exp2(scores - first), 0.0).astype(BF16)
    top[...] = first
    den[...] = jnp.sum(weight.astype(F32), axis=1, keepdims=True)
    acc_own[...] = jnp.dot(weight, extra[:, :LATENT], preferred_element_type=F32)
    prefix_part(q1, acc_own)
    own_top = top[...]
    own_den = den[...]

    swap.wait_recv()
    top[...] = jnp.full((nq, 1), NEGATIVE, F32)
    den[...] = jnp.zeros((nq, 1), F32)
    acc_peer[...] = jnp.zeros_like(acc_peer)
    prefix_part(q2, acc_peer)
    numer_out[...] = (acc_peer[...] / den[...]).astype(BF16)
    lse = top[...] + jnp.log2(den[...])
    diagonal = iota((nq, nq), 0) == iota((nq, nq), 1)
    lse_out[...] = jnp.broadcast_to(
        jnp.sum(jnp.where(diagonal, lse, 0.0), axis=0, keepdims=True), (8, nq)
    )
    back = [
        pltpu.make_async_remote_copy(
            src_ref=numer_out,
            dst_ref=numer_in,
            send_sem=zsend.at[1],
            recv_sem=zrecv.at[1],
            device_id={"tp": peer_t},
            device_id_type=MESH,
        ),
        pltpu.make_async_remote_copy(
            src_ref=lse_out,
            dst_ref=lse_in,
            send_sem=zsend.at[2],
            recv_sem=zrecv.at[2],
            device_id={"tp": peer_t},
            device_id_type=MESH,
        ),
    ]
    for copy in back:
        copy.start()
    for copy in weights:
        copy.wait()
    for copy in back:
        copy.wait_recv()
    lse = jnp.sum(jnp.where(diagonal, lse_in[0:1, :], 0.0), axis=1, keepdims=True)
    both = jnp.maximum(own_top, lse)
    mine = jnp.exp2(own_top - both)
    theirs = jnp.exp2(lse - both)
    scaled = 1.0 / (own_den * mine + theirs)
    latent[...] = (
        acc_own[...] * (mine * scaled) + numer_in[...].astype(F32) * (theirs * scaled)
    ).astype(BF16)

    head_of = iota((nq, 128), 0) % 8
    for h in range(8):
        value = jnp.dot(latent[...], wuv[h], preferred_element_type=F32)
        flatm[:, h * 128 : (h + 1) * 128] = jnp.where(head_of == h, value, 0.0).astype(BF16)
    o, n = iota((ROWS, nq), 0), iota((ROWS, nq), 1)
    chosen = ((n // 32) == o % 12) & ((n // 8) % 4 == o // 12)
    flat = jnp.dot(
        jnp.where(chosen, 1.0, 0.0).astype(BF16), flatm[...], preferred_element_type=F32
    ).astype(BF16)

    def spread(part, dst, s):
        for d in range(1, 8):
            to = lax.rem(t + d, 8)
            pltpu.make_async_remote_copy(
                src_ref=part(to),
                dst_ref=dst.at[t],
                send_sem=tsend.at[s],
                recv_sem=trecv.at[s],
                device_id={"tp": to},
                device_id_type=MESH,
            ).start()

    def slabs(left_side, weight, dst):
        for j in range(4):
            wide = jnp.dot(
                left_side, weight[:, 896 * j : 896 * (j + 1)], preferred_element_type=F32
            ).astype(BF16)
            dst[2 * j, :, :SLAB] = wide[:, :SLAB]
            dst[2 * j + 1, :, :SLAB] = wide[:, SLAB:]

    mix[0, :, :, SLAB:] = jnp.zeros((8, ROWS, SLABW - SLAB), BF16)
    mix[1, :, :, SLAB:] = jnp.zeros((8, ROWS, SLABW - SLAB), BF16)
    slabs(flat, wout, mix.at[0])
    spread(lambda to: mix.at[0, to], rs1, 0)
    rs1[t] = mix[0, t]
    o, m = iota((ROWS, nt), 0), iota((ROWS, nt), 1)
    line = (m // 32) * 8 + m % 8
    chosen = (line - 12 == o % 12) & ((m // 8) % 4 == o // 12)
    hidden = jnp.dot(
        jnp.where(chosen, 1.0, 0.0).astype(BF16),
        extra[:, :SLABW],
        preferred_element_type=F32,
    )
    drain(rs1.at[pl.ds(0, 7)], trecv.at[0])
    for j in range(8):
        hidden = hidden + rs1[j].astype(F32)
    lane = iota((ROWS, SLABW), 1)
    hidden = jnp.where(lane < SLAB, hidden, 0.0)
    square = jnp.sum(hidden * hidden, axis=1, keepdims=True)
    high = square.astype(BF16).astype(F32)
    low = square - high
    packed = jnp.where(
        lane < SLAB, hidden * gain_ref[...], jnp.where(lane < SLAB + 32, high, low)
    ).astype(BF16)
    agout[...] = packed
    spread(lambda to: agout, ag, 1)
    ag[t] = packed
    drain(ag.at[pl.ds(0, 7)], trecv.at[1])
    total = jnp.zeros((ROWS, 1), F32)
    gate = jnp.zeros((ROWS, 128), F32)
    upward = jnp.zeros((ROWS, 128), F32)
    for j in range(8):
        block = ag[j]
        total = total + (
            block[:, SLAB : SLAB + 1].astype(F32) + block[:, SLAB + 32 : SLAB + 33].astype(F32)
        )
        at = slice(SLAB * j, SLAB * (j + 1))
        gate = gate + jnp.dot(block[:, :SLAB], wgate[at], preferred_element_type=F32)
        upward = upward + jnp.dot(block[:, :SLAB], wup[at], preferred_element_type=F32)
    factor = lax.rsqrt(total * (1.0 / 3584.0) + EPSILON)
    gate = gate * factor
    upward = upward * factor
    active = (gate / (1.0 + jnp.exp(-gate)) * upward).astype(BF16)
    slabs(active, wdown, mix.at[1])
    spread(lambda to: mix.at[1, to], rs2, 2)
    rs2[t] = mix[1, t]
    drain(rs2.at[pl.ds(0, 7)], trecv.at[2])
    for j in range(8):
        hidden = hidden + rs2[j].astype(F32)

    o, m = iota((64, ROWS), 0), iota((64, ROWS), 1)
    chosen = (o // 16 == m // 12) & (o % 16 == m % 12)
    fin[...] = (
        jnp.dot(
            jnp.where(chosen, 1.0, 0.0).astype(BF16),
            hidden.astype(BF16),
            preferred_element_type=F32,
        )
        .astype(BF16)
        .reshape(4, 16, SLABW)
    )

    @pl.loop(1, GROUPS)
    def _(d):
        to = lax.rem(g + d, GROUPS)
        sback[to] = fin[retk_ref[to]]
        pltpu.make_async_remote_copy(
            src_ref=sback.at[to],
            dst_ref=rback.at[g],
            send_sem=hsend.at[2],
            recv_sem=hrecv.at[2],
            device_id={"grp": to},
            device_id_type=MESH,
        ).start()

    rback[g] = fin[retk_ref[g]]
    drain(rback.at[pl.ds(0, GROUPS - 1)], hrecv.at[2])
    for k in range(4):
        out_ref[k] = rback[reads_ref[k]][:, :SLAB]

    @pl.when(g >= NP)
    def _():
        drain(send_ref.at[pl.ds(0, NP)], hsend.at[0])

    @pl.when(g < NP)
    def _():
        drain(send_ref.at[pl.ds(0, NP - 1)], hsend.at[0])
        drain(s2.at[pl.ds(0, GROUPS - 1)], hsend.at[1])

    drain(sback.at[pl.ds(0, GROUPS - 1)], hsend.at[2])
    to_right.wait_send()
    to_left.wait_send()
    on_right.wait_send()
    on_left.wait_send()
    swap.wait_send()
    for copy in back:
        copy.wait_send()
    for s in range(3):
        drain(rs1.at[pl.ds(0, 7)], tsend.at[s])


def on_device(
    pool_pages,
    page_table,
    read_list,
    context,
    queries,
    tail_keys,
    residual,
    w_uv,
    w_out,
    norm_gain,
    w_gate,
    w_up,
    w_down,
):
    g = lax.axis_index("grp")
    t = lax.axis_index("tp")
    asked = queries.reshape(4, 3, 4, 8, 576).transpose(1, 2, 0, 3, 4)
    marks = context.reshape(4, 3).T[:, None, :, None, None]
    marks = jnp.concatenate(
        [
            jnp.broadcast_to(marks // 64, (3, 4, 4, 8, 32)),
            jnp.broadcast_to(marks % 64, (3, 4, 4, 8, 32)),
        ],
        axis=-1,
    ).astype(BF16)
    asked = jnp.concatenate([asked, marks], axis=-1).reshape(QP, 16, WIDE)
    tail = jnp.pad(tail_keys.reshape(4, 12, 576), ((0, 0), (0, 0), (0, WIDE - 576)))
    slab = lax.dynamic_slice_in_dim(residual, t * SLAB, SLAB, 2).reshape(4, 12, SLAB)
    slab = jnp.pad(slab, ((0, 0), (0, 0), (0, WIDE - SLAB)))
    extra = jnp.concatenate([tail, slab], axis=1).reshape(4, 3, 8, WIDE)
    extra = extra.transpose(1, 0, 2, 3).reshape(EP, 16, WIDE)
    send = jnp.concatenate([asked, extra], axis=0)

    every = jnp.arange(GROUPS, dtype=jnp.int32)
    hit = read_list.T[:, :, None] == every[None, None, :]
    inv = jnp.sum(jnp.where(hit, every[None, :, None], 0), axis=1).astype(jnp.int32)
    retk = jnp.sum(
        jnp.where(read_list == g, jnp.arange(4, dtype=jnp.int32)[None, :], 0), axis=1
    ).astype(jnp.int32)
    reads = lax.dynamic_index_in_dim(read_list, g, 0, keepdims=False)
    table = lax.dynamic_index_in_dim(page_table, g, 0, keepdims=False)
    pos = (table[:, None] * 128 + jnp.arange(128, dtype=jnp.int32)[None, :]).astype(F32)
    pos = pos.reshape(8, 1, 768)
    gain = lax.dynamic_slice_in_dim(norm_gain, t * SLAB, SLAB, 0)
    gain = jnp.pad(gain, (0, SLABW - SLAB)).reshape(1, SLABW)

    smem = pl.BlockSpec(memory_space=pltpu.SMEM)
    vmem = pl.BlockSpec(memory_space=pltpu.VMEM)
    anym = pl.BlockSpec(memory_space=pl.ANY)
    dma = pltpu.SemaphoreType.DMA
    nq = QP * 16
    done = pl.pallas_call(
        kernel,
        out_shape=jax.ShapeDtypeStruct((4, 16, SLAB), BF16),
        in_specs=[smem] * 3 + [vmem] * 3 + [anym] * 6,
        out_specs=vmem,
        scratch_shapes=[
            pltpu.VMEM((GROUPS, 16, WIDE), BF16),
            pltpu.VMEM((GROUPS, 16, WIDE), BF16),
            pltpu.VMEM((NP, 16, WIDE), BF16),
            pltpu.VMEM((QP, 16, WIDE), BF16),
            pltpu.VMEM((4, 6, 128, 576), BF16),
            pltpu.VMEM((nq, LATENT), F32),
            pltpu.VMEM((nq, LATENT), F32),
            pltpu.VMEM((nq, 1), F32),
            pltpu.VMEM((nq, 1), F32),
            pltpu.VMEM((nq, LATENT), BF16),
            pltpu.VMEM((nq, LATENT), BF16),
            pltpu.VMEM((8, nq), F32),
            pltpu.VMEM((8, nq), F32),
            pltpu.VMEM((nq, LATENT), BF16),
            pltpu.VMEM((nq, 1024), BF16),
            pltpu.VMEM((8, 512, 128), BF16),
            pltpu.VMEM((1024, 3584), BF16),
            pltpu.VMEM((3584, 128), BF16),
            pltpu.VMEM((3584, 128), BF16),
            pltpu.VMEM((128, 3584), BF16),
            pltpu.VMEM((2, 8, ROWS, SLABW), BF16),
            pltpu.VMEM((8, ROWS, SLABW), BF16),
            pltpu.VMEM((ROWS, SLABW), BF16),
            pltpu.VMEM((8, ROWS, SLABW), BF16),
            pltpu.VMEM((8, ROWS, SLABW), BF16),
            pltpu.VMEM((4, 16, SLABW), BF16),
            pltpu.VMEM((GROUPS, 16, SLABW), BF16),
            pltpu.VMEM((GROUPS, 16, SLABW), BF16),
            dma((6,)),
            dma((4,)),
            dma((4,)),
            dma((3,)),
            dma((3,)),
            dma((3,)),
            dma((3,)),
            dma((3,)),
            dma((3,)),
        ],
        compiler_params=pltpu.CompilerParams(
            collective_id=0, has_side_effects=True, vmem_limit_bytes=56 * 1024 * 1024
        ),
    )(
        inv,
        retk,
        reads,
        send,
        pos,
        gain,
        pool_pages.reshape(6, 128, 576),
        w_uv,
        w_out,
        w_gate,
        w_up,
        w_down,
    )
    return done[:, :12].reshape(12, 4, SLAB)


def solution(mesh):
    placed = (
        P("grp", "tp", None, None),
        P(),
        P(),
        P("grp"),
        P("grp", None, "tp", None),
        P("grp", None, None),
        P("grp", None, None),
        P("tp", None, None),
        P("tp", None),
        P(),
        P(None, "tp"),
        P(None, "tp"),
        P("tp", None),
    )
    return jax.shard_map(
        on_device, mesh=mesh, in_specs=placed, out_specs=P("grp", None, "tp"), check_vma=False
    )
```

```python
import functools

import jax
import jax.numpy as jnp
import numpy as np
from jax import lax
from jax.experimental import pallas as pl
from jax.experimental.pallas import tpu as pltpu
from jax.sharding import PartitionSpec as P

LATENT = 512
SCALE = 192.0 ** (-0.5)
SCALE2 = SCALE * 1.4426950408889634
NEGATIVE = -1e30
EPSILON = 1e-06
MESH = pl.DeviceIdType.MESH
F32 = jnp.float32
BF16 = jnp.bfloat16

GROUPS = 32
QP = 24
EP = 6
NP = QP + EP
WIDE = 640
SLAB = 448
SLABW = 512
ROWS = 48
RET = 384
NT = (((1,), (1,)), ((), ()))


def drain(ref, sem):
    pltpu.make_async_copy(ref, ref, sem).wait()


def iota(shape, dim):
    return lax.broadcasted_iota(jnp.int32, shape, dim)


def kernel(
    reads_ref,
    table_ref,
    context_ref,
    reads_vec,
    queries_ref,
    tail_ref,
    resid_ref,
    gain_ref,
    pool_ref,
    wuv_hbm,
    wout_hbm,
    wgate_hbm,
    wup_hbm,
    wdown_hbm,
    out_ref,
    send_ref,
    inv_vec,
    inv_ref,
    pos_ref,
    gain_slab,
    h1,
    s2,
    q1,
    q2,
    kbuf,
    acc_own,
    acc_peer,
    own_top,
    own_den,
    peer_top,
    peer_den,
    numer_out,
    numer_in,
    lse_out,
    lse_in,
    latent,
    flatm,
    wuv,
    wout,
    wgate,
    wup,
    wdown,
    mix,
    rs1,
    agout,
    ag,
    rs2,
    fin,
    sback,
    rback,
    wsem,
    ksend,
    krecv,
    hsend,
    hrecv,
    zsend,
    zrecv,
    tsend,
    trecv,
):
    g = lax.axis_index("grp")
    t = lax.axis_index("tp")
    x, z = t // 2, t % 2
    right = lax.rem(x + 1, 4)
    left = lax.rem(x + 3, 4)
    across = lax.rem(x + 2, 4)
    right_t = right * 2 + z
    left_t = left * 2 + z
    peer_t = x * 2 + (1 - z)

    pending = {}

    def finish(*names):
        for name in names or list(pending):
            pending.pop(name)()

    barrier = pltpu.get_barrier_semaphore()

    @pl.loop(1, GROUPS)
    def _(d):
        pl.semaphore_signal(
            barrier, inc=1, device_id={"grp": lax.rem(g + d, GROUPS)}, device_id_type=MESH
        )

    @pl.loop(1, 8)
    def _(d):
        pl.semaphore_signal(
            barrier, inc=1, device_id={"tp": lax.rem(t + d, 8)}, device_id_type=MESH
        )

    own_keys = pltpu.make_async_copy(pool_ref, kbuf.at[x], wsem.at[0])
    own_keys.start()
    weights = [
        pltpu.make_async_copy(wuv_hbm, wuv, wsem.at[1]),
        pltpu.make_async_copy(wout_hbm, wout, wsem.at[2]),
        pltpu.make_async_copy(wgate_hbm, wgate, wsem.at[3]),
        pltpu.make_async_copy(wup_hbm, wup, wsem.at[4]),
        pltpu.make_async_copy(wdown_hbm, wdown, wsem.at[5]),
    ]
    for copy in weights:
        copy.start()
    pending["own_keys"] = own_keys.wait
    pending["weights"] = lambda: [copy.wait() for copy in weights]

    half = iota((8, 64), 1) < 32
    for k in range(0, 4, 2):
        for r in range(3):
            marks = []
            for n in (k * 3 + r, (k + 1) * 3 + r):
                length = context_ref[n]
                marks.append(
                    jnp.where(half, length // 64, length % 64).astype(F32).astype(BF16)
                )
            for s in range(4):
                i = (r * 4 + s) * 2 + k // 2
                send_ref[i, 0:8, 0:576] = queries_ref[k * 3 + r, s]
                send_ref[i, 8:16, 0:576] = queries_ref[(k + 1) * 3 + r, s]
                send_ref[i, 0:8, 576:] = marks[0]
                send_ref[i, 8:16, 576:] = marks[1]
    for j in range(8):

        @pl.when(t == j)
        def _():
            at = slice(SLAB * j, SLAB * (j + 1))
            gain_slab[:, :SLAB] = gain_ref[:, at]
            gain_slab[:, SLAB:] = jnp.zeros((1, SLABW - SLAB), F32)
            for k in range(0, 4, 2):

                def line(n, b):
                    if b < 3:
                        block = tail_ref[n * 3 + b].astype(F32)
                    else:
                        block = resid_ref[n * 3 + b - 3, :, at].astype(F32)
                    return jnp.pad(block, ((0, 0), (0, WIDE - block.shape[1])))

                for e in range(3):
                    send_ref[QP + e * 2 + k // 2] = jnp.concatenate(
                        [line(k, 2 * e), line(k, 2 * e + 1), line(k + 1, 2 * e), line(k + 1, 2 * e + 1)],
                        axis=0,
                    ).astype(BF16)

    @pl.when(g < NP)
    def _():
        h1[g] = send_ref[g]

    pl.semaphore_wait(barrier, GROUPS - 1 + 7)

    @pl.loop(1, GROUPS)
    def _(d):
        to = lax.rem(g + d, GROUPS)

        @pl.when(to < NP)
        def _():
            pltpu.make_async_remote_copy(
                src_ref=send_ref.at[to],
                dst_ref=h1.at[g],
                send_sem=hsend.at[0],
                recv_sem=hrecv.at[0],
                device_id={"grp": to},
                device_id_type=MESH,
            ).start()

    def hop1_sent():
        @pl.when(g >= NP)
        def _():
            drain(send_ref.at[pl.ds(0, NP)], hsend.at[0])

        @pl.when(g < NP)
        def _():
            drain(send_ref.at[pl.ds(0, NP - 1)], hsend.at[0])

    def hop1_arrived():
        @pl.when(g < NP)
        def _():
            drain(h1.at[pl.ds(0, GROUPS - 1)], hrecv.at[0])

    pending["hop1_sent"] = hop1_sent
    pending["hop1"] = hop1_arrived

    place, group = iota((GROUPS, 128), 1), iota((GROUPS, 128), 0)
    inv_vec[...] = jnp.zeros((8, 128), jnp.int32)
    for k in range(4):
        asked_here = reads_vec[:, k : k + 1] == place
        inv_vec[k : k + 1, :] = jnp.max(
            jnp.where(asked_here, group, 0), axis=0, keepdims=True
        )
    askers = pltpu.make_async_copy(inv_vec, inv_ref, wsem.at[6])
    askers.start()
    offset = iota((1, 128), 1)
    for j in range(48):
        pos_ref[j // 6, :, (j % 6) * 128 : (j % 6 + 1) * 128] = (
            table_ref[g, j] * 128 + offset
        ).astype(F32)
    askers.wait()

    to_right = pltpu.make_async_remote_copy(
        src_ref=pool_ref,
        dst_ref=kbuf.at[x],
        send_sem=ksend.at[0],
        recv_sem=krecv.at[0],
        device_id={"tp": right_t},
        device_id_type=MESH,
    )
    to_left = pltpu.make_async_remote_copy(
        src_ref=pool_ref,
        dst_ref=kbuf.at[x],
        send_sem=ksend.at[1],
        recv_sem=krecv.at[1],
        device_id={"tp": left_t},
        device_id_type=MESH,
    )
    to_right.start()
    to_left.start()
    pending["right_sent"] = to_right.wait_send
    pending["left_sent"] = to_left.wait_send
    pending["from_left"] = to_right.wait_recv
    pending["from_right"] = to_left.wait_recv

    finish("hop1")
    @pl.when(g < NP)
    def _():
        kp = lax.rem(g, 2)
        upper = iota((16, WIDE), 0) < 8

        def picked(to):
            first = h1[inv_ref[2 * kp, to]]
            second = h1[inv_ref[2 * kp + 1, to]]
            return jnp.where(upper, first, second)

        @pl.loop(1, GROUPS)
        def _(d):
            to = lax.rem(g + d, GROUPS)
            s2[to] = picked(to)
            pltpu.make_async_remote_copy(
                src_ref=s2.at[to],
                dst_ref=q1.at[g],
                send_sem=hsend.at[1],
                recv_sem=hrecv.at[1],
                device_id={"grp": to},
                device_id_type=MESH,
            ).start()

        q1[g] = picked(g)

    def hop2_sent():
        @pl.when(g < NP)
        def _():
            drain(s2.at[pl.ds(0, GROUPS - 1)], hsend.at[1])

    def hop2_arrived():
        @pl.when(g < NP)
        def _():
            drain(q1.at[pl.ds(0, NP - 1)], hrecv.at[1])

        @pl.when(g >= NP)
        def _():
            drain(q1.at[pl.ds(0, NP)], hrecv.at[1])

    pending["hop2_sent"] = hop2_sent
    pending["hop2"] = hop2_arrived

    finish("from_left")
    on_right = pltpu.make_async_remote_copy(
        src_ref=kbuf.at[left, pl.ds(0, 3)],
        dst_ref=kbuf.at[left, pl.ds(0, 3)],
        send_sem=ksend.at[2],
        recv_sem=krecv.at[2],
        device_id={"tp": right_t},
        device_id_type=MESH,
    )
    on_right.start()
    finish("from_right")
    on_left = pltpu.make_async_remote_copy(
        src_ref=kbuf.at[right, pl.ds(3, 3)],
        dst_ref=kbuf.at[right, pl.ds(3, 3)],
        send_sem=ksend.at[3],
        recv_sem=krecv.at[3],
        device_id={"tp": left_t},
        device_id_type=MESH,
    )
    on_left.start()
    pending["on_right_sent"] = on_right.wait_send
    pending["on_left_sent"] = on_left.wait_send
    pending["across_1"] = on_right.wait_recv
    pending["across_2"] = on_left.wait_recv
    finish("hop2")

    swaps = [
        pltpu.make_async_remote_copy(
            src_ref=q1.at[pl.ds(8 * c, 8)],
            dst_ref=q2.at[pl.ds(8 * c, 8)],
            send_sem=zsend.at[c],
            recv_sem=zrecv.at[c],
            device_id={"tp": peer_t},
            device_id_type=MESH,
        )
        for c in range(3)
    ]
    for c in range(3):
        swaps[c].start()
        pending["swap_sent", c] = swaps[c].wait_send
        pending["swap", c] = swaps[c].wait_recv

    finish("own_keys", "across_1", "across_2")

    nq = QP * 16

    def prefix_part(asked, acc, top, den):
        def block(b, carry):
            rows = asked[...]
            rows = rows.reshape(rows.shape[0] * 16, WIDE)
            lengths = rows[:, 576:577].astype(F32) * 64.0 + rows[:, 608:609].astype(F32)
            keys = kbuf[b].reshape(768, 576)
            scores = lax.dot_general(rows[:, :576], keys, NT, preferred_element_type=F32)
            position = pos_ref[b * 2 + z]
            scores = jnp.where(position < lengths, scores * SCALE2, NEGATIVE)
            old = top[...]
            new = jnp.maximum(old, jnp.max(scores, axis=1, keepdims=True))
            weight = jnp.exp2(scores - new).astype(BF16)
            keep = jnp.exp2(old - new)
            top[...] = new
            den[...] = den[...] * keep + jnp.sum(weight.astype(F32), axis=1, keepdims=True)
            acc[...] = acc[...] * keep + jnp.dot(
                weight, keys[:, :LATENT], preferred_element_type=F32
            )
            return carry

        lax.fori_loop(0, 4, block, 0)

    rows = q1[pl.ds(0, QP)].reshape(nq, WIDE)
    extra = q1[pl.ds(QP, EP)].reshape(EP * 16, WIDE)
    nt = EP * 16
    scores = lax.dot_general(
        rows[:, :576], extra[:, :576], NT, preferred_element_type=F32
    )
    n, m = iota((nq, nt), 0), iota((nq, nt), 1)
    line = (m // 32) * 8 + m % 8
    seen = (line < 12) & (line // 4 == n // 128) & ((m // 8) % 4 == (n // 8) % 4)
    seen = seen & (line % 4 <= (n // 32) % 4)
    scores = jnp.where(seen, scores * SCALE2, NEGATIVE)
    first = jnp.max(scores, axis=1, keepdims=True)
    weight = jnp.where(seen, jnp.exp2(scores - first), 0.0).astype(BF16)
    own_top[...] = first
    own_den[...] = jnp.sum(weight.astype(F32), axis=1, keepdims=True)
    acc_own[...] = jnp.dot(weight, extra[:, :LATENT], preferred_element_type=F32)
    prefix_part(q1.at[pl.ds(0, QP)], acc_own, own_top, own_den)

    diagonal = iota((128, 128), 0) == iota((128, 128), 1)
    for c in range(3):
        finish(("swap", c))
        peer_top[...] = jnp.full((128, 1), NEGATIVE, F32)
        peer_den[...] = jnp.zeros((128, 1), F32)
        acc_peer[...] = jnp.zeros_like(acc_peer)
        prefix_part(q2.at[pl.ds(8 * c, 8)], acc_peer, peer_top, peer_den)
        numer_out[c] = (acc_peer[...] / peer_den[...]).astype(BF16)
        lse = peer_top[...] + jnp.log2(peer_den[...])
        lse_out[c] = jnp.broadcast_to(
            jnp.sum(jnp.where(diagonal, lse, 0.0), axis=0, keepdims=True), (8, 128)
        )
        for s, (src, dst) in enumerate([(numer_out, numer_in), (lse_out, lse_in)]):
            copy = pltpu.make_async_remote_copy(
                src_ref=src.at[c],
                dst_ref=dst.at[c],
                send_sem=zsend.at[3 + 2 * c + s],
                recv_sem=zrecv.at[3 + 2 * c + s],
                device_id={"tp": peer_t},
                device_id_type=MESH,
            )
            copy.start()
            pending["back_sent", c, s] = copy.wait_send
            pending["back", c, s] = copy.wait_recv
    finish("weights")
    for c in range(3):
        finish(("back", c, 0), ("back", c, 1))
        at = slice(128 * c, 128 * (c + 1))
        lse = jnp.sum(jnp.where(diagonal, lse_in[c, 0:1, :], 0.0), axis=1, keepdims=True)
        both = jnp.maximum(own_top[at], lse)
        mine = jnp.exp2(own_top[at] - both)
        theirs = jnp.exp2(lse - both)
        scaled = 1.0 / (own_den[at] * mine + theirs)
        latent[at] = (
            acc_own[at] * (mine * scaled) + numer_in[c].astype(F32) * (theirs * scaled)
        ).astype(BF16)

    head_of = iota((nq, 128), 0) % 8
    for h in range(8):
        value = jnp.dot(latent[...], wuv[h], preferred_element_type=F32)
        flatm[:, h * 128 : (h + 1) * 128] = jnp.where(head_of == h, value, 0.0).astype(BF16)
    o, n = iota((ROWS, nq), 0), iota((ROWS, nq), 1)
    chosen = ((n // 32) == o % 12) & ((n // 8) % 4 == o // 12)
    flat = jnp.dot(
        jnp.where(chosen, 1.0, 0.0).astype(BF16), flatm[...], preferred_element_type=F32
    ).astype(BF16)

    def spread(part, dst, s):
        for d in range(1, 8):
            to = lax.rem(t + d, 8)
            pltpu.make_async_remote_copy(
                src_ref=part(to),
                dst_ref=dst.at[t],
                send_sem=tsend.at[s],
                recv_sem=trecv.at[s],
                device_id={"tp": to},
                device_id_type=MESH,
            ).start()
        pending["spread_sent", s] = lambda: drain(rs1.at[pl.ds(0, 7)], tsend.at[s])
        pending["spread", s] = lambda: drain(dst.at[pl.ds(0, 7)], trecv.at[s])

    def slabs(left_side, weight, dst):
        for j in range(4):
            wide = jnp.dot(
                left_side, weight[:, 896 * j : 896 * (j + 1)], preferred_element_type=F32
            ).astype(BF16)
            dst[2 * j, :, :SLAB] = wide[:, :SLAB]
            dst[2 * j + 1, :, :SLAB] = wide[:, SLAB:]

    mix[0, :, :, SLAB:] = jnp.zeros((8, ROWS, SLABW - SLAB), BF16)
    mix[1, :, :, SLAB:] = jnp.zeros((8, ROWS, SLABW - SLAB), BF16)
    slabs(flat, wout, mix.at[0])
    spread(lambda to: mix.at[0, to], rs1, 0)
    rs1[t] = mix[0, t]
    o, m = iota((ROWS, nt), 0), iota((ROWS, nt), 1)
    line = (m // 32) * 8 + m % 8
    chosen = (line - 12 == o % 12) & ((m // 8) % 4 == o // 12)
    hidden = jnp.dot(
        jnp.where(chosen, 1.0, 0.0).astype(BF16),
        extra[:, :SLABW],
        preferred_element_type=F32,
    )
    finish(("spread", 0))
    for j in range(8):
        hidden = hidden + rs1[j].astype(F32)
    lane = iota((ROWS, SLABW), 1)
    hidden = jnp.where(lane < SLAB, hidden, 0.0)
    square = jnp.sum(hidden * hidden, axis=1, keepdims=True)
    high = square.astype(BF16).astype(F32)
    low = square - high
    packed = jnp.where(
        lane < SLAB, hidden * gain_slab[...], jnp.where(lane < SLAB + 32, high, low)
    ).astype(BF16)
    agout[...] = packed
    spread(lambda to: agout, ag, 1)
    ag[t] = packed
    finish(("spread", 1))
    total = jnp.zeros((ROWS, 1), F32)
    gate = jnp.zeros((ROWS, 128), F32)
    upward = jnp.zeros((ROWS, 128), F32)
    for j in range(8):
        block = ag[j]
        total = total + (
            block[:, SLAB : SLAB + 1].astype(F32) + block[:, SLAB + 32 : SLAB + 33].astype(F32)
        )
        at = slice(SLAB * j, SLAB * (j + 1))
        gate = gate + jnp.dot(block[:, :SLAB], wgate[at], preferred_element_type=F32)
        upward = upward + jnp.dot(block[:, :SLAB], wup[at], preferred_element_type=F32)
    factor = lax.rsqrt(total * (1.0 / 3584.0) + EPSILON)
    gate = gate * factor
    upward = upward * factor
    active = (gate / (1.0 + jnp.exp(-gate)) * upward).astype(BF16)
    slabs(active, wdown, mix.at[1])
    spread(lambda to: mix.at[1, to], rs2, 2)
    rs2[t] = mix[1, t]
    finish(("spread", 2))
    for j in range(8):
        hidden = hidden + rs2[j].astype(F32)

    o, m = iota((64, ROWS), 0), iota((64, ROWS), 1)
    result = hidden.astype(BF16)

    def placed(chosen, columns):
        return jnp.dot(
            jnp.where((o // 16 == m // 12) & chosen, 1.0, 0.0).astype(BF16),
            columns,
            preferred_element_type=F32,
        )

    wide = placed(o % 16 == m % 12, result[:, :RET])
    rest = [
        placed(o % 16 - 12 + 4 * r == m % 12, result[:, RET:SLAB]) for r in range(3)
    ]
    rest = jnp.concatenate(rest + [jnp.zeros((64, RET - 192), F32)], axis=1)
    lower = iota((64, RET), 0) % 16 >= 12
    fin[...] = jnp.where(lower, rest, wide).astype(BF16).reshape(4, 16, RET)

    def answer(to):
        slot = jnp.where(reads_ref[to, 3] == g, 3, 0)
        slot = jnp.where(reads_ref[to, 2] == g, 2, slot)
        slot = jnp.where(reads_ref[to, 1] == g, 1, slot)
        return fin[slot]

    @pl.loop(1, GROUPS)
    def _(d):
        to = lax.rem(g + d, GROUPS)
        sback[to] = answer(to)
        pltpu.make_async_remote_copy(
            src_ref=sback.at[to],
            dst_ref=rback.at[g],
            send_sem=hsend.at[2],
            recv_sem=hrecv.at[2],
            device_id={"grp": to},
            device_id_type=MESH,
        ).start()

    rback[g] = answer(g)
    pending["return_sent"] = lambda: drain(sback.at[pl.ds(0, GROUPS - 1)], hsend.at[2])
    pending["return"] = lambda: drain(rback.at[pl.ds(0, GROUPS - 1)], hrecv.at[2])
    finish("return")
    for k in range(4):
        block = rback[reads_ref[g, k]].astype(F32)
        for r in range(3):
            out_ref[3 * k + r, :, :RET] = block[4 * r : 4 * r + 4].astype(BF16)
            out_ref[3 * k + r, :, RET:] = block[12:, 64 * r : 64 * r + 64].astype(BF16)

    finish()


def on_device(
    pool_pages,
    page_table,
    read_list,
    context,
    queries,
    tail_keys,
    residual,
    w_uv,
    w_out,
    norm_gain,
    w_gate,
    w_up,
    w_down,
):
    smem = pl.BlockSpec(memory_space=pltpu.SMEM)
    vmem = pl.BlockSpec(memory_space=pltpu.VMEM)
    anym = pl.BlockSpec(memory_space=pl.ANY)
    dma = pltpu.SemaphoreType.DMA
    nq = QP * 16
    return pl.pallas_call(
        kernel,
        out_shape=jax.ShapeDtypeStruct((12, 4, SLAB), BF16),
        in_specs=[smem] * 3 + [vmem] * 5 + [anym] * 6,
        out_specs=vmem,
        scratch_shapes=[
            pltpu.VMEM((NP, 16, WIDE), BF16),
            pltpu.VMEM((8, 128), jnp.int32),
            pltpu.SMEM((8, 128), jnp.int32),
            pltpu.VMEM((8, 1, 768), F32),
            pltpu.VMEM((1, SLABW), F32),
            pltpu.VMEM((GROUPS, 16, WIDE), BF16),
            pltpu.VMEM((GROUPS, 16, WIDE), BF16),
            pltpu.VMEM((NP, 16, WIDE), BF16),
            pltpu.VMEM((QP, 16, WIDE), BF16),
            pltpu.VMEM((4, 6, 128, 576), BF16),
            pltpu.VMEM((nq, LATENT), F32),
            pltpu.VMEM((128, LATENT), F32),
            pltpu.VMEM((nq, 1), F32),
            pltpu.VMEM((nq, 1), F32),
            pltpu.VMEM((128, 1), F32),
            pltpu.VMEM((128, 1), F32),
            pltpu.VMEM((3, 128, LATENT), BF16),
            pltpu.VMEM((3, 128, LATENT), BF16),
            pltpu.VMEM((3, 8, 128), F32),
            pltpu.VMEM((3, 8, 128), F32),
            pltpu.VMEM((nq, LATENT), BF16),
            pltpu.VMEM((nq, 1024), BF16),
            pltpu.VMEM((8, 512, 128), BF16),
            pltpu.VMEM((1024, 3584), BF16),
            pltpu.VMEM((3584, 128), BF16),
            pltpu.VMEM((3584, 128), BF16),
            pltpu.VMEM((128, 3584), BF16),
            pltpu.VMEM((2, 8, ROWS, SLABW), BF16),
            pltpu.VMEM((8, ROWS, SLABW), BF16),
            pltpu.VMEM((ROWS, SLABW), BF16),
            pltpu.VMEM((8, ROWS, SLABW), BF16),
            pltpu.VMEM((8, ROWS, SLABW), BF16),
            pltpu.VMEM((4, 16, RET), BF16),
            pltpu.VMEM((GROUPS, 16, RET), BF16),
            pltpu.VMEM((GROUPS, 16, RET), BF16),
            dma((7,)),
            dma((4,)),
            dma((4,)),
            dma((3,)),
            dma((3,)),
            dma((9,)),
            dma((9,)),
            dma((3,)),
            dma((3,)),
        ],
        compiler_params=pltpu.CompilerParams(
            collective_id=0, has_side_effects=True, vmem_limit_bytes=56 * 1024 * 1024
        ),
    )(
        read_list,
        page_table,
        context,
        read_list,
        queries,
        tail_keys,
        residual,
        norm_gain.reshape(1, 3584),
        pool_pages.reshape(6, 128, 576),
        w_uv,
        w_out,
        w_gate,
        w_up,
        w_down,
    )


def solution(mesh):
    placed = (
        P("grp", "tp", None, None),
        P(),
        P(),
        P("grp"),
        P("grp", None, "tp", None),
        P("grp", None, None),
        P("grp", None, None),
        P("tp", None, None),
        P("tp", None),
        P(),
        P(None, "tp"),
        P(None, "tp"),
        P("tp", None),
    )
    return jax.shard_map(
        on_device, mesh=mesh, in_specs=placed, out_specs=P("grp", None, "tp"), check_vma=False
    )
```

```python
import functools

import jax
import jax.numpy as jnp
import numpy as np
from jax import lax
from jax.experimental import pallas as pl
from jax.experimental.pallas import tpu as pltpu
from jax.sharding import PartitionSpec as P

LATENT = 512
SCALE = 192.0 ** (-0.5)
SCALE2 = SCALE * 1.4426950408889634
NEGATIVE = -1e30
EPSILON = 1e-06
MESH = pl.DeviceIdType.MESH
F32 = jnp.float32
BF16 = jnp.bfloat16

GROUPS = 32
QP = 24
EP = 6
NP = QP + EP
WIDE = 640
SLAB = 448
SLABW = 512
ROWS = 48
RET = 384
NT = (((1,), (1,)), ((), ()))


def drain(ref, sem):
    pltpu.make_async_copy(ref, ref, sem).wait()


def iota(shape, dim):
    return lax.broadcasted_iota(jnp.int32, shape, dim)


def kernel(
    reads_ref,
    table_ref,
    context_ref,
    reads_vec,
    queries_ref,
    tail_ref,
    resid_ref,
    gain_ref,
    pool_ref,
    wuv_hbm,
    wout_hbm,
    wgate_hbm,
    wup_hbm,
    wdown_hbm,
    out_ref,
    send_ref,
    inv_vec,
    inv_ref,
    pos_ref,
    gain_slab,
    h1,
    s2,
    q1,
    q2,
    kbuf,
    acc_own,
    sbuf,
    numer_out,
    numer_in,
    lse_out,
    lse_in,
    latent,
    flatm,
    wuv,
    wout,
    wgate,
    wup,
    wdown,
    mix,
    rs1,
    agout,
    ag,
    rs2,
    fin,
    sback,
    rback,
    wsem,
    ksend,
    krecv,
    hsend,
    hrecv,
    qrecv,
    zsend,
    zrecv,
    tsend,
    trecv,
):
    g = lax.axis_index("grp")
    t = lax.axis_index("tp")
    x, z = t // 2, t % 2
    right = lax.rem(x + 1, 4)
    left = lax.rem(x + 3, 4)
    across = lax.rem(x + 2, 4)
    right_t = right * 2 + z
    left_t = left * 2 + z
    peer_t = x * 2 + (1 - z)

    pending = {}

    def finish(*names):
        for name in names or list(pending):
            pending.pop(name)()

    barrier = pltpu.get_barrier_semaphore()

    @pl.loop(1, GROUPS)
    def _(d):
        pl.semaphore_signal(
            barrier, inc=1, device_id={"grp": lax.rem(g + d, GROUPS)}, device_id_type=MESH
        )

    @pl.loop(1, 8)
    def _(d):
        pl.semaphore_signal(
            barrier, inc=1, device_id={"tp": lax.rem(t + d, 8)}, device_id_type=MESH
        )

    plane = lax.rem(g // 2, 4)
    turn = 2 * z - 1

    @pl.loop(0, 16)
    def _(d):
        far = lax.rem(plane + 2 - (d % 2) * turn, 4)
        to = (d // 4) * 8 + far * 2 + (d // 2) % 2
        pl.semaphore_signal(
            barrier, inc=1, device_id={"grp": to, "tp": peer_t}, device_id_type=MESH
        )

    own_keys = pltpu.make_async_copy(pool_ref, kbuf.at[x], wsem.at[0])
    own_keys.start()
    weights = [
        pltpu.make_async_copy(wuv_hbm, wuv, wsem.at[1]),
        pltpu.make_async_copy(wout_hbm, wout, wsem.at[2]),
        pltpu.make_async_copy(wgate_hbm, wgate, wsem.at[3]),
        pltpu.make_async_copy(wup_hbm, wup, wsem.at[4]),
        pltpu.make_async_copy(wdown_hbm, wdown, wsem.at[5]),
    ]
    for copy in weights:
        copy.start()
    pending["own_keys"] = own_keys.wait
    pending["weights"] = lambda: [copy.wait() for copy in weights]

    half = iota((8, 64), 1) < 32
    for k in range(0, 4, 2):
        for r in range(3):
            marks = []
            for n in (k * 3 + r, (k + 1) * 3 + r):
                length = context_ref[n]
                marks.append(
                    jnp.where(half, length // 64, length % 64).astype(F32).astype(BF16)
                )
            for s in range(4):
                i = (r * 4 + s) * 2 + k // 2
                send_ref[i, 0:8, 0:576] = queries_ref[k * 3 + r, s]
                send_ref[i, 8:16, 0:576] = queries_ref[(k + 1) * 3 + r, s]
                send_ref[i, 0:8, 576:] = marks[0]
                send_ref[i, 8:16, 576:] = marks[1]
    for j in range(8):

        @pl.when(t == j)
        def _():
            at = slice(SLAB * j, SLAB * (j + 1))
            gain_slab[0, :SLAB] = gain_ref[at]
            gain_slab[:, SLAB:] = jnp.zeros((1, SLABW - SLAB), F32)
            for k in range(0, 4, 2):

                def line(n, b):
                    if b < 3:
                        block = tail_ref[n * 3 + b].astype(F32)
                    else:
                        block = resid_ref[n * 3 + b - 3, :, at].astype(F32)
                    return jnp.pad(block, ((0, 0), (0, WIDE - block.shape[1])))

                for e in range(3):
                    send_ref[QP + e * 2 + k // 2] = jnp.concatenate(
                        [line(k, 2 * e), line(k, 2 * e + 1), line(k + 1, 2 * e), line(k + 1, 2 * e + 1)],
                        axis=0,
                    ).astype(BF16)

    @pl.when(g < NP)
    def _():
        h1[g] = send_ref[g]

    pl.semaphore_wait(barrier, GROUPS - 1 + 7 + 16)

    @pl.loop(1, GROUPS)
    def _(d):
        to = lax.rem(g + d, GROUPS)

        @pl.when(to < NP)
        def _():
            pltpu.make_async_remote_copy(
                src_ref=send_ref.at[to],
                dst_ref=h1.at[g],
                send_sem=hsend.at[0],
                recv_sem=hrecv.at[0],
                device_id={"grp": to},
                device_id_type=MESH,
            ).start()

    def hop1_sent():
        @pl.when(g >= NP)
        def _():
            drain(send_ref.at[pl.ds(0, NP)], hsend.at[0])

        @pl.when(g < NP)
        def _():
            drain(send_ref.at[pl.ds(0, NP - 1)], hsend.at[0])

    def hop1_arrived():
        @pl.when(g < NP)
        def _():
            drain(h1.at[pl.ds(0, GROUPS - 1)], hrecv.at[0])

    pending["hop1_sent"] = hop1_sent
    pending["hop1"] = hop1_arrived

    place, group = iota((GROUPS, 128), 1), iota((GROUPS, 128), 0)
    inv_vec[...] = jnp.zeros((8, 128), jnp.int32)
    columns = reads_vec[...].T
    for k in range(4):
        asked_here = columns[:, k : k + 1] == place
        inv_vec[k : k + 1, :] = jnp.max(
            jnp.where(asked_here, group, 0), axis=0, keepdims=True
        )
    askers = pltpu.make_async_copy(inv_vec, inv_ref, wsem.at[6])
    askers.start()
    offset = iota((1, 128), 1)
    for j in range(48):
        pos_ref[j // 6, :, (j % 6) * 128 : (j % 6 + 1) * 128] = (
            table_ref[g, j] * 128 + offset
        ).astype(F32)
    askers.wait()

    to_right = pltpu.make_async_remote_copy(
        src_ref=pool_ref,
        dst_ref=kbuf.at[x],
        send_sem=ksend.at[0],
        recv_sem=krecv.at[0],
        device_id={"tp": right_t},
        device_id_type=MESH,
    )
    to_left = pltpu.make_async_remote_copy(
        src_ref=pool_ref,
        dst_ref=kbuf.at[x],
        send_sem=ksend.at[1],
        recv_sem=krecv.at[1],
        device_id={"tp": left_t},
        device_id_type=MESH,
    )
    to_right.start()
    to_left.start()
    pending["right_sent"] = to_right.wait_send
    pending["left_sent"] = to_left.wait_send
    pending["from_left"] = to_right.wait_recv
    pending["from_right"] = to_left.wait_recv

    finish("hop1")
    @pl.when(g < NP)
    def _():
        kp = lax.rem(g, 2)
        upper = iota((16, WIDE), 0) < 8

        def picked(to):
            first = h1[inv_ref[2 * kp, to]]
            second = h1[inv_ref[2 * kp + 1, to]]
            return jnp.where(upper, first, second)

        @pl.loop(1, GROUPS)
        def _(d):
            to = lax.rem(g + d, GROUPS)
            s2[to] = picked(to)
            away = lax.rem(lax.rem(to // 2, 4) - plane + 4, 4)
            crossing = (g < QP) & ((away == 2) | (away == 2 - turn))

            @pl.when(crossing)
            def _():
                pltpu.make_async_remote_copy(
                    src_ref=s2.at[to],
                    dst_ref=q2.at[g],
                    send_sem=hsend.at[1],
                    recv_sem=qrecv.at[g // 8],
                    device_id={"grp": to, "tp": peer_t},
                    device_id_type=MESH,
                ).start()

            @pl.when(jnp.logical_not(crossing))
            def _():
                pltpu.make_async_remote_copy(
                    src_ref=s2.at[to],
                    dst_ref=q1.at[g],
                    send_sem=hsend.at[1],
                    recv_sem=qrecv.at[g // 8],
                    device_id={"grp": to},
                    device_id_type=MESH,
                ).start()

        q1[g] = picked(g)

    def hop2_sent():
        @pl.when(g < NP)
        def _():
            drain(s2.at[pl.ds(0, GROUPS - 1)], hsend.at[1])

    def hop2_arrived(c):
        count = 8 if c < 3 else EP

        @pl.when(g // 8 == c)
        def _():
            @pl.when(g < NP)
            def _():
                drain(q1.at[pl.ds(0, count - 1)], qrecv.at[c])

        @pl.when((g // 8 != c) | (g >= NP))
        def _():
            drain(q1.at[pl.ds(0, count)], qrecv.at[c])

    pending["hop2_sent"] = hop2_sent
    for c in range(4):
        pending["hop2", c] = functools.partial(hop2_arrived, c)

    finish("from_left")
    on_right = pltpu.make_async_remote_copy(
        src_ref=kbuf.at[left, pl.ds(0, 3)],
        dst_ref=kbuf.at[left, pl.ds(0, 3)],
        send_sem=ksend.at[2],
        recv_sem=krecv.at[2],
        device_id={"tp": right_t},
        device_id_type=MESH,
    )
    on_right.start()
    finish("from_right")
    on_left = pltpu.make_async_remote_copy(
        src_ref=kbuf.at[right, pl.ds(3, 3)],
        dst_ref=kbuf.at[right, pl.ds(3, 3)],
        send_sem=ksend.at[3],
        recv_sem=krecv.at[3],
        device_id={"tp": left_t},
        device_id_type=MESH,
    )
    on_left.start()
    pending["on_right_sent"] = on_right.wait_send
    pending["on_left_sent"] = on_left.wait_send
    pending["across_1"] = on_right.wait_recv
    pending["across_2"] = on_left.wait_recv
    def swap_arrived(c):
        drain(q2.at[pl.ds(0, 8)], zrecv.at[c])

    def swap_sent(c):
        drain(q2.at[pl.ds(0, 8)], zsend.at[c])

    near = lax.rem(plane + turn + 4, 4)
    far = lax.rem(plane + 2, 4)
    for c in range(3):
        finish(("hop2", c))
        for src, dst, at in ((q1, q2, plane), (q1, q2, near), (q2, q1, near), (q2, q1, far)):
            part = pl.ds(8 * c + 2 * at, 2)
            pltpu.make_async_remote_copy(
                src_ref=src.at[part],
                dst_ref=dst.at[part],
                send_sem=zsend.at[c],
                recv_sem=zrecv.at[c],
                device_id={"tp": peer_t},
                device_id_type=MESH,
            ).start()
        pending["swap_sent", c] = functools.partial(swap_sent, c)
        pending["swap", c] = functools.partial(swap_arrived, c)
    finish(("hop2", 3))
    finish("own_keys", "across_1", "across_2")

    nq = QP * 16
    nt = EP * 16
    extra = q1[pl.ds(QP, EP)].reshape(nt, WIDE)

    def keys_of(b, width):
        return jnp.concatenate([kbuf[b, j, :width] for j in range(6)], axis=1)

    def attend(rows, buf, tail=None):
        lengths = rows[:, 576:577].astype(F32) * 64.0 + rows[:, 608:609].astype(F32)
        top = jnp.full((128, 1), NEGATIVE, F32)
        if tail is not None:
            top = jnp.max(tail, axis=1, keepdims=True)
        for b in range(4):
            scores = jnp.dot(rows[:, :576], keys_of(b, 576), preferred_element_type=F32)
            scores = jnp.where(pos_ref[b * 2 + z] < lengths, scores * SCALE2, NEGATIVE)
            buf[b] = scores
            top = jnp.maximum(top, jnp.max(scores, axis=1, keepdims=True))
        den = jnp.zeros((128, 1), F32)
        acc = jnp.zeros((128, LATENT), F32)
        if tail is not None:
            weight = jnp.exp2(tail - top).astype(BF16)
            den = jnp.sum(weight.astype(F32), axis=1, keepdims=True)
            acc = jnp.dot(weight, extra[:, :LATENT], preferred_element_type=F32)
        for b in range(4):
            weight = jnp.exp2(buf[b] - top).astype(BF16)
            den = den + jnp.sum(weight.astype(F32), axis=1, keepdims=True)
            acc = acc + lax.dot_general(
                weight, keys_of(b, LATENT), NT, preferred_element_type=F32
            )
        return top, den, acc

    diagonal = iota((128, 128), 0) == iota((128, 128), 1)
    n, m = iota((128, nt), 0), iota((128, nt), 1)
    line = (m // 32) * 8 + m % 8
    in_place = (line % 4 <= n // 32) & ((m // 8) % 4 == (n // 8) % 4)
    own_top, own_den = [], []
    for c in range(3):
        finish(("swap", c))
        top, den, acc = attend(q2[pl.ds(8 * c, 8)].reshape(128, WIDE), sbuf.at[0])
        numer_out[c] = (acc / den).astype(BF16)
        lse = top + jnp.log2(den)
        lse_out[c] = jnp.broadcast_to(
            jnp.sum(jnp.where(diagonal, lse, 0.0), axis=0, keepdims=True), (8, 128)
        )
        for s, (src, dst) in enumerate([(numer_out, numer_in), (lse_out, lse_in)]):
            copy = pltpu.make_async_remote_copy(
                src_ref=src.at[c],
                dst_ref=dst.at[c],
                send_sem=zsend.at[3 + 2 * c + s],
                recv_sem=zrecv.at[3 + 2 * c + s],
                device_id={"tp": peer_t},
                device_id_type=MESH,
            )
            copy.start()
            pending["back_sent", c, s] = copy.wait_send
            pending["back", c, s] = copy.wait_recv
        rows = q1[pl.ds(8 * c, 8)].reshape(128, WIDE)
        tail = lax.dot_general(
            rows[:, :576], extra[:, :576], NT, preferred_element_type=F32
        )
        tail = jnp.where(in_place & (line // 4 == c), tail * SCALE2, NEGATIVE)
        top, den, acc = attend(rows, sbuf.at[1], tail)
        own_top.append(top)
        own_den.append(den)
        acc_own[128 * c : 128 * (c + 1)] = acc
    finish("weights")
    for c in range(3):
        finish(("back", c, 0), ("back", c, 1))
        at = slice(128 * c, 128 * (c + 1))
        lse = jnp.sum(jnp.where(diagonal, lse_in[c, 0:1, :], 0.0), axis=1, keepdims=True)
        both = jnp.maximum(own_top[c], lse)
        mine = jnp.exp2(own_top[c] - both)
        theirs = jnp.exp2(lse - both)
        scaled = 1.0 / (own_den[c] * mine + theirs)
        latent[at] = (
            acc_own[at] * (mine * scaled) + numer_in[c].astype(F32) * (theirs * scaled)
        ).astype(BF16)

    head_of = iota((nq, 128), 0) % 8
    for h in range(8):
        value = jnp.dot(latent[...], wuv[h], preferred_element_type=F32)
        flatm[:, h * 128 : (h + 1) * 128] = jnp.where(head_of == h, value, 0.0).astype(BF16)
    o, n = iota((ROWS, nq), 0), iota((ROWS, nq), 1)
    chosen = ((n // 32) == o % 12) & ((n // 8) % 4 == o // 12)
    flat = jnp.dot(
        jnp.where(chosen, 1.0, 0.0).astype(BF16), flatm[...], preferred_element_type=F32
    ).astype(BF16)

    def spread(part, dst, s):
        for d in range(1, 8):
            to = lax.rem(t + d, 8)
            pltpu.make_async_remote_copy(
                src_ref=part(to),
                dst_ref=dst.at[t],
                send_sem=tsend.at[s],
                recv_sem=trecv.at[s],
                device_id={"tp": to},
                device_id_type=MESH,
            ).start()
        pending["spread_sent", s] = lambda: drain(rs1.at[pl.ds(0, 7)], tsend.at[s])
        pending["spread", s] = lambda: drain(dst.at[pl.ds(0, 7)], trecv.at[s])

    def slabs(left_side, weight, dst):
        for j in range(4):
            wide = jnp.dot(
                left_side, weight[:, 896 * j : 896 * (j + 1)], preferred_element_type=F32
            ).astype(BF16)
            dst[2 * j, :, :SLAB] = wide[:, :SLAB]
            dst[2 * j + 1, :, :SLAB] = wide[:, SLAB:]

    mix[0, :, :, SLAB:] = jnp.zeros((8, ROWS, SLABW - SLAB), BF16)
    mix[1, :, :, SLAB:] = jnp.zeros((8, ROWS, SLABW - SLAB), BF16)
    slabs(flat, wout, mix.at[0])
    spread(lambda to: mix.at[0, to], rs1, 0)
    rs1[t] = mix[0, t]
    o, m = iota((ROWS, nt), 0), iota((ROWS, nt), 1)
    line = (m // 32) * 8 + m % 8
    chosen = (line - 12 == o % 12) & ((m // 8) % 4 == o // 12)
    hidden = jnp.dot(
        jnp.where(chosen, 1.0, 0.0).astype(BF16),
        extra[:, :SLABW],
        preferred_element_type=F32,
    )
    finish(("spread", 0))
    for j in range(8):
        hidden = hidden + rs1[j].astype(F32)
    lane = iota((ROWS, SLABW), 1)
    hidden = jnp.where(lane < SLAB, hidden, 0.0)
    square = jnp.sum(hidden * hidden, axis=1, keepdims=True)
    high = square.astype(BF16).astype(F32)
    low = square - high
    packed = jnp.where(
        lane < SLAB, hidden * gain_slab[...], jnp.where(lane < SLAB + 32, high, low)
    ).astype(BF16)
    agout[...] = packed
    spread(lambda to: agout, ag, 1)
    ag[t] = packed
    finish(("spread", 1))
    total = jnp.zeros((ROWS, 1), F32)
    gate = jnp.zeros((ROWS, 128), F32)
    upward = jnp.zeros((ROWS, 128), F32)
    for j in range(8):
        block = ag[j]
        total = total + (
            block[:, SLAB : SLAB + 1].astype(F32) + block[:, SLAB + 32 : SLAB + 33].astype(F32)
        )
        at = slice(SLAB * j, SLAB * (j + 1))
        gate = gate + jnp.dot(block[:, :SLAB], wgate[at], preferred_element_type=F32)
        upward = upward + jnp.dot(block[:, :SLAB], wup[at], preferred_element_type=F32)
    factor = lax.rsqrt(total * (1.0 / 3584.0) + EPSILON)
    gate = gate * factor
    upward = upward * factor
    active = (gate / (1.0 + jnp.exp(-gate)) * upward).astype(BF16)
    slabs(active, wdown, mix.at[1])
    spread(lambda to: mix.at[1, to], rs2, 2)
    rs2[t] = mix[1, t]
    finish(("spread", 2))
    for j in range(8):
        hidden = hidden + rs2[j].astype(F32)

    o, m = iota((64, ROWS), 0), iota((64, ROWS), 1)
    result = hidden.astype(BF16)

    def placed(chosen, columns):
        return jnp.dot(
            jnp.where((o // 16 == m // 12) & chosen, 1.0, 0.0).astype(BF16),
            columns,
            preferred_element_type=F32,
        )

    wide = placed(o % 16 == m % 12, result[:, :RET])
    rest = [
        placed(o % 16 - 12 + 4 * r == m % 12, result[:, RET:SLAB]) for r in range(3)
    ]
    rest = jnp.concatenate(rest + [jnp.zeros((64, RET - 192), F32)], axis=1)
    lower = iota((64, RET), 0) % 16 >= 12
    fin[...] = jnp.where(lower, rest, wide).astype(BF16).reshape(4, 16, RET)

    def answer(to):
        slot = jnp.where(reads_ref[3, to] == g, 3, 0)
        slot = jnp.where(reads_ref[2, to] == g, 2, slot)
        slot = jnp.where(reads_ref[1, to] == g, 1, slot)
        return fin[slot]

    @pl.loop(1, GROUPS)
    def _(d):
        to = lax.rem(g + d, GROUPS)
        sback[to] = answer(to)
        pltpu.make_async_remote_copy(
            src_ref=sback.at[to],
            dst_ref=rback.at[g],
            send_sem=hsend.at[2],
            recv_sem=hrecv.at[2],
            device_id={"grp": to},
            device_id_type=MESH,
        ).start()

    rback[g] = answer(g)
    pending["return_sent"] = lambda: drain(sback.at[pl.ds(0, GROUPS - 1)], hsend.at[2])
    pending["return"] = lambda: drain(rback.at[pl.ds(0, GROUPS - 1)], hrecv.at[2])
    finish("return")
    for k in range(4):
        block = rback[reads_ref[k, g]].astype(F32)
        for r in range(3):
            out_ref[3 * k + r, :, :RET] = block[4 * r : 4 * r + 4].astype(BF16)
            out_ref[3 * k + r, :, RET:] = block[12:, 64 * r : 64 * r + 64].astype(BF16)

    finish()


def on_device(
    pool_pages,
    page_table,
    read_list,
    context,
    queries,
    tail_keys,
    residual,
    w_uv,
    w_out,
    norm_gain,
    w_gate,
    w_up,
    w_down,
):
    smem = pl.BlockSpec(memory_space=pltpu.SMEM)
    vmem = pl.BlockSpec(memory_space=pltpu.VMEM)
    anym = pl.BlockSpec(memory_space=pl.ANY)
    dma = pltpu.SemaphoreType.DMA
    nq = QP * 16
    return pl.pallas_call(
        kernel,
        out_shape=jax.ShapeDtypeStruct((12, 4, SLAB), BF16),
        in_specs=[smem] * 3 + [vmem] * 5 + [anym] * 6,
        out_specs=vmem,
        scratch_shapes=[
            pltpu.VMEM((NP, 16, WIDE), BF16),
            pltpu.VMEM((8, 128), jnp.int32),
            pltpu.SMEM((8, 128), jnp.int32),
            pltpu.VMEM((8, 1, 768), F32),
            pltpu.VMEM((1, SLABW), F32),
            pltpu.VMEM((GROUPS, 16, WIDE), BF16),
            pltpu.VMEM((GROUPS, 16, WIDE), BF16),
            pltpu.VMEM((NP, 16, WIDE), BF16),
            pltpu.VMEM((QP, 16, WIDE), BF16),
            pltpu.VMEM((4, 6, 576, 128), BF16),
            pltpu.VMEM((nq, LATENT), F32),
            pltpu.VMEM((2, 4, 128, 768), F32),
            pltpu.VMEM((3, 128, LATENT), BF16),
            pltpu.VMEM((3, 128, LATENT), BF16),
            pltpu.VMEM((3, 8, 128), F32),
            pltpu.VMEM((3, 8, 128), F32),
            pltpu.VMEM((nq, LATENT), BF16),
            pltpu.VMEM((nq, 1024), BF16),
            pltpu.VMEM((8, 512, 128), BF16),
            pltpu.VMEM((1024, 3584), BF16),
            pltpu.VMEM((3584, 128), BF16),
            pltpu.VMEM((3584, 128), BF16),
            pltpu.VMEM((128, 3584), BF16),
            pltpu.VMEM((2, 8, ROWS, SLABW), BF16),
            pltpu.VMEM((8, ROWS, SLABW), BF16),
            pltpu.VMEM((ROWS, SLABW), BF16),
            pltpu.VMEM((8, ROWS, SLABW), BF16),
            pltpu.VMEM((8, ROWS, SLABW), BF16),
            pltpu.VMEM((4, 16, RET), BF16),
            pltpu.VMEM((GROUPS, 16, RET), BF16),
            pltpu.VMEM((GROUPS, 16, RET), BF16),
            dma((7,)),
            dma((4,)),
            dma((4,)),
            dma((3,)),
            dma((3,)),
            dma((4,)),
            dma((9,)),
            dma((9,)),
            dma((3,)),
            dma((3,)),
        ],
        compiler_params=pltpu.CompilerParams(
            collective_id=0, has_side_effects=True, vmem_limit_bytes=56 * 1024 * 1024
        ),
    )(
        read_list.T,
        page_table,
        context,
        read_list.T,
        queries,
        tail_keys,
        residual,
        norm_gain,
        pool_pages.reshape(6, 128, 576).transpose(0, 2, 1),
        w_uv,
        w_out,
        w_gate,
        w_up,
        w_down,
    )


def solution(mesh):
    placed = (
        P("grp", "tp", None, None),
        P(),
        P(),
        P("grp"),
        P("grp", None, "tp", None),
        P("grp", None, None),
        P("grp", None, None),
        P("tp", None, None),
        P("tp", None),
        P(),
        P(None, "tp"),
        P(None, "tp"),
        P("tp", None),
    )
    return jax.shard_map(
        on_device, mesh=mesh, in_specs=placed, out_specs=P("grp", None, "tp"), check_vma=False
    )
```

```python
import functools

import jax
import jax.numpy as jnp
import numpy as np
from jax import lax
from jax.experimental import pallas as pl
from jax.experimental.pallas import tpu as pltpu
from jax.sharding import PartitionSpec as P

LATENT = 512
SCALE = 192.0 ** (-0.5)
SCALE2 = SCALE * 1.4426950408889634
NEGATIVE = -1e30
EPSILON = 1e-06
MESH = pl.DeviceIdType.MESH
F32 = jnp.float32
BF16 = jnp.bfloat16

GROUPS = 32
QP = 24
EP = 6
NP = QP + EP
WIDE = 640
SLAB = 448
SLABW = 512
ROWS = 48
RET = 384
TILES = WIDE // 128
CUTS = ((0, 2), (2, 2), (4, 1))
NT = (((1,), (1,)), ((), ()))


def drain(ref, sem):
    pltpu.make_async_copy(ref, ref, sem).wait()


def iota(shape, dim):
    return lax.broadcasted_iota(jnp.int32, shape, dim)


def kernel(
    reads_ref,
    table_ref,
    context_ref,
    reads_vec,
    queries_ref,
    tail_ref,
    resid_ref,
    gain_ref,
    pool_ref,
    wuv_hbm,
    wout_hbm,
    wgate_hbm,
    wup_hbm,
    wdown_hbm,
    out_ref,
    send_ref,
    inv_vec,
    inv_ref,
    pos_ref,
    gain_slab,
    h1_0,
    h1_1,
    h1_2,
    s2,
    q1,
    q2,
    kbuf,
    acc_own,
    sbuf,
    numer_out,
    numer_in,
    lse_out,
    lse_in,
    latent,
    flatm,
    wuv,
    wout,
    wgate,
    wup,
    wdown,
    mix,
    rs1,
    agout,
    ag,
    rs2,
    fin,
    sback,
    rback,
    wsem,
    ksend,
    krecv,
    hsend,
    hrecv,
    zsend,
    zrecv,
    tsend,
    trecv,
):
    g = lax.axis_index("grp")
    t = lax.axis_index("tp")
    x, z = t // 2, t % 2
    right = lax.rem(x + 1, 4)
    left = lax.rem(x + 3, 4)
    across = lax.rem(x + 2, 4)
    right_t = right * 2 + z
    left_t = left * 2 + z
    peer_t = x * 2 + (1 - z)

    pending = {}
    h1 = (h1_0, h1_1, h1_2)

    def finish(*names):
        for name in names or list(pending):
            pending.pop(name)()

    barrier = pltpu.get_barrier_semaphore()

    @pl.loop(1, GROUPS)
    def _(d):
        pl.semaphore_signal(
            barrier, inc=1, device_id={"grp": lax.rem(g + d, GROUPS)}, device_id_type=MESH
        )

    @pl.loop(1, 8)
    def _(d):
        pl.semaphore_signal(
            barrier, inc=1, device_id={"tp": lax.rem(t + d, 8)}, device_id_type=MESH
        )

    plane = lax.rem(g // 2, 4)
    turn = 2 * z - 1

    @pl.loop(0, 16)
    def _(d):
        far = lax.rem(plane + 2 - (d % 2) * turn, 4)
        to = (d // 4) * 8 + far * 2 + (d // 2) % 2
        pl.semaphore_signal(
            barrier, inc=1, device_id={"grp": to, "tp": peer_t}, device_id_type=MESH
        )

    own_keys = pltpu.make_async_copy(pool_ref, kbuf.at[x], wsem.at[0])
    own_keys.start()
    weights = [
        pltpu.make_async_copy(wuv_hbm, wuv, wsem.at[1]),
        pltpu.make_async_copy(wout_hbm, wout, wsem.at[2]),
        pltpu.make_async_copy(wgate_hbm, wgate, wsem.at[3]),
        pltpu.make_async_copy(wup_hbm, wup, wsem.at[4]),
        pltpu.make_async_copy(wdown_hbm, wdown, wsem.at[5]),
    ]
    for copy in weights:
        copy.start()
    pending["own_keys"] = own_keys.wait
    pending["weights"] = lambda: [copy.wait() for copy in weights]

    half = iota((8, 64), 1) < 32
    for k in range(0, 4, 2):
        for r in range(3):
            marks = []
            for n in (k * 3 + r, (k + 1) * 3 + r):
                length = context_ref[n]
                marks.append(
                    jnp.where(half, length // 64, length % 64).astype(F32).astype(BF16)
                )
            for s in range(4):
                i = (r * 4 + s) * 2 + k // 2
                for h in range(2):
                    row = jnp.concatenate([queries_ref[(k + h) * 3 + r, s], marks[h]], axis=1)
                    for w in range(TILES):
                        send_ref[w, i, 8 * h : 8 * h + 8] = row[:, 128 * w : 128 * (w + 1)]
    for j in range(8):

        @pl.when(t == j)
        def _():
            at = slice(SLAB * j, SLAB * (j + 1))
            gain_slab[0, :SLAB] = gain_ref[at]
            gain_slab[:, SLAB:] = jnp.zeros((1, SLABW - SLAB), F32)
            for k in range(0, 4, 2):

                def line(n, b):
                    if b < 3:
                        block = tail_ref[n * 3 + b].astype(F32)
                    else:
                        block = resid_ref[n * 3 + b - 3, :, at].astype(F32)
                    return jnp.pad(block, ((0, 0), (0, WIDE - block.shape[1])))

                for e in range(3):
                    block = jnp.concatenate(
                        [line(k, 2 * e), line(k, 2 * e + 1), line(k + 1, 2 * e), line(k + 1, 2 * e + 1)],
                        axis=0,
                    ).astype(BF16)
                    for w in range(TILES):
                        send_ref[w, QP + e * 2 + k // 2] = block[:, 128 * w : 128 * (w + 1)]

    @pl.when(g < NP)
    def _():
        for w in range(TILES):
            h1[w // 2][w % 2, g] = send_ref[w, g]

    pl.semaphore_wait(barrier, GROUPS - 1 + 7 + 16)

    def hop1_sent(c):
        chunk = pl.ds(*CUTS[c])

        @pl.when(g >= NP)
        def _():
            drain(send_ref.at[chunk, pl.ds(0, NP)], hsend.at[c])

        @pl.when(g < NP)
        def _():
            drain(send_ref.at[chunk, pl.ds(0, NP - 1)], hsend.at[c])

    for c in range(3):
        chunk = pl.ds(*CUTS[c])

        @pl.loop(1, GROUPS)
        def _(d):
            to = lax.rem(g + d, GROUPS)

            @pl.when(to < NP)
            def _():
                pltpu.make_async_remote_copy(
                    src_ref=send_ref.at[chunk, to],
                    dst_ref=h1[c].at[:, g],
                    send_sem=hsend.at[c],
                    recv_sem=hrecv.at[c],
                    device_id={"grp": to},
                    device_id_type=MESH,
                ).start()

        pending["hop1_sent", c] = functools.partial(hop1_sent, c)

    place, group = iota((GROUPS, 128), 1), iota((GROUPS, 128), 0)
    inv_vec[...] = jnp.zeros((8, 128), jnp.int32)
    columns = reads_vec[...].T
    for k in range(4):
        asked_here = columns[:, k : k + 1] == place
        inv_vec[k : k + 1, :] = jnp.max(
            jnp.where(asked_here, group, 0), axis=0, keepdims=True
        )
    askers = pltpu.make_async_copy(inv_vec, inv_ref, wsem.at[6])
    askers.start()
    offset = iota((1, 128), 1)
    for j in range(48):
        pos_ref[j // 6, :, (j % 6) * 128 : (j % 6 + 1) * 128] = (
            table_ref[g, j] * 128 + offset
        ).astype(F32)
    askers.wait()

    to_right = pltpu.make_async_remote_copy(
        src_ref=pool_ref,
        dst_ref=kbuf.at[x],
        send_sem=ksend.at[0],
        recv_sem=krecv.at[0],
        device_id={"tp": right_t},
        device_id_type=MESH,
    )
    to_left = pltpu.make_async_remote_copy(
        src_ref=pool_ref,
        dst_ref=kbuf.at[x],
        send_sem=ksend.at[1],
        recv_sem=krecv.at[1],
        device_id={"tp": left_t},
        device_id_type=MESH,
    )
    to_right.start()
    to_left.start()
    pending["right_sent"] = to_right.wait_send
    pending["left_sent"] = to_left.wait_send
    pending["from_left"] = to_right.wait_recv
    pending["from_right"] = to_left.wait_recv

    def hop2_sent(c):
        @pl.when(g < NP)
        def _():
            drain(s2.at[pl.ds(*CUTS[c]), pl.ds(0, GROUPS - 1)], hsend.at[3 + c])

    def hop2_arrived(c):
        chunk = pl.ds(*CUTS[c])

        @pl.when(g < NP)
        def _():
            drain(q1.at[chunk, pl.ds(0, NP - 1)], hrecv.at[3 + c])

        @pl.when(g >= NP)
        def _():
            drain(q1.at[chunk, pl.ds(0, NP)], hrecv.at[3 + c])

    for c in range(3):

        @pl.when(g < NP)
        def _():
            chunk = pl.ds(*CUTS[c])
            tiles = range(CUTS[c][0], CUTS[c][0] + CUTS[c][1])
            drain(h1[c].at[:, pl.ds(0, GROUPS - 1)], hrecv.at[c])
            kp = lax.rem(g, 2)
            upper = iota((16, 128), 0) < 8

            def picked(w, to):
                first = h1[c][w % 2, inv_ref[2 * kp, to]]
                second = h1[c][w % 2, inv_ref[2 * kp + 1, to]]
                return jnp.where(upper, first, second)

            @pl.loop(1, GROUPS)
            def _(d):
                to = lax.rem(g + d, GROUPS)
                for w in tiles:
                    s2[w, to] = picked(w, to)
                away = lax.rem(lax.rem(to // 2, 4) - plane + 4, 4)
                crossing = (g < QP) & ((away == 2) | (away == 2 - turn))

                @pl.when(crossing)
                def _():
                    pltpu.make_async_remote_copy(
                        src_ref=s2.at[chunk, to],
                        dst_ref=q2.at[chunk, g],
                        send_sem=hsend.at[3 + c],
                        recv_sem=hrecv.at[3 + c],
                        device_id={"grp": to, "tp": peer_t},
                        device_id_type=MESH,
                    ).start()

                @pl.when(jnp.logical_not(crossing))
                def _():
                    pltpu.make_async_remote_copy(
                        src_ref=s2.at[chunk, to],
                        dst_ref=q1.at[chunk, g],
                        send_sem=hsend.at[3 + c],
                        recv_sem=hrecv.at[3 + c],
                        device_id={"grp": to},
                        device_id_type=MESH,
                    ).start()

            for w in tiles:
                q1[w, g] = picked(w, g)

        pending["hop2_sent", c] = functools.partial(hop2_sent, c)
        pending["hop2", c] = functools.partial(hop2_arrived, c)

    def swap_arrived(c, r):
        drain(q2.at[pl.ds(*CUTS[c]), pl.ds(0, 8)], zrecv.at[3 * c + r])

    def swap_sent(c, r):
        drain(q2.at[pl.ds(*CUTS[c]), pl.ds(0, 8)], zsend.at[3 * c + r])

    near = lax.rem(plane + turn + 4, 4)
    far = lax.rem(plane + 2, 4)

    def swap(c):
        finish(("hop2", c))
        for r in range(3):
            for src, dst, at in ((q1, q2, plane), (q1, q2, near), (q2, q1, near), (q2, q1, far)):
                part = pl.ds(8 * r + 2 * at, 2)
                pltpu.make_async_remote_copy(
                    src_ref=src.at[pl.ds(*CUTS[c]), part],
                    dst_ref=dst.at[pl.ds(*CUTS[c]), part],
                    send_sem=zsend.at[3 * c + r],
                    recv_sem=zrecv.at[3 * c + r],
                    device_id={"tp": peer_t},
                    device_id_type=MESH,
                ).start()
            pending["swap_sent", c, r] = functools.partial(swap_sent, c, r)
            pending["swap", c, r] = functools.partial(swap_arrived, c, r)

    swap(0)

    finish("from_left")
    on_right = pltpu.make_async_remote_copy(
        src_ref=kbuf.at[left, pl.ds(0, 3)],
        dst_ref=kbuf.at[left, pl.ds(0, 3)],
        send_sem=ksend.at[2],
        recv_sem=krecv.at[2],
        device_id={"tp": right_t},
        device_id_type=MESH,
    )
    on_right.start()
    finish("from_right")
    on_left = pltpu.make_async_remote_copy(
        src_ref=kbuf.at[right, pl.ds(3, 3)],
        dst_ref=kbuf.at[right, pl.ds(3, 3)],
        send_sem=ksend.at[3],
        recv_sem=krecv.at[3],
        device_id={"tp": left_t},
        device_id_type=MESH,
    )
    on_left.start()
    pending["on_right_sent"] = on_right.wait_send
    pending["on_left_sent"] = on_left.wait_send
    pending["across_1"] = on_right.wait_recv
    pending["across_2"] = on_left.wait_recv
    swap(1)
    swap(2)
    finish("own_keys")

    nq = QP * 16
    nt = EP * 16

    def lines(ref, first, count):
        return jnp.concatenate(
            [ref[w, pl.ds(first, count)].reshape(count * 16, 128) for w in range(TILES)], axis=1
        )

    extra = lines(q1, QP, EP)

    def keys_of(b, width):
        return jnp.concatenate([kbuf[b, j, :width] for j in range(6)], axis=1)

    def attend(rows, buf, tail=None):
        count = rows.shape[0]
        lengths = rows[:, 576:577].astype(F32) * 64.0 + rows[:, 608:609].astype(F32)
        top = jnp.full((count, 1), NEGATIVE, F32)
        if tail is not None:
            top = jnp.max(tail, axis=1, keepdims=True)
        for i, b in enumerate((x, left, right, across)):
            if i == 3 and "across_1" in pending:
                finish("across_1", "across_2")
            scores = jnp.dot(rows[:, :576], keys_of(b, 576), preferred_element_type=F32)
            scores = jnp.where(pos_ref[b * 2 + z] < lengths, scores * SCALE2, NEGATIVE)
            buf[i] = scores
            top = jnp.maximum(top, jnp.max(scores, axis=1, keepdims=True))
        den = jnp.zeros((count, 1), F32)
        acc = jnp.zeros((count, LATENT), F32)
        if tail is not None:
            weight = jnp.exp2(tail - top).astype(BF16)
            den = jnp.sum(weight.astype(F32), axis=1, keepdims=True)
            acc = jnp.dot(weight, extra[:, :LATENT], preferred_element_type=F32)
        for i, b in enumerate((x, left, right, across)):
            weight = jnp.exp2(buf[i] - top).astype(BF16)
            den = den + jnp.sum(weight.astype(F32), axis=1, keepdims=True)
            acc = acc + lax.dot_general(
                weight, keys_of(b, LATENT), NT, preferred_element_type=F32
            )
        return top, den, acc

    diagonal = iota((128, 128), 0) == iota((128, 128), 1)
    for c in range(3):
        finish(*[("swap", i, c) for i in range(3)])
        top, den, acc = attend(lines(q2, 8 * c, 8), sbuf.at[:, pl.ds(128 * c, 128)])
        numer_out[c] = (acc / den).astype(BF16)
        lse = top + jnp.log2(den)
        lse_out[c] = jnp.broadcast_to(
            jnp.sum(jnp.where(diagonal, lse, 0.0), axis=0, keepdims=True), (8, 128)
        )
        for s, (src, dst) in enumerate([(numer_out, numer_in), (lse_out, lse_in)]):
            copy = pltpu.make_async_remote_copy(
                src_ref=src.at[c],
                dst_ref=dst.at[c],
                send_sem=zsend.at[9 + 2 * c + s],
                recv_sem=zrecv.at[9 + 2 * c + s],
                device_id={"tp": peer_t},
                device_id_type=MESH,
            )
            copy.start()
            pending["back_sent", c, s] = copy.wait_send
            pending["back", c, s] = copy.wait_recv
    rows = lines(q1, 0, QP)
    n, m = iota((nq, nt), 0), iota((nq, nt), 1)
    line = (m // 32) * 8 + m % 8
    seen = (line // 4 == n // 128) & (line % 4 <= (n // 32) % 4)
    seen = seen & ((m // 8) % 4 == (n // 8) % 4)
    tail = lax.dot_general(rows[:, :576], extra[:, :576], NT, preferred_element_type=F32)
    tail = jnp.where(seen, tail * SCALE2, NEGATIVE)
    own_top, own_den, acc_own[...] = attend(rows, sbuf, tail)
    finish("weights")
    for c in range(3):
        finish(("back", c, 0), ("back", c, 1))
        at = slice(128 * c, 128 * (c + 1))
        lse = jnp.sum(jnp.where(diagonal, lse_in[c, 0:1, :], 0.0), axis=1, keepdims=True)
        both = jnp.maximum(own_top[at], lse)
        mine = jnp.exp2(own_top[at] - both)
        theirs = jnp.exp2(lse - both)
        scaled = 1.0 / (own_den[at] * mine + theirs)
        latent[at] = (
            acc_own[at] * (mine * scaled) + numer_in[c].astype(F32) * (theirs * scaled)
        ).astype(BF16)

    head_of = iota((nq, 128), 0) % 8
    for h in range(8):
        value = jnp.dot(latent[...], wuv[h], preferred_element_type=F32)
        flatm[:, h * 128 : (h + 1) * 128] = jnp.where(head_of == h, value, 0.0).astype(BF16)
    o, n = iota((ROWS, nq), 0), iota((ROWS, nq), 1)
    chosen = ((n // 32) == o % 12) & ((n // 8) % 4 == o // 12)
    flat = jnp.dot(
        jnp.where(chosen, 1.0, 0.0).astype(BF16), flatm[...], preferred_element_type=F32
    ).astype(BF16)

    def spread(part, dst, s):
        for d in range(1, 8):
            to = lax.rem(t + d, 8)
            pltpu.make_async_remote_copy(
                src_ref=part(to),
                dst_ref=dst.at[t],
                send_sem=tsend.at[s],
                recv_sem=trecv.at[s],
                device_id={"tp": to},
                device_id_type=MESH,
            ).start()
        pending["spread_sent", s] = lambda: drain(rs1.at[pl.ds(0, 7)], tsend.at[s])
        pending["spread", s] = lambda: drain(dst.at[pl.ds(0, 7)], trecv.at[s])

    def slabs(left_side, weight, dst):
        for j in range(4):
            wide = jnp.dot(
                left_side, weight[:, 896 * j : 896 * (j + 1)], preferred_element_type=F32
            ).astype(BF16)
            dst[2 * j, :, :SLAB] = wide[:, :SLAB]
            dst[2 * j + 1, :, :SLAB] = wide[:, SLAB:]

    mix[0, :, :, SLAB:] = jnp.zeros((8, ROWS, SLABW - SLAB), BF16)
    mix[1, :, :, SLAB:] = jnp.zeros((8, ROWS, SLABW - SLAB), BF16)
    slabs(flat, wout, mix.at[0])
    spread(lambda to: mix.at[0, to], rs1, 0)
    rs1[t] = mix[0, t]
    o, m = iota((ROWS, nt), 0), iota((ROWS, nt), 1)
    line = (m // 32) * 8 + m % 8
    chosen = (line - 12 == o % 12) & ((m // 8) % 4 == o // 12)
    hidden = jnp.dot(
        jnp.where(chosen, 1.0, 0.0).astype(BF16),
        extra[:, :SLABW],
        preferred_element_type=F32,
    )
    finish(("spread", 0))
    for j in range(8):
        hidden = hidden + rs1[j].astype(F32)
    lane = iota((ROWS, SLABW), 1)
    hidden = jnp.where(lane < SLAB, hidden, 0.0)
    square = jnp.sum(hidden * hidden, axis=1, keepdims=True)
    high = square.astype(BF16).astype(F32)
    low = square - high
    packed = jnp.where(
        lane < SLAB, hidden * gain_slab[...], jnp.where(lane < SLAB + 32, high, low)
    ).astype(BF16)
    agout[...] = packed
    spread(lambda to: agout, ag, 1)
    ag[t] = packed
    finish(("spread", 1))
    total = jnp.zeros((ROWS, 1), F32)
    gate = jnp.zeros((ROWS, 128), F32)
    upward = jnp.zeros((ROWS, 128), F32)
    for j in range(8):
        block = ag[j]
        total = total + (
            block[:, SLAB : SLAB + 1].astype(F32) + block[:, SLAB + 32 : SLAB + 33].astype(F32)
        )
        at = slice(SLAB * j, SLAB * (j + 1))
        gate = gate + jnp.dot(block[:, :SLAB], wgate[at], preferred_element_type=F32)
        upward = upward + jnp.dot(block[:, :SLAB], wup[at], preferred_element_type=F32)
    factor = lax.rsqrt(total * (1.0 / 3584.0) + EPSILON)
    gate = gate * factor
    upward = upward * factor
    active = (gate / (1.0 + jnp.exp(-gate)) * upward).astype(BF16)
    slabs(active, wdown, mix.at[1])
    spread(lambda to: mix.at[1, to], rs2, 2)
    rs2[t] = mix[1, t]
    finish(("spread", 2))
    for j in range(8):
        hidden = hidden + rs2[j].astype(F32)

    o, m = iota((64, ROWS), 0), iota((64, ROWS), 1)
    result = hidden.astype(BF16)

    def placed(chosen, columns):
        return jnp.dot(
            jnp.where((o // 16 == m // 12) & chosen, 1.0, 0.0).astype(BF16),
            columns,
            preferred_element_type=F32,
        )

    wide = placed(o % 16 == m % 12, result[:, :RET])
    rest = [
        placed(o % 16 - 12 + 4 * r == m % 12, result[:, RET:SLAB]) for r in range(3)
    ]
    rest = jnp.concatenate(rest + [jnp.zeros((64, RET - 192), F32)], axis=1)
    lower = iota((64, RET), 0) % 16 >= 12
    fin[...] = jnp.where(lower, rest, wide).astype(BF16).reshape(4, 16, RET)

    def answer(to):
        slot = jnp.where(reads_ref[3, to] == g, 3, 0)
        slot = jnp.where(reads_ref[2, to] == g, 2, slot)
        slot = jnp.where(reads_ref[1, to] == g, 1, slot)
        return fin[slot]

    @pl.loop(1, GROUPS)
    def _(d):
        to = lax.rem(g + d, GROUPS)
        sback[to] = answer(to)
        pltpu.make_async_remote_copy(
            src_ref=sback.at[to],
            dst_ref=rback.at[g],
            send_sem=hsend.at[6],
            recv_sem=hrecv.at[6],
            device_id={"grp": to},
            device_id_type=MESH,
        ).start()

    rback[g] = answer(g)
    pending["return_sent"] = lambda: drain(sback.at[pl.ds(0, GROUPS - 1)], hsend.at[6])
    pending["return"] = lambda: drain(rback.at[pl.ds(0, GROUPS - 1)], hrecv.at[6])
    finish("return")
    for k in range(4):
        block = rback[reads_ref[k, g]].astype(F32)
        for r in range(3):
            out_ref[3 * k + r, :, :RET] = block[4 * r : 4 * r + 4].astype(BF16)
            out_ref[3 * k + r, :, RET:] = block[12:, 64 * r : 64 * r + 64].astype(BF16)

    finish()


def on_device(
    pool_pages,
    page_table,
    read_list,
    context,
    queries,
    tail_keys,
    residual,
    w_uv,
    w_out,
    norm_gain,
    w_gate,
    w_up,
    w_down,
):
    smem = pl.BlockSpec(memory_space=pltpu.SMEM)
    vmem = pl.BlockSpec(memory_space=pltpu.VMEM)
    anym = pl.BlockSpec(memory_space=pl.ANY)
    dma = pltpu.SemaphoreType.DMA
    nq = QP * 16
    return pl.pallas_call(
        kernel,
        out_shape=jax.ShapeDtypeStruct((12, 4, SLAB), BF16),
        in_specs=[smem] * 3 + [vmem] * 5 + [anym] * 6,
        out_specs=vmem,
        scratch_shapes=[
            pltpu.VMEM((TILES, NP, 16, 128), BF16),
            pltpu.VMEM((8, 128), jnp.int32),
            pltpu.SMEM((8, 128), jnp.int32),
            pltpu.VMEM((8, 1, 768), F32),
            pltpu.VMEM((1, SLABW), F32),
            pltpu.VMEM((2, GROUPS, 16, 128), BF16),
            pltpu.VMEM((2, GROUPS, 16, 128), BF16),
            pltpu.VMEM((1, GROUPS, 16, 128), BF16),
            pltpu.VMEM((TILES, GROUPS, 16, 128), BF16),
            pltpu.VMEM((TILES, NP, 16, 128), BF16),
            pltpu.VMEM((TILES, QP, 16, 128), BF16),
            pltpu.VMEM((4, 6, 576, 128), BF16),
            pltpu.VMEM((nq, LATENT), F32),
            pltpu.VMEM((4, nq, 768), F32),
            pltpu.VMEM((3, 128, LATENT), BF16),
            pltpu.VMEM((3, 128, LATENT), BF16),
            pltpu.VMEM((3, 8, 128), F32),
            pltpu.VMEM((3, 8, 128), F32),
            pltpu.VMEM((nq, LATENT), BF16),
            pltpu.VMEM((nq, 1024), BF16),
            pltpu.VMEM((8, 512, 128), BF16),
            pltpu.VMEM((1024, 3584), BF16),
            pltpu.VMEM((3584, 128), BF16),
            pltpu.VMEM((3584, 128), BF16),
            pltpu.VMEM((128, 3584), BF16),
            pltpu.VMEM((2, 8, ROWS, SLABW), BF16),
            pltpu.VMEM((8, ROWS, SLABW), BF16),
            pltpu.VMEM((ROWS, SLABW), BF16),
            pltpu.VMEM((8, ROWS, SLABW), BF16),
            pltpu.VMEM((8, ROWS, SLABW), BF16),
            pltpu.VMEM((4, 16, RET), BF16),
            pltpu.VMEM((GROUPS, 16, RET), BF16),
            pltpu.VMEM((GROUPS, 16, RET), BF16),
            dma((7,)),
            dma((4,)),
            dma((4,)),
            dma((7,)),
            dma((7,)),
            dma((15,)),
            dma((15,)),
            dma((3,)),
            dma((3,)),
        ],
        compiler_params=pltpu.CompilerParams(
            collective_id=0, has_side_effects=True, vmem_limit_bytes=56 * 1024 * 1024
        ),
    )(
        read_list.T,
        page_table,
        context,
        read_list.T,
        queries,
        tail_keys,
        residual,
        norm_gain,
        pool_pages.reshape(6, 128, 576).transpose(0, 2, 1),
        w_uv,
        w_out,
        w_gate,
        w_up,
        w_down,
    )


def solution(mesh):
    placed = (
        P("grp", "tp", None, None),
        P(),
        P(),
        P("grp"),
        P("grp", None, "tp", None),
        P("grp", None, None),
        P("grp", None, None),
        P("tp", None, None),
        P("tp", None),
        P(),
        P(None, "tp"),
        P(None, "tp"),
        P("tp", None),
    )
    return jax.shard_map(
        on_device, mesh=mesh, in_specs=placed, out_specs=P("grp", None, "tp"), check_vma=False
    )
```

```python
import functools

import jax
import jax.numpy as jnp
import numpy as np
from jax import lax
from jax.experimental import pallas as pl
from jax.experimental.pallas import tpu as pltpu
from jax.sharding import PartitionSpec as P

LATENT = 512
SCALE = 192.0 ** (-0.5)
SCALE2 = SCALE * 1.4426950408889634
NEGATIVE = -1e30
EPSILON = 1e-06
MESH = pl.DeviceIdType.MESH
F32 = jnp.float32
BF16 = jnp.bfloat16

GROUPS = 32
QP = 24
EP = 6
NP = QP + EP
WIDE = 640
SLAB = 448
SLABW = 512
ROWS = 48
RET = 384
TILES = WIDE // 128
CUTS = ((0, 2), (2, 2), (4, 1))
NT = (((1,), (1,)), ((), ()))


def drain(ref, sem):
    pltpu.make_async_copy(ref, ref, sem).wait()


def iota(shape, dim):
    return lax.broadcasted_iota(jnp.int32, shape, dim)


def kernel(
    reads_ref,
    table_ref,
    context_ref,
    reads_vec,
    queries_ref,
    tail_ref,
    resid_ref,
    gain_ref,
    pool_ref,
    wuv_hbm,
    wout_hbm,
    wgate_hbm,
    wup_hbm,
    wdown_hbm,
    out_ref,
    send_ref,
    inv_vec,
    inv_ref,
    pos_ref,
    gain_slab,
    h1_0,
    h1_1,
    h1_2,
    s2,
    q1,
    q2,
    kbuf,
    acc_own,
    sbuf,
    numer_out,
    numer_in,
    lse_out,
    lse_in,
    latent,
    flatm,
    wuv,
    wout,
    wgate,
    wup,
    wdown,
    mix,
    rs1,
    agout,
    ag,
    rs2,
    fin,
    sback,
    rback,
    home_out,
    home_mid,
    home_next,
    home_in,
    wsem,
    ksend,
    krecv,
    hsend,
    hrecv,
    zsend,
    zrecv,
    tsend,
    trecv,
    bsend,
    brecv,
):
    g = lax.axis_index("grp")
    t = lax.axis_index("tp")
    x, z = t // 2, t % 2
    right = lax.rem(x + 1, 4)
    left = lax.rem(x + 3, 4)
    across = lax.rem(x + 2, 4)
    right_t = right * 2 + z
    left_t = left * 2 + z
    peer_t = x * 2 + (1 - z)

    pending = {}
    h1 = (h1_0, h1_1, h1_2)

    def finish(*names):
        for name in names or list(pending):
            pending.pop(name)()

    barrier = pltpu.get_barrier_semaphore()

    @pl.loop(1, GROUPS)
    def _(d):
        pl.semaphore_signal(
            barrier, inc=1, device_id={"grp": lax.rem(g + d, GROUPS)}, device_id_type=MESH
        )

    @pl.loop(1, 8)
    def _(d):
        pl.semaphore_signal(
            barrier, inc=1, device_id={"tp": lax.rem(t + d, 8)}, device_id_type=MESH
        )

    plane = lax.rem(g // 2, 4)
    turn = 2 * z - 1

    @pl.loop(0, 16)
    def _(d):
        far = lax.rem(plane + 2 - (d % 2) * turn, 4)
        to = (d // 4) * 8 + far * 2 + (d // 2) % 2
        pl.semaphore_signal(
            barrier, inc=1, device_id={"grp": to, "tp": peer_t}, device_id_type=MESH
        )

    own_keys = pltpu.make_async_copy(pool_ref, kbuf.at[x], wsem.at[0])
    own_keys.start()
    weights = [
        pltpu.make_async_copy(wuv_hbm, wuv, wsem.at[1]),
        pltpu.make_async_copy(wout_hbm, wout, wsem.at[2]),
        pltpu.make_async_copy(wgate_hbm, wgate, wsem.at[3]),
        pltpu.make_async_copy(wup_hbm, wup, wsem.at[4]),
        pltpu.make_async_copy(wdown_hbm, wdown, wsem.at[5]),
    ]
    for copy in weights:
        copy.start()
    pending["own_keys"] = own_keys.wait
    pending["weights"] = lambda: [copy.wait() for copy in weights]

    half = iota((8, 64), 1) < 32
    for k in range(0, 4, 2):
        for r in range(3):
            marks = []
            for n in (k * 3 + r, (k + 1) * 3 + r):
                length = context_ref[n]
                marks.append(
                    jnp.where(half, length // 64, length % 64).astype(F32).astype(BF16)
                )
            for s in range(4):
                i = (r * 4 + s) * 2 + k // 2
                for h in range(2):
                    row = jnp.concatenate([queries_ref[(k + h) * 3 + r, s], marks[h]], axis=1)
                    for w in range(TILES):
                        send_ref[w, i, 8 * h : 8 * h + 8] = row[:, 128 * w : 128 * (w + 1)]
    for j in range(8):

        @pl.when(t == j)
        def _():
            at = slice(SLAB * j, SLAB * (j + 1))
            gain_slab[0, :SLAB] = gain_ref[at]
            gain_slab[:, SLAB:] = jnp.zeros((1, SLABW - SLAB), F32)
            for k in range(0, 4, 2):

                def line(n, b):
                    if b < 3:
                        block = tail_ref[n * 3 + b].astype(F32)
                    else:
                        block = resid_ref[n * 3 + b - 3, :, at].astype(F32)
                    return jnp.pad(block, ((0, 0), (0, WIDE - block.shape[1])))

                for e in range(3):
                    block = jnp.concatenate(
                        [line(k, 2 * e), line(k, 2 * e + 1), line(k + 1, 2 * e), line(k + 1, 2 * e + 1)],
                        axis=0,
                    ).astype(BF16)
                    for w in range(TILES):
                        send_ref[w, QP + e * 2 + k // 2] = block[:, 128 * w : 128 * (w + 1)]

    @pl.when(g < NP)
    def _():
        for w in range(TILES):
            h1[w // 2][w % 2, g] = send_ref[w, g]

    pl.semaphore_wait(barrier, GROUPS - 1 + 7 + 16)

    def hop1_sent(c):
        chunk = pl.ds(*CUTS[c])

        @pl.when(g >= NP)
        def _():
            drain(send_ref.at[chunk, pl.ds(0, NP)], hsend.at[c])

        @pl.when(g < NP)
        def _():
            drain(send_ref.at[chunk, pl.ds(0, NP - 1)], hsend.at[c])

    for c in range(3):
        chunk = pl.ds(*CUTS[c])

        @pl.loop(1, GROUPS)
        def _(d):
            to = lax.rem(g + d, GROUPS)

            @pl.when(to < NP)
            def _():
                pltpu.make_async_remote_copy(
                    src_ref=send_ref.at[chunk, to],
                    dst_ref=h1[c].at[:, g],
                    send_sem=hsend.at[c],
                    recv_sem=hrecv.at[c],
                    device_id={"grp": to},
                    device_id_type=MESH,
                ).start()

        pending["hop1_sent", c] = functools.partial(hop1_sent, c)

    place, group = iota((GROUPS, 128), 1), iota((GROUPS, 128), 0)
    inv_vec[...] = jnp.zeros((8, 128), jnp.int32)
    columns = reads_vec[...].T
    for k in range(4):
        asked_here = columns[:, k : k + 1] == place
        inv_vec[k : k + 1, :] = jnp.max(
            jnp.where(asked_here, group, 0), axis=0, keepdims=True
        )
    askers = pltpu.make_async_copy(inv_vec, inv_ref, wsem.at[6])
    askers.start()
    offset = iota((1, 128), 1)
    for j in range(48):
        pos_ref[j // 6, :, (j % 6) * 128 : (j % 6 + 1) * 128] = (
            table_ref[g, j] * 128 + offset
        ).astype(F32)
    askers.wait()

    to_right = pltpu.make_async_remote_copy(
        src_ref=pool_ref,
        dst_ref=kbuf.at[x],
        send_sem=ksend.at[0],
        recv_sem=krecv.at[0],
        device_id={"tp": right_t},
        device_id_type=MESH,
    )
    to_left = pltpu.make_async_remote_copy(
        src_ref=pool_ref,
        dst_ref=kbuf.at[x],
        send_sem=ksend.at[1],
        recv_sem=krecv.at[1],
        device_id={"tp": left_t},
        device_id_type=MESH,
    )
    to_right.start()
    to_left.start()
    pending["right_sent"] = to_right.wait_send
    pending["left_sent"] = to_left.wait_send
    pending["from_left"] = to_right.wait_recv
    pending["from_right"] = to_left.wait_recv

    def hop2_sent(c):
        @pl.when(g < NP)
        def _():
            drain(s2.at[pl.ds(*CUTS[c]), pl.ds(0, GROUPS - 1)], hsend.at[3 + c])

    def hop2_arrived(c):
        chunk = pl.ds(*CUTS[c])

        @pl.when(g < NP)
        def _():
            drain(q1.at[chunk, pl.ds(0, NP - 1)], hrecv.at[3 + c])

        @pl.when(g >= NP)
        def _():
            drain(q1.at[chunk, pl.ds(0, NP)], hrecv.at[3 + c])

    for c in range(3):

        @pl.when(g < NP)
        def _():
            chunk = pl.ds(*CUTS[c])
            tiles = range(CUTS[c][0], CUTS[c][0] + CUTS[c][1])
            drain(h1[c].at[:, pl.ds(0, GROUPS - 1)], hrecv.at[c])
            kp = lax.rem(g, 2)
            upper = iota((16, 128), 0) < 8

            def picked(w, to):
                first = h1[c][w % 2, inv_ref[2 * kp, to]]
                second = h1[c][w % 2, inv_ref[2 * kp + 1, to]]
                return jnp.where(upper, first, second)

            @pl.loop(1, GROUPS)
            def _(d):
                to = lax.rem(g + d, GROUPS)
                for w in tiles:
                    s2[w, to] = picked(w, to)
                away = lax.rem(lax.rem(to // 2, 4) - plane + 4, 4)
                crossing = (g < QP) & ((away == 2) | (away == 2 - turn))

                @pl.when(crossing)
                def _():
                    pltpu.make_async_remote_copy(
                        src_ref=s2.at[chunk, to],
                        dst_ref=q2.at[chunk, g],
                        send_sem=hsend.at[3 + c],
                        recv_sem=hrecv.at[3 + c],
                        device_id={"grp": to, "tp": peer_t},
                        device_id_type=MESH,
                    ).start()

                @pl.when(jnp.logical_not(crossing))
                def _():
                    pltpu.make_async_remote_copy(
                        src_ref=s2.at[chunk, to],
                        dst_ref=q1.at[chunk, g],
                        send_sem=hsend.at[3 + c],
                        recv_sem=hrecv.at[3 + c],
                        device_id={"grp": to},
                        device_id_type=MESH,
                    ).start()

            for w in tiles:
                q1[w, g] = picked(w, g)

        pending["hop2_sent", c] = functools.partial(hop2_sent, c)
        pending["hop2", c] = functools.partial(hop2_arrived, c)

    def swap_arrived(c, r):
        drain(q2.at[pl.ds(*CUTS[c]), pl.ds(0, 8)], zrecv.at[3 * c + r])

    def swap_sent(c, r):
        drain(q2.at[pl.ds(*CUTS[c]), pl.ds(0, 8)], zsend.at[3 * c + r])

    near = lax.rem(plane + turn + 4, 4)
    far = lax.rem(plane + 2, 4)

    def swap(c):
        finish(("hop2", c))
        for r in range(3):
            for src, dst, at in ((q1, q2, plane), (q1, q2, near), (q2, q1, near), (q2, q1, far)):
                part = pl.ds(8 * r + 2 * at, 2)
                pltpu.make_async_remote_copy(
                    src_ref=src.at[pl.ds(*CUTS[c]), part],
                    dst_ref=dst.at[pl.ds(*CUTS[c]), part],
                    send_sem=zsend.at[3 * c + r],
                    recv_sem=zrecv.at[3 * c + r],
                    device_id={"tp": peer_t},
                    device_id_type=MESH,
                ).start()
            pending["swap_sent", c, r] = functools.partial(swap_sent, c, r)
            pending["swap", c, r] = functools.partial(swap_arrived, c, r)

    finish("from_left")
    on_right = pltpu.make_async_remote_copy(
        src_ref=kbuf.at[left, pl.ds(0, 3)],
        dst_ref=kbuf.at[left, pl.ds(0, 3)],
        send_sem=ksend.at[2],
        recv_sem=krecv.at[2],
        device_id={"tp": right_t},
        device_id_type=MESH,
    )
    on_right.start()
    finish("from_right")
    on_left = pltpu.make_async_remote_copy(
        src_ref=kbuf.at[right, pl.ds(3, 3)],
        dst_ref=kbuf.at[right, pl.ds(3, 3)],
        send_sem=ksend.at[3],
        recv_sem=krecv.at[3],
        device_id={"tp": left_t},
        device_id_type=MESH,
    )
    on_left.start()
    pending["on_right_sent"] = on_right.wait_send
    pending["on_left_sent"] = on_left.wait_send
    pending["across_1"] = on_right.wait_recv
    pending["across_2"] = on_left.wait_recv
    swap(0)
    swap(1)
    swap(2)
    finish("own_keys")

    nq = QP * 16
    nt = EP * 16

    def lines(ref, first, count):
        return jnp.concatenate(
            [ref[w, pl.ds(first, count)].reshape(count * 16, 128) for w in range(TILES)], axis=1
        )

    extra = lines(q1, QP, EP)

    def keys_of(b, width):
        return jnp.concatenate([kbuf[b, j, :width] for j in range(6)], axis=1)

    def attend(rows, buf, tail=None):
        count = rows.shape[0]
        lengths = rows[:, 576:577].astype(F32) * 64.0 + rows[:, 608:609].astype(F32)
        top = jnp.full((count, 1), NEGATIVE, F32)
        if tail is not None:
            top = jnp.max(tail, axis=1, keepdims=True)
        for i, b in enumerate((x, left, right, across)):
            if i == 3 and "across_1" in pending:
                finish("across_1", "across_2")
            scores = jnp.dot(rows[:, :576], keys_of(b, 576), preferred_element_type=F32)
            scores = jnp.where(pos_ref[b * 2 + z] < lengths, scores * SCALE2, NEGATIVE)
            buf[i] = scores
            top = jnp.maximum(top, jnp.max(scores, axis=1, keepdims=True))
        den = jnp.zeros((count, 1), F32)
        acc = jnp.zeros((count, LATENT), F32)
        if tail is not None:
            weight = jnp.exp2(tail - top).astype(BF16)
            den = jnp.sum(weight.astype(F32), axis=1, keepdims=True)
            acc = jnp.dot(weight, extra[:, :LATENT], preferred_element_type=F32)
        for i, b in enumerate((x, left, right, across)):
            weight = jnp.exp2(buf[i] - top).astype(BF16)
            den = den + jnp.sum(weight.astype(F32), axis=1, keepdims=True)
            acc = acc + lax.dot_general(
                weight, keys_of(b, LATENT), NT, preferred_element_type=F32
            )
        return top, den, acc

    diagonal = iota((128, 128), 0) == iota((128, 128), 1)
    for c in range(3):
        finish(*[("swap", i, c) for i in range(3)])
        top, den, acc = attend(lines(q2, 8 * c, 8), sbuf.at[:, pl.ds(128 * c, 128)])
        numer_out[c] = (acc / den).astype(BF16)
        lse = top + jnp.log2(den)
        lse_out[c] = jnp.broadcast_to(
            jnp.sum(jnp.where(diagonal, lse, 0.0), axis=0, keepdims=True), (8, 128)
        )
        for s, (src, dst) in enumerate([(numer_out, numer_in), (lse_out, lse_in)]):
            copy = pltpu.make_async_remote_copy(
                src_ref=src.at[c],
                dst_ref=dst.at[c],
                send_sem=zsend.at[9 + 2 * c + s],
                recv_sem=zrecv.at[9 + 2 * c + s],
                device_id={"tp": peer_t},
                device_id_type=MESH,
            )
            copy.start()
            pending["back_sent", c, s] = copy.wait_send
            pending["back", c, s] = copy.wait_recv
    rows = lines(q1, 0, QP)
    n, m = iota((nq, nt), 0), iota((nq, nt), 1)
    line = (m // 32) * 8 + m % 8
    seen = (line // 4 == n // 128) & (line % 4 <= (n // 32) % 4)
    seen = seen & ((m // 8) % 4 == (n // 8) % 4)
    tail = lax.dot_general(rows[:, :576], extra[:, :576], NT, preferred_element_type=F32)
    tail = jnp.where(seen, tail * SCALE2, NEGATIVE)
    own_top, own_den, acc_own[...] = attend(rows, sbuf, tail)
    finish("weights")
    for c in range(3):
        finish(("back", c, 0), ("back", c, 1))
        at = slice(128 * c, 128 * (c + 1))
        lse = jnp.sum(jnp.where(diagonal, lse_in[c, 0:1, :], 0.0), axis=1, keepdims=True)
        both = jnp.maximum(own_top[at], lse)
        mine = jnp.exp2(own_top[at] - both)
        theirs = jnp.exp2(lse - both)
        scaled = 1.0 / (own_den[at] * mine + theirs)
        latent[at] = (
            acc_own[at] * (mine * scaled) + numer_in[c].astype(F32) * (theirs * scaled)
        ).astype(BF16)

    head_of = iota((nq, 128), 0) % 8
    for h in range(8):
        value = jnp.dot(latent[...], wuv[h], preferred_element_type=F32)
        flatm[:, h * 128 : (h + 1) * 128] = jnp.where(head_of == h, value, 0.0).astype(BF16)
    o, n = iota((ROWS, nq), 0), iota((ROWS, nq), 1)
    chosen = ((n // 32) == o % 12) & ((n // 8) % 4 == o // 12)
    flat = jnp.dot(
        jnp.where(chosen, 1.0, 0.0).astype(BF16), flatm[...], preferred_element_type=F32
    ).astype(BF16)

    def spread(part, dst, s):
        for d in range(1, 8):
            to = lax.rem(t + d, 8)
            pltpu.make_async_remote_copy(
                src_ref=part(to),
                dst_ref=dst.at[t],
                send_sem=tsend.at[s],
                recv_sem=trecv.at[s],
                device_id={"tp": to},
                device_id_type=MESH,
            ).start()
        pending["spread_sent", s] = lambda: drain(rs1.at[pl.ds(0, 7)], tsend.at[s])
        pending["spread", s] = lambda: drain(dst.at[pl.ds(0, 7)], trecv.at[s])

    def slabs(left_side, weight, dst):
        for j in range(4):
            wide = jnp.dot(
                left_side, weight[:, 896 * j : 896 * (j + 1)], preferred_element_type=F32
            ).astype(BF16)
            dst[2 * j, :, :SLAB] = wide[:, :SLAB]
            dst[2 * j + 1, :, :SLAB] = wide[:, SLAB:]

    mix[0, :, :, SLAB:] = jnp.zeros((8, ROWS, SLABW - SLAB), BF16)
    mix[1, :, :, SLAB:] = jnp.zeros((8, ROWS, SLABW - SLAB), BF16)
    slabs(flat, wout, mix.at[0])
    spread(lambda to: mix.at[0, to], rs1, 0)
    rs1[t] = mix[0, t]
    o, m = iota((ROWS, nt), 0), iota((ROWS, nt), 1)
    line = (m // 32) * 8 + m % 8
    chosen = (line - 12 == o % 12) & ((m // 8) % 4 == o // 12)
    hidden = jnp.dot(
        jnp.where(chosen, 1.0, 0.0).astype(BF16),
        extra[:, :SLABW],
        preferred_element_type=F32,
    )
    finish(("spread", 0))
    for j in range(8):
        hidden = hidden + rs1[j].astype(F32)
    lane = iota((ROWS, SLABW), 1)
    hidden = jnp.where(lane < SLAB, hidden, 0.0)
    square = jnp.sum(hidden * hidden, axis=1, keepdims=True)
    high = square.astype(BF16).astype(F32)
    low = square - high
    packed = jnp.where(
        lane < SLAB, hidden * gain_slab[...], jnp.where(lane < SLAB + 32, high, low)
    ).astype(BF16)
    agout[...] = packed
    spread(lambda to: agout, ag, 1)
    ag[t] = packed

    o, m = iota((64, ROWS), 0), iota((64, ROWS), 1)

    def placed(chosen, columns):
        return jnp.dot(
            jnp.where((o // 16 == m // 12) & chosen, 1.0, 0.0).astype(BF16),
            columns,
            preferred_element_type=F32,
        )

    rounded = hidden.astype(BF16)
    wide = placed(o % 16 == m % 12, rounded[:, :RET])
    rest = [
        placed(o % 16 - 12 + 4 * r == m % 12, rounded[:, RET:SLAB]) for r in range(3)
    ]
    rest = jnp.concatenate(rest + [jnp.zeros((64, RET - 192), F32)], axis=1)
    lower = iota((64, RET), 0) % 16 >= 12
    block = jnp.where(lower, rest, wide).astype(BF16)
    for i in range(12):
        home_out[i] = block[16 * (i // 3) : 16 * (i // 3) + 16, 128 * (i % 3) : 128 * (i % 3 + 1)]
        copy = pltpu.make_async_remote_copy(
            src_ref=home_out.at[i],
            dst_ref=home_mid.at[g],
            send_sem=bsend.at[i],
            recv_sem=brecv.at[0],
            device_id={"grp": i},
            device_id_type=MESH,
        )

        @pl.when(g != i)
        def _():
            copy.start()

        @pl.when(g == i)
        def _():
            home_mid[g] = home_out[i]

    def home_sent():
        for i in range(12):

            @pl.when(g != i)
            def _():
                drain(home_out.at[i], bsend.at[i])

        @pl.when(g < 12)
        def _():
            drain(home_next.at[pl.ds(0, GROUPS - 1)], bsend.at[12])

    def home_arrived():
        @pl.when(g < 12)
        def _():
            drain(home_in.at[pl.ds(0, 11)], brecv.at[1])

        @pl.when(g >= 12)
        def _():
            drain(home_in.at[pl.ds(0, 12)], brecv.at[1])

    finish(("spread", 1))
    total = jnp.zeros((ROWS, 1), F32)
    gate = jnp.zeros((ROWS, 128), F32)
    upward = jnp.zeros((ROWS, 128), F32)
    for j in range(8):
        block = ag[j]
        total = total + (
            block[:, SLAB : SLAB + 1].astype(F32) + block[:, SLAB + 32 : SLAB + 33].astype(F32)
        )
        at = slice(SLAB * j, SLAB * (j + 1))
        gate = gate + jnp.dot(block[:, :SLAB], wgate[at], preferred_element_type=F32)
        upward = upward + jnp.dot(block[:, :SLAB], wup[at], preferred_element_type=F32)
    factor = lax.rsqrt(total * (1.0 / 3584.0) + EPSILON)
    gate = gate * factor
    upward = upward * factor
    active = (gate / (1.0 + jnp.exp(-gate)) * upward).astype(BF16)

    fin[...] = placed(o % 16 == m % 12, active).astype(BF16).reshape(4, 16, 128)

    def answer(to):
        slot = jnp.where(reads_ref[3, to] == g, 3, 0)
        slot = jnp.where(reads_ref[2, to] == g, 2, slot)
        slot = jnp.where(reads_ref[1, to] == g, 1, slot)
        return fin[slot]

    @pl.loop(1, GROUPS)
    def _(d):
        to = lax.rem(g + d, GROUPS)
        sback[to] = answer(to)
        pltpu.make_async_remote_copy(
            src_ref=sback.at[to],
            dst_ref=rback.at[g],
            send_sem=hsend.at[6],
            recv_sem=hrecv.at[6],
            device_id={"grp": to},
            device_id_type=MESH,
        ).start()

    rback[g] = answer(g)
    pending["return_sent"] = lambda: drain(sback.at[pl.ds(0, GROUPS - 1)], hsend.at[6])
    pending["return"] = lambda: drain(rback.at[pl.ds(0, GROUPS - 1)], hrecv.at[6])

    @pl.when(g < 12)
    def _():
        drain(home_mid.at[pl.ds(0, GROUPS - 1)], brecv.at[0])
        k = g // 3

        @pl.loop(1, GROUPS)
        def _(d):
            to = lax.rem(g + d, GROUPS)
            home_next[to] = home_mid[reads_ref[k, to]]
            pltpu.make_async_remote_copy(
                src_ref=home_next.at[to],
                dst_ref=home_in.at[g],
                send_sem=bsend.at[12],
                recv_sem=brecv.at[1],
                device_id={"grp": to},
                device_id_type=MESH,
            ).start()

        home_in[g] = home_mid[reads_ref[k, g]]

    pending["home_sent"] = home_sent
    pending["home"] = home_arrived
    finish("return")
    o, m = iota((ROWS, 64), 0), iota((ROWS, 64), 1)
    blocks = jnp.concatenate([rback[reads_ref[k, g]] for k in range(4)], axis=0)
    active = jnp.dot(
        jnp.where((o // 12 == m // 16) & (o % 12 == m % 16), 1.0, 0.0).astype(BF16),
        blocks,
        preferred_element_type=F32,
    ).astype(BF16)
    slabs(active, wdown, mix.at[1])
    spread(lambda to: mix.at[1, to], rs2, 2)
    rs2[t] = mix[1, t]
    finish("home")
    finish(("spread", 2))
    summed = rs2[0].astype(F32)
    for j in range(1, 8):
        summed = summed + rs2[j].astype(F32)
    for k in range(4):
        block = jnp.concatenate([home_in[3 * k + j] for j in range(3)], axis=1).astype(F32)
        for r in range(3):
            at = slice(12 * k + 4 * r, 12 * k + 4 * r + 4)
            out_ref[3 * k + r, :, :RET] = (
                summed[at, :RET] + block[4 * r : 4 * r + 4]
            ).astype(BF16)
            out_ref[3 * k + r, :, RET:] = (
                summed[at, RET:SLAB] + block[12:, 64 * r : 64 * r + 64]
            ).astype(BF16)

    finish()


def on_device(
    pool_pages,
    page_table,
    read_list,
    context,
    queries,
    tail_keys,
    residual,
    w_uv,
    w_out,
    norm_gain,
    w_gate,
    w_up,
    w_down,
):
    smem = pl.BlockSpec(memory_space=pltpu.SMEM)
    vmem = pl.BlockSpec(memory_space=pltpu.VMEM)
    anym = pl.BlockSpec(memory_space=pl.ANY)
    dma = pltpu.SemaphoreType.DMA
    nq = QP * 16
    return pl.pallas_call(
        kernel,
        out_shape=jax.ShapeDtypeStruct((12, 4, SLAB), BF16),
        in_specs=[smem] * 3 + [vmem] * 5 + [anym] * 6,
        out_specs=vmem,
        scratch_shapes=[
            pltpu.VMEM((TILES, NP, 16, 128), BF16),
            pltpu.VMEM((8, 128), jnp.int32),
            pltpu.SMEM((8, 128), jnp.int32),
            pltpu.VMEM((8, 1, 768), F32),
            pltpu.VMEM((1, SLABW), F32),
            pltpu.VMEM((2, GROUPS, 16, 128), BF16),
            pltpu.VMEM((2, GROUPS, 16, 128), BF16),
            pltpu.VMEM((1, GROUPS, 16, 128), BF16),
            pltpu.VMEM((TILES, GROUPS, 16, 128), BF16),
            pltpu.VMEM((TILES, NP, 16, 128), BF16),
            pltpu.VMEM((TILES, QP, 16, 128), BF16),
            pltpu.VMEM((4, 6, 576, 128), BF16),
            pltpu.VMEM((nq, LATENT), F32),
            pltpu.VMEM((4, nq, 768), F32),
            pltpu.VMEM((3, 128, LATENT), BF16),
            pltpu.VMEM((3, 128, LATENT), BF16),
            pltpu.VMEM((3, 8, 128), F32),
            pltpu.VMEM((3, 8, 128), F32),
            pltpu.VMEM((nq, LATENT), BF16),
            pltpu.VMEM((nq, 1024), BF16),
            pltpu.VMEM((8, 512, 128), BF16),
            pltpu.VMEM((1024, 3584), BF16),
            pltpu.VMEM((3584, 128), BF16),
            pltpu.VMEM((3584, 128), BF16),
            pltpu.VMEM((128, 3584), BF16),
            pltpu.VMEM((2, 8, ROWS, SLABW), BF16),
            pltpu.VMEM((8, ROWS, SLABW), BF16),
            pltpu.VMEM((ROWS, SLABW), BF16),
            pltpu.VMEM((8, ROWS, SLABW), BF16),
            pltpu.VMEM((8, ROWS, SLABW), BF16),
            pltpu.VMEM((4, 16, 128), BF16),
            pltpu.VMEM((GROUPS, 16, 128), BF16),
            pltpu.VMEM((GROUPS, 16, 128), BF16),
            pltpu.VMEM((12, 16, 128), BF16),
            pltpu.VMEM((GROUPS, 16, 128), BF16),
            pltpu.VMEM((GROUPS, 16, 128), BF16),
            pltpu.VMEM((12, 16, 128), BF16),
            dma((7,)),
            dma((4,)),
            dma((4,)),
            dma((7,)),
            dma((7,)),
            dma((15,)),
            dma((15,)),
            dma((3,)),
            dma((3,)),
            dma((13,)),
            dma((2,)),
        ],
        compiler_params=pltpu.CompilerParams(
            collective_id=0, has_side_effects=True, vmem_limit_bytes=56 * 1024 * 1024
        ),
    )(
        read_list.T,
        page_table,
        context,
        read_list.T,
        queries,
        tail_keys,
        residual,
        norm_gain,
        pool_pages.reshape(6, 128, 576).transpose(0, 2, 1),
        w_uv,
        w_out,
        w_gate,
        w_up,
        w_down,
    )


def solution(mesh):
    placed = (
        P("grp", "tp", None, None),
        P(),
        P(),
        P("grp"),
        P("grp", None, "tp", None),
        P("grp", None, None),
        P("grp", None, None),
        P("tp", None, None),
        P("tp", None),
        P(),
        P(None, "tp"),
        P(None, "tp"),
        P("tp", None),
    )
    return jax.shard_map(
        on_device, mesh=mesh, in_specs=placed, out_specs=P("grp", None, "tp"), check_vma=False
    )
```

```python
import functools

import jax
import jax.numpy as jnp
import numpy as np
from jax import lax
from jax.experimental import pallas as pl
from jax.experimental.pallas import tpu as pltpu
from jax.sharding import PartitionSpec as P

LATENT = 512
SCALE = 192.0 ** (-0.5)
SCALE2 = SCALE * 1.4426950408889634
NEGATIVE = -1e30
EPSILON = 1e-06
MESH = pl.DeviceIdType.MESH
F32 = jnp.float32
BF16 = jnp.bfloat16

GROUPS = 32
QP = 24
EP = 6
NP = QP + EP
WIDE = 640
SLAB = 448
SLABW = 512
ROWS = 48
RET = 384
TILES = WIDE // 128
CUTS = ((0, 2), (2, 2), (4, 1))
HALF = 192
NT = (((1,), (1,)), ((), ()))


def drain(ref, sem):
    pltpu.make_async_copy(ref, ref, sem).wait()


def iota(shape, dim):
    return lax.broadcasted_iota(jnp.int32, shape, dim)


def kernel(
    reads_ref,
    table_ref,
    context_ref,
    reads_vec,
    queries_ref,
    tail_ref,
    resid_ref,
    gain_ref,
    pool_ref,
    wuv_hbm,
    wout_hbm,
    wgate_hbm,
    wup_hbm,
    wdown_hbm,
    out_ref,
    send_ref,
    inv_vec,
    inv_ref,
    pos_ref,
    gain_slab,
    h1_0,
    h1_1,
    h1_2,
    s2,
    q1,
    q2,
    kbuf,
    acc_own,
    sbuf,
    numer_out,
    numer_in,
    lse_out,
    lse_in,
    latent,
    flatm,
    wuv,
    wout,
    wgate,
    wup,
    wdown,
    mix,
    rs1,
    agout,
    ag,
    rs2,
    fin,
    sback,
    rback,
    home_out,
    home_mid,
    home_next,
    home_in,
    wsem,
    ksend,
    krecv,
    hsend,
    hrecv,
    zsend,
    zrecv,
    tsend,
    trecv,
    bsend,
    brecv,
):
    g = lax.axis_index("grp")
    t = lax.axis_index("tp")
    x, z = t // 2, t % 2
    right = lax.rem(x + 1, 4)
    left = lax.rem(x + 3, 4)
    across = lax.rem(x + 2, 4)
    right_t = right * 2 + z
    left_t = left * 2 + z
    peer_t = x * 2 + (1 - z)

    pending = {}
    h1 = (h1_0, h1_1, h1_2)

    def finish(*names):
        for name in names or list(pending):
            pending.pop(name)()

    barrier = pltpu.get_barrier_semaphore()

    @pl.loop(1, GROUPS)
    def _(d):
        pl.semaphore_signal(
            barrier, inc=1, device_id={"grp": lax.rem(g + d, GROUPS)}, device_id_type=MESH
        )

    @pl.loop(1, 8)
    def _(d):
        pl.semaphore_signal(
            barrier, inc=1, device_id={"tp": lax.rem(t + d, 8)}, device_id_type=MESH
        )

    plane = lax.rem(g // 2, 4)
    turn = 2 * z - 1

    @pl.loop(0, 16)
    def _(d):
        far = lax.rem(plane + 2 - (d % 2) * turn, 4)
        to = (d // 4) * 8 + far * 2 + (d // 2) % 2
        pl.semaphore_signal(
            barrier, inc=1, device_id={"grp": to, "tp": peer_t}, device_id_type=MESH
        )

    own_keys = pltpu.make_async_copy(pool_ref, kbuf.at[x], wsem.at[0])
    own_keys.start()
    weights = [
        pltpu.make_async_copy(wuv_hbm, wuv, wsem.at[1]),
        pltpu.make_async_copy(wout_hbm, wout, wsem.at[2]),
        pltpu.make_async_copy(wgate_hbm, wgate, wsem.at[3]),
        pltpu.make_async_copy(wup_hbm, wup, wsem.at[4]),
        pltpu.make_async_copy(wdown_hbm, wdown, wsem.at[5]),
    ]
    for copy in weights:
        copy.start()
    pending["own_keys"] = own_keys.wait
    pending["weights"] = lambda: [copy.wait() for copy in weights]

    half = iota((8, 64), 1) < 32
    for k in range(0, 4, 2):
        for r in range(3):
            marks = []
            for n in (k * 3 + r, (k + 1) * 3 + r):
                length = context_ref[n]
                marks.append(
                    jnp.where(half, length // 64, length % 64).astype(F32).astype(BF16)
                )
            for s in range(4):
                for h in range(2):
                    row = jnp.concatenate([queries_ref[(k + h) * 3 + r, s], marks[h]], axis=1)
                    for w in range(TILES):
                        u = (r * 4 + s) * TILES + w
                        send_ref[k + u % 2, u // 2, 8 * h : 8 * h + 8] = row[
                            :, 128 * w : 128 * (w + 1)
                        ]
    for j in range(8):

        @pl.when(t == j)
        def _():
            at = slice(SLAB * j, SLAB * (j + 1))
            gain_slab[0, :SLAB] = gain_ref[at]
            gain_slab[:, SLAB:] = jnp.zeros((1, SLABW - SLAB), F32)
            for k in range(0, 4, 2):

                def line(n, b):
                    if b < 3:
                        block = tail_ref[n * 3 + b].astype(F32)
                    else:
                        block = resid_ref[n * 3 + b - 3, :, at].astype(F32)
                    return jnp.pad(block, ((0, 0), (0, WIDE - block.shape[1])))

                for e in range(3):
                    block = jnp.concatenate(
                        [line(k, 2 * e), line(k, 2 * e + 1), line(k + 1, 2 * e), line(k + 1, 2 * e + 1)],
                        axis=0,
                    ).astype(BF16)
                    for w in range(TILES):
                        send_ref[4, (e * 2 + k // 2) * TILES + w] = block[
                            :, 128 * w : 128 * (w + 1)
                        ]

    @pl.when(g < NP)
    def _():
        for w in range(TILES):
            h1[w // 2][w % 2, g] = send_ref[w, g]

    pl.semaphore_wait(barrier, GROUPS - 1 + 7 + 16)

    def hop1_sent(c):
        chunk = pl.ds(*CUTS[c])

        @pl.when(g >= NP)
        def _():
            drain(send_ref.at[chunk, pl.ds(0, NP)], hsend.at[c])

        @pl.when(g < NP)
        def _():
            drain(send_ref.at[chunk, pl.ds(0, NP - 1)], hsend.at[c])

    for c in range(3):
        chunk = pl.ds(*CUTS[c])

        @pl.loop(1, GROUPS)
        def _(d):
            to = lax.rem(g + d, GROUPS)

            @pl.when(to < NP)
            def _():
                pltpu.make_async_remote_copy(
                    src_ref=send_ref.at[chunk, to],
                    dst_ref=h1[c].at[:, g],
                    send_sem=hsend.at[c],
                    recv_sem=hrecv.at[c],
                    device_id={"grp": to},
                    device_id_type=MESH,
                ).start()

        pending["hop1_sent", c] = functools.partial(hop1_sent, c)

    place, group = iota((GROUPS, 128), 1), iota((GROUPS, 128), 0)
    inv_vec[...] = jnp.zeros((8, 128), jnp.int32)
    columns = reads_vec[...].T
    for k in range(4):
        asked_here = columns[:, k : k + 1] == place
        inv_vec[k : k + 1, :] = jnp.max(
            jnp.where(asked_here, group, 0), axis=0, keepdims=True
        )
    askers = pltpu.make_async_copy(inv_vec, inv_ref, wsem.at[6])
    askers.start()
    offset = iota((1, 128), 1)
    for j in range(48):
        pos_ref[j // 6, :, (j % 6) * 128 : (j % 6 + 1) * 128] = (
            table_ref[g, j] * 128 + offset
        ).astype(F32)
    askers.wait()

    to_right = pltpu.make_async_remote_copy(
        src_ref=pool_ref,
        dst_ref=kbuf.at[x],
        send_sem=ksend.at[0],
        recv_sem=krecv.at[0],
        device_id={"tp": right_t},
        device_id_type=MESH,
    )
    to_left = pltpu.make_async_remote_copy(
        src_ref=pool_ref,
        dst_ref=kbuf.at[x],
        send_sem=ksend.at[1],
        recv_sem=krecv.at[1],
        device_id={"tp": left_t},
        device_id_type=MESH,
    )
    to_right.start()
    to_left.start()
    pending["right_sent"] = to_right.wait_send
    pending["left_sent"] = to_left.wait_send
    pending["from_left"] = to_right.wait_recv
    pending["from_right"] = to_left.wait_recv

    def hop2_sent(c):
        @pl.when(g < NP)
        def _():
            drain(s2.at[pl.ds(*CUTS[c]), pl.ds(0, GROUPS - 1)], hsend.at[3 + c])

    near = lax.rem(plane + turn + 4, 4)
    far = lax.rem(plane + 2, 4)

    def hop2_arrived(c):
        chunk = pl.ds(*CUTS[c])
        count = jnp.int32(NP)
        if c < 2:
            count = GROUPS - 2 * jnp.where((plane == 3) | (far == 3), 1, 0)
            count = count - 4 * jnp.where(near == 3, 1, 0)
        count = count - jnp.where(g < NP, 1, 0)
        for n in range(GROUPS - 5, GROUPS + 1):

            @pl.when(count == n)
            def _():
                drain(q1.at[chunk, pl.ds(0, n)], hrecv.at[3 + c])

    for c in range(3):

        @pl.when(g < NP)
        def _():
            chunk = pl.ds(*CUTS[c])
            tiles = range(CUTS[c][0], CUTS[c][0] + CUTS[c][1])
            drain(h1[c].at[:, pl.ds(0, GROUPS - 1)], hrecv.at[c])
            kp = (0, 1, lax.rem(g // TILES, 2))[c]
            upper = iota((16, 128), 0) < 8

            def picked(w, to):
                first = h1[c][w % 2, inv_ref[2 * kp, to]]
                second = h1[c][w % 2, inv_ref[2 * kp + 1, to]]
                return jnp.where(upper, first, second)

            @pl.loop(1, GROUPS)
            def _(d):
                to = lax.rem(g + d, GROUPS)
                for w in tiles:
                    s2[w, to] = picked(w, to)
                away = lax.rem(lax.rem(to // 2, 4) - plane + 4, 4)
                crossing = (away == 2) | (away == 2 - turn)

                def hop2(dst, device):
                    pltpu.make_async_remote_copy(
                        src_ref=s2.at[chunk, to],
                        dst_ref=dst.at[chunk, g],
                        send_sem=hsend.at[3 + c],
                        recv_sem=hrecv.at[3 + c],
                        device_id=device,
                        device_id_type=MESH,
                    ).start()

                if c == 2:
                    hop2(q1, {"grp": to})
                else:
                    pl.when(crossing)(lambda: hop2(q2, {"grp": to, "tp": peer_t}))
                    pl.when(jnp.logical_not(crossing))(lambda: hop2(q1, {"grp": to}))

            for w in tiles:
                q1[w, g] = picked(w, g)

        pending["hop2_sent", c] = functools.partial(hop2_sent, c)
        pending["hop2", c] = functools.partial(hop2_arrived, c)

    def swap_arrived(c):
        drain(q2.at[pl.ds(*CUTS[c])], zrecv.at[c])

    def swap_sent(c):
        drain(q2.at[pl.ds(*CUTS[c])], zsend.at[c])

    def swap(c):
        finish(("hop2", c))
        for src, dst, at in ((q1, q2, plane), (q1, q2, near), (q2, q1, near), (q2, q1, far)):
            for y in range(4):
                part = pl.ds(8 * y + 2 * at, 2)
                pltpu.make_async_remote_copy(
                    src_ref=src.at[pl.ds(*CUTS[c]), part],
                    dst_ref=dst.at[pl.ds(*CUTS[c]), part],
                    send_sem=zsend.at[c],
                    recv_sem=zrecv.at[c],
                    device_id={"tp": peer_t},
                    device_id_type=MESH,
                ).start()
        pending["swap_sent", c] = functools.partial(swap_sent, c)
        pending["swap", c] = functools.partial(swap_arrived, c)

    finish("from_left")
    on_right = pltpu.make_async_remote_copy(
        src_ref=kbuf.at[left, pl.ds(0, 3)],
        dst_ref=kbuf.at[left, pl.ds(0, 3)],
        send_sem=ksend.at[2],
        recv_sem=krecv.at[2],
        device_id={"tp": right_t},
        device_id_type=MESH,
    )
    on_right.start()
    finish("from_right")
    on_left = pltpu.make_async_remote_copy(
        src_ref=kbuf.at[right, pl.ds(3, 3)],
        dst_ref=kbuf.at[right, pl.ds(3, 3)],
        send_sem=ksend.at[3],
        recv_sem=krecv.at[3],
        device_id={"tp": left_t},
        device_id_type=MESH,
    )
    on_left.start()
    pending["on_right_sent"] = on_right.wait_send
    pending["on_left_sent"] = on_left.wait_send
    pending["across_1"] = on_right.wait_recv
    pending["across_2"] = on_left.wait_recv
    swap(0)
    swap(1)
    finish("own_keys")

    nq = QP * 16
    nt = EP * 16

    def lines(ref, slot, step, count):
        pieces = []
        for i in range(count):
            units = [i * TILES + w for w in range(TILES)]
            pieces.append(
                jnp.concatenate([ref[slot + u % step, u // step] for u in units], axis=1)
            )
        return jnp.concatenate(pieces, axis=0)

    def keys_of(b, width):
        return jnp.concatenate([kbuf[b, j, :width] for j in range(6)], axis=1)

    def attend(rows, buf, tail=None):
        count = rows.shape[0]
        lengths = rows[:, 576:577].astype(F32) * 64.0 + rows[:, 608:609].astype(F32)
        top = jnp.full((count, 1), NEGATIVE, F32)
        if tail is not None:
            top = jnp.max(tail, axis=1, keepdims=True)
        for i, b in enumerate((x, left, right, across)):
            if i == 3 and "across_1" in pending:
                finish("across_1", "across_2")
            scores = jnp.dot(rows[:, :576], keys_of(b, 576), preferred_element_type=F32)
            scores = jnp.where(pos_ref[b * 2 + z] < lengths, scores * SCALE2, NEGATIVE)
            buf[i] = scores
            top = jnp.maximum(top, jnp.max(scores, axis=1, keepdims=True))
        den = jnp.zeros((count, 1), F32)
        acc = jnp.zeros((count, LATENT), F32)
        if tail is not None:
            weight = jnp.exp2(tail - top).astype(BF16)
            den = jnp.sum(weight.astype(F32), axis=1, keepdims=True)
            acc = jnp.dot(weight, extra[:, :LATENT], preferred_element_type=F32)
        for i, b in enumerate((x, left, right, across)):
            weight = jnp.exp2(buf[i] - top).astype(BF16)
            den = den + jnp.sum(weight.astype(F32), axis=1, keepdims=True)
            acc = acc + lax.dot_general(
                weight, keys_of(b, LATENT), NT, preferred_element_type=F32
            )
        return top, den, acc

    diagonal = iota((HALF, HALF), 0) == iota((HALF, HALF), 1)
    n, m = iota((HALF, nt), 0), iota((HALF, nt), 1)
    line = (m // 32) * 8 + m % 8
    in_place = (line // 4 == n // 64) & (line % 4 <= (n // 16) % 4)
    own_top, own_den = [], []
    for c in range(2):
        finish(("swap", c))
        top, den, acc = attend(lines(q2, 2 * c, 2, 12), sbuf.at[0])
        numer_out[c] = (acc / den).astype(BF16)
        lse = top + jnp.log2(den)
        lse_out[c] = jnp.broadcast_to(
            jnp.sum(jnp.where(diagonal, lse, 0.0), axis=0, keepdims=True), (8, HALF)
        )
        for s, (src, dst) in enumerate([(numer_out, numer_in), (lse_out, lse_in)]):
            copy = pltpu.make_async_remote_copy(
                src_ref=src.at[c],
                dst_ref=dst.at[c],
                send_sem=zsend.at[2 + 2 * c + s],
                recv_sem=zrecv.at[2 + 2 * c + s],
                device_id={"tp": peer_t},
                device_id_type=MESH,
            )
            copy.start()
            pending["back_sent", c, s] = copy.wait_send
            pending["back", c, s] = copy.wait_recv
        if c == 0:
            finish(("hop2", 2))
            extra = lines(q1, 4, 1, EP)
        rows = lines(q1, 2 * c, 2, 12)
        tail = lax.dot_general(
            rows[:, :576], extra[:, :576], NT, preferred_element_type=F32
        )
        seen = in_place & ((m // 8) % 4 == 2 * c + (n // 8) % 2)
        tail = jnp.where(seen, tail * SCALE2, NEGATIVE)
        top, den, acc = attend(rows, sbuf.at[1], tail)
        own_top.append(top)
        own_den.append(den)
        acc_own[HALF * c : HALF * (c + 1)] = acc
    finish("weights")
    for c in range(2):
        finish(("back", c, 0), ("back", c, 1))
        at = slice(HALF * c, HALF * (c + 1))
        lse = jnp.sum(jnp.where(diagonal, lse_in[c, 0:1, :], 0.0), axis=1, keepdims=True)
        both = jnp.maximum(own_top[c], lse)
        mine = jnp.exp2(own_top[c] - both)
        theirs = jnp.exp2(lse - both)
        scaled = 1.0 / (own_den[c] * mine + theirs)
        latent[at] = (
            acc_own[at] * (mine * scaled) + numer_in[c].astype(F32) * (theirs * scaled)
        ).astype(BF16)

    head_of = iota((nq, 128), 0) % 8
    for h in range(8):
        value = jnp.dot(latent[...], wuv[h], preferred_element_type=F32)
        flatm[:, h * 128 : (h + 1) * 128] = jnp.where(head_of == h, value, 0.0).astype(BF16)
    o, n = iota((ROWS, nq), 0), iota((ROWS, nq), 1)
    chosen = (n % HALF) // 16 == o % 12
    chosen = chosen & ((n // HALF) * 2 + (n // 8) % 2 == o // 12)
    flat = jnp.dot(
        jnp.where(chosen, 1.0, 0.0).astype(BF16), flatm[...], preferred_element_type=F32
    ).astype(BF16)

    def spread(part, dst, s):
        for d in range(1, 8):
            to = lax.rem(t + d, 8)
            pltpu.make_async_remote_copy(
                src_ref=part(to),
                dst_ref=dst.at[t],
                send_sem=tsend.at[s],
                recv_sem=trecv.at[s],
                device_id={"tp": to},
                device_id_type=MESH,
            ).start()
        pending["spread_sent", s] = lambda: drain(rs1.at[pl.ds(0, 7)], tsend.at[s])
        pending["spread", s] = lambda: drain(dst.at[pl.ds(0, 7)], trecv.at[s])

    def slabs(left_side, weight, dst):
        for j in range(4):
            wide = jnp.dot(
                left_side, weight[:, 896 * j : 896 * (j + 1)], preferred_element_type=F32
            ).astype(BF16)
            dst[2 * j, :, :SLAB] = wide[:, :SLAB]
            dst[2 * j + 1, :, :SLAB] = wide[:, SLAB:]

    mix[0, :, :, SLAB:] = jnp.zeros((8, ROWS, SLABW - SLAB), BF16)
    mix[1, :, :, SLAB:] = jnp.zeros((8, ROWS, SLABW - SLAB), BF16)
    slabs(flat, wout, mix.at[0])
    spread(lambda to: mix.at[0, to], rs1, 0)
    rs1[t] = mix[0, t]
    o, m = iota((ROWS, nt), 0), iota((ROWS, nt), 1)
    line = (m // 32) * 8 + m % 8
    chosen = (line - 12 == o % 12) & ((m // 8) % 4 == o // 12)
    hidden = jnp.dot(
        jnp.where(chosen, 1.0, 0.0).astype(BF16),
        extra[:, :SLABW],
        preferred_element_type=F32,
    )
    finish(("spread", 0))
    for j in range(8):
        hidden = hidden + rs1[j].astype(F32)
    lane = iota((ROWS, SLABW), 1)
    hidden = jnp.where(lane < SLAB, hidden, 0.0)
    square = jnp.sum(hidden * hidden, axis=1, keepdims=True)
    high = square.astype(BF16).astype(F32)
    low = square - high
    packed = jnp.where(
        lane < SLAB, hidden * gain_slab[...], jnp.where(lane < SLAB + 32, high, low)
    ).astype(BF16)
    agout[...] = packed
    spread(lambda to: agout, ag, 1)
    ag[t] = packed

    o, m = iota((64, ROWS), 0), iota((64, ROWS), 1)

    def placed(chosen, columns):
        return jnp.dot(
            jnp.where((o // 16 == m // 12) & chosen, 1.0, 0.0).astype(BF16),
            columns,
            preferred_element_type=F32,
        )

    rounded = hidden.astype(BF16)
    wide = placed(o % 16 == m % 12, rounded[:, :RET])
    rest = [
        placed(o % 16 - 12 + 4 * r == m % 12, rounded[:, RET:SLAB]) for r in range(3)
    ]
    rest = jnp.concatenate(rest + [jnp.zeros((64, RET - 192), F32)], axis=1)
    lower = iota((64, RET), 0) % 16 >= 12
    block = jnp.where(lower, rest, wide).astype(BF16)
    for i in range(12):
        home_out[i] = block[16 * (i // 3) : 16 * (i // 3) + 16, 128 * (i % 3) : 128 * (i % 3 + 1)]
        copy = pltpu.make_async_remote_copy(
            src_ref=home_out.at[i],
            dst_ref=home_mid.at[g],
            send_sem=bsend.at[i],
            recv_sem=brecv.at[0],
            device_id={"grp": i},
            device_id_type=MESH,
        )

        @pl.when(g != i)
        def _():
            copy.start()

        @pl.when(g == i)
        def _():
            home_mid[g] = home_out[i]

    def home_sent():
        for i in range(12):

            @pl.when(g != i)
            def _():
                drain(home_out.at[i], bsend.at[i])

        @pl.when(g < 12)
        def _():
            drain(home_next.at[pl.ds(0, GROUPS - 1)], bsend.at[12])

    def home_arrived():
        @pl.when(g < 12)
        def _():
            drain(home_in.at[pl.ds(0, 11)], brecv.at[1])

        @pl.when(g >= 12)
        def _():
            drain(home_in.at[pl.ds(0, 12)], brecv.at[1])

    finish(("spread", 1))
    total = jnp.zeros((ROWS, 1), F32)
    gate = jnp.zeros((ROWS, 128), F32)
    upward = jnp.zeros((ROWS, 128), F32)
    for j in range(8):
        block = ag[j]
        total = total + (
            block[:, SLAB : SLAB + 1].astype(F32) + block[:, SLAB + 32 : SLAB + 33].astype(F32)
        )
        at = slice(SLAB * j, SLAB * (j + 1))
        gate = gate + jnp.dot(block[:, :SLAB], wgate[at], preferred_element_type=F32)
        upward = upward + jnp.dot(block[:, :SLAB], wup[at], preferred_element_type=F32)
    factor = lax.rsqrt(total * (1.0 / 3584.0) + EPSILON)
    gate = gate * factor
    upward = upward * factor
    active = (gate / (1.0 + jnp.exp(-gate)) * upward).astype(BF16)

    fin[...] = placed(o % 16 == m % 12, active).astype(BF16).reshape(4, 16, 128)

    def answer(to):
        slot = jnp.where(reads_ref[3, to] == g, 3, 0)
        slot = jnp.where(reads_ref[2, to] == g, 2, slot)
        slot = jnp.where(reads_ref[1, to] == g, 1, slot)
        return fin[slot]

    @pl.loop(1, GROUPS)
    def _(d):
        to = lax.rem(g + d, GROUPS)
        sback[to] = answer(to)
        pltpu.make_async_remote_copy(
            src_ref=sback.at[to],
            dst_ref=rback.at[g],
            send_sem=hsend.at[6],
            recv_sem=hrecv.at[6],
            device_id={"grp": to},
            device_id_type=MESH,
        ).start()

    rback[g] = answer(g)
    pending["return_sent"] = lambda: drain(sback.at[pl.ds(0, GROUPS - 1)], hsend.at[6])
    pending["return"] = lambda: drain(rback.at[pl.ds(0, GROUPS - 1)], hrecv.at[6])

    @pl.when(g < 12)
    def _():
        drain(home_mid.at[pl.ds(0, GROUPS - 1)], brecv.at[0])
        k = g // 3

        @pl.loop(1, GROUPS)
        def _(d):
            to = lax.rem(g + d, GROUPS)
            home_next[to] = home_mid[reads_ref[k, to]]
            pltpu.make_async_remote_copy(
                src_ref=home_next.at[to],
                dst_ref=home_in.at[g],
                send_sem=bsend.at[12],
                recv_sem=brecv.at[1],
                device_id={"grp": to},
                device_id_type=MESH,
            ).start()

        home_in[g] = home_mid[reads_ref[k, g]]

    pending["home_sent"] = home_sent
    pending["home"] = home_arrived
    finish("return")
    o, m = iota((ROWS, 64), 0), iota((ROWS, 64), 1)
    blocks = jnp.concatenate([rback[reads_ref[k, g]] for k in range(4)], axis=0)
    active = jnp.dot(
        jnp.where((o // 12 == m // 16) & (o % 12 == m % 16), 1.0, 0.0).astype(BF16),
        blocks,
        preferred_element_type=F32,
    ).astype(BF16)
    slabs(active, wdown, mix.at[1])
    spread(lambda to: mix.at[1, to], rs2, 2)
    rs2[t] = mix[1, t]
    finish("home")
    finish(("spread", 2))
    summed = rs2[0].astype(F32)
    for j in range(1, 8):
        summed = summed + rs2[j].astype(F32)
    for k in range(4):
        block = jnp.concatenate([home_in[3 * k + j] for j in range(3)], axis=1).astype(F32)
        for r in range(3):
            at = slice(12 * k + 4 * r, 12 * k + 4 * r + 4)
            out_ref[3 * k + r, :, :RET] = (
                summed[at, :RET] + block[4 * r : 4 * r + 4]
            ).astype(BF16)
            out_ref[3 * k + r, :, RET:] = (
                summed[at, RET:SLAB] + block[12:, 64 * r : 64 * r + 64]
            ).astype(BF16)

    finish()


def on_device(
    pool_pages,
    page_table,
    read_list,
    context,
    queries,
    tail_keys,
    residual,
    w_uv,
    w_out,
    norm_gain,
    w_gate,
    w_up,
    w_down,
):
    smem = pl.BlockSpec(memory_space=pltpu.SMEM)
    vmem = pl.BlockSpec(memory_space=pltpu.VMEM)
    anym = pl.BlockSpec(memory_space=pl.ANY)
    dma = pltpu.SemaphoreType.DMA
    nq = QP * 16
    return pl.pallas_call(
        kernel,
        out_shape=jax.ShapeDtypeStruct((12, 4, SLAB), BF16),
        in_specs=[smem] * 3 + [vmem] * 5 + [anym] * 6,
        out_specs=vmem,
        scratch_shapes=[
            pltpu.VMEM((TILES, NP, 16, 128), BF16),
            pltpu.VMEM((8, 128), jnp.int32),
            pltpu.SMEM((8, 128), jnp.int32),
            pltpu.VMEM((8, 1, 768), F32),
            pltpu.VMEM((1, SLABW), F32),
            pltpu.VMEM((2, GROUPS, 16, 128), BF16),
            pltpu.VMEM((2, GROUPS, 16, 128), BF16),
            pltpu.VMEM((1, GROUPS, 16, 128), BF16),
            pltpu.VMEM((TILES, GROUPS, 16, 128), BF16),
            pltpu.VMEM((TILES, GROUPS, 16, 128), BF16),
            pltpu.VMEM((4, GROUPS, 16, 128), BF16),
            pltpu.VMEM((4, 6, 576, 128), BF16),
            pltpu.VMEM((nq, LATENT), F32),
            pltpu.VMEM((2, 4, HALF, 768), F32),
            pltpu.VMEM((2, HALF, LATENT), BF16),
            pltpu.VMEM((2, HALF, LATENT), BF16),
            pltpu.VMEM((2, 8, HALF), F32),
            pltpu.VMEM((2, 8, HALF), F32),
            pltpu.VMEM((nq, LATENT), BF16),
            pltpu.VMEM((nq, 1024), BF16),
            pltpu.VMEM((8, 512, 128), BF16),
            pltpu.VMEM((1024, 3584), BF16),
            pltpu.VMEM((3584, 128), BF16),
            pltpu.VMEM((3584, 128), BF16),
            pltpu.VMEM((128, 3584), BF16),
            pltpu.VMEM((2, 8, ROWS, SLABW), BF16),
            pltpu.VMEM((8, ROWS, SLABW), BF16),
            pltpu.VMEM((ROWS, SLABW), BF16),
            pltpu.VMEM((8, ROWS, SLABW), BF16),
            pltpu.VMEM((8, ROWS, SLABW), BF16),
            pltpu.VMEM((4, 16, 128), BF16),
            pltpu.VMEM((GROUPS, 16, 128), BF16),
            pltpu.VMEM((GROUPS, 16, 128), BF16),
            pltpu.VMEM((12, 16, 128), BF16),
            pltpu.VMEM((GROUPS, 16, 128), BF16),
            pltpu.VMEM((GROUPS, 16, 128), BF16),
            pltpu.VMEM((12, 16, 128), BF16),
            dma((7,)),
            dma((4,)),
            dma((4,)),
            dma((7,)),
            dma((7,)),
            dma((6,)),
            dma((6,)),
            dma((3,)),
            dma((3,)),
            dma((13,)),
            dma((2,)),
        ],
        compiler_params=pltpu.CompilerParams(
            collective_id=0, has_side_effects=True, vmem_limit_bytes=56 * 1024 * 1024
        ),
    )(
        read_list.T,
        page_table,
        context,
        read_list.T,
        queries,
        tail_keys,
        residual,
        norm_gain,
        pool_pages.reshape(6, 128, 576).transpose(0, 2, 1),
        w_uv,
        w_out,
        w_gate,
        w_up,
        w_down,
    )


def solution(mesh):
    placed = (
        P("grp", "tp", None, None),
        P(),
        P(),
        P("grp"),
        P("grp", None, "tp", None),
        P("grp", None, None),
        P("grp", None, None),
        P("tp", None, None),
        P("tp", None),
        P(),
        P(None, "tp"),
        P(None, "tp"),
        P("tp", None),
    )
    return jax.shard_map(
        on_device, mesh=mesh, in_specs=placed, out_specs=P("grp", None, "tp"), check_vma=False
    )
```

```python
import functools

import jax
import jax.numpy as jnp
import numpy as np
from jax import lax
from jax.experimental import pallas as pl
from jax.experimental.pallas import tpu as pltpu
from jax.sharding import PartitionSpec as P

LATENT = 512
SCALE = 192.0 ** (-0.5)
SCALE2 = SCALE * 1.4426950408889634
NEGATIVE = -1e30
EPSILON = 1e-06
MESH = pl.DeviceIdType.MESH
F32 = jnp.float32
BF16 = jnp.bfloat16

GROUPS = 32
QP = 24
EP = 6
NP = QP + EP
WIDE = 640
SLAB = 448
SLABW = 512
ROWS = 48
RET = 384
TILES = WIDE // 128
CUTS = ((0, 2), (2, 2), (4, 1))
HALF = 192
NT = (((1,), (1,)), ((), ()))


def drain(ref, sem):
    pltpu.make_async_copy(ref, ref, sem).wait()


def iota(shape, dim):
    return lax.broadcasted_iota(jnp.int32, shape, dim)


def kernel(
    reads_ref,
    table_ref,
    context_ref,
    reads_vec,
    queries_ref,
    tail_ref,
    resid_ref,
    gain_ref,
    pool_ref,
    wuv_hbm,
    wout_hbm,
    wgate_hbm,
    wup_hbm,
    wdown_hbm,
    out_ref,
    send_ref,
    inv_vec,
    inv_ref,
    pos_ref,
    gain_slab,
    h1_0,
    h1_1,
    h1_2,
    s2,
    q1,
    q2,
    kbuf,
    acc_own,
    sbuf,
    numer_out,
    numer_in,
    lse_out,
    lse_in,
    latent,
    flatm,
    wuv,
    wout,
    wgate,
    wup,
    wdown,
    mix,
    rs1,
    agout,
    ag,
    rs2,
    fin,
    sback,
    rback,
    home_out,
    home_mid,
    home_next,
    home_in,
    wsem,
    ksend,
    krecv,
    hsend,
    hrecv,
    zsend,
    zrecv,
    tsend,
    trecv,
    bsend,
    brecv,
):
    g = lax.axis_index("grp")
    t = lax.axis_index("tp")
    x, z = t // 2, t % 2
    right = lax.rem(x + 1, 4)
    left = lax.rem(x + 3, 4)
    across = lax.rem(x + 2, 4)
    right_t = right * 2 + z
    left_t = left * 2 + z
    peer_t = x * 2 + (1 - z)

    pending = {}
    h1 = (h1_0, h1_1, h1_2)

    def finish(*names):
        for name in names or list(pending):
            pending.pop(name)()

    barrier = pltpu.get_barrier_semaphore()

    @pl.loop(1, GROUPS)
    def _(d):
        pl.semaphore_signal(
            barrier, inc=1, device_id={"grp": lax.rem(g + d, GROUPS)}, device_id_type=MESH
        )

    @pl.loop(1, 8)
    def _(d):
        pl.semaphore_signal(
            barrier, inc=1, device_id={"tp": lax.rem(t + d, 8)}, device_id_type=MESH
        )

    plane = lax.rem(g // 2, 4)
    turn = 2 * z - 1

    @pl.loop(0, 16)
    def _(d):
        far = lax.rem(plane + 2 - (d % 2) * turn, 4)
        to = (d // 4) * 8 + far * 2 + (d // 2) % 2
        pl.semaphore_signal(
            barrier, inc=1, device_id={"grp": to, "tp": peer_t}, device_id_type=MESH
        )

    own_keys = pltpu.make_async_copy(pool_ref, kbuf.at[x], wsem.at[0])
    own_keys.start()
    weights = [
        pltpu.make_async_copy(wuv_hbm, wuv, wsem.at[1]),
        pltpu.make_async_copy(wout_hbm, wout, wsem.at[2]),
        pltpu.make_async_copy(wgate_hbm, wgate, wsem.at[3]),
        pltpu.make_async_copy(wup_hbm, wup, wsem.at[4]),
        pltpu.make_async_copy(wdown_hbm, wdown, wsem.at[5]),
    ]
    for copy in weights:
        copy.start()
    pending["own_keys"] = own_keys.wait
    pending["weights"] = lambda: [copy.wait() for copy in weights]

    half = iota((8, 64), 1) < 32
    for k in range(0, 4, 2):
        for r in range(3):
            marks = []
            for n in (k * 3 + r, (k + 1) * 3 + r):
                length = context_ref[n]
                marks.append(
                    jnp.where(half, length // 64, length % 64).astype(F32).astype(BF16)
                )
            for s in range(4):
                for h in range(2):
                    row = jnp.concatenate([queries_ref[(k + h) * 3 + r, s], marks[h]], axis=1)
                    for w in range(TILES):
                        u = (r * 4 + s) * TILES + w
                        send_ref[k + u % 2, u // 2, 8 * h : 8 * h + 8] = row[
                            :, 128 * w : 128 * (w + 1)
                        ]
    for j in range(8):

        @pl.when(t == j)
        def _():
            at = slice(SLAB * j, SLAB * (j + 1))
            gain_slab[0, :SLAB] = gain_ref[at]
            gain_slab[:, SLAB:] = jnp.zeros((1, SLABW - SLAB), F32)
            for k in range(0, 4, 2):

                def line(n, b):
                    if b < 3:
                        block = tail_ref[n * 3 + b].astype(F32)
                    else:
                        block = resid_ref[n * 3 + b - 3, :, at].astype(F32)
                    return jnp.pad(block, ((0, 0), (0, WIDE - block.shape[1])))

                for e in range(3):
                    block = jnp.concatenate(
                        [line(k, 2 * e), line(k, 2 * e + 1), line(k + 1, 2 * e), line(k + 1, 2 * e + 1)],
                        axis=0,
                    ).astype(BF16)
                    for w in range(TILES):
                        send_ref[4, (e * 2 + k // 2) * TILES + w] = block[
                            :, 128 * w : 128 * (w + 1)
                        ]

    @pl.when(g < NP)
    def _():
        for w in range(TILES):
            h1[w // 2][w % 2, g] = send_ref[w, g]

    pl.semaphore_wait(barrier, GROUPS - 1 + 7 + 16)

    def hop1_sent(c):
        chunk = pl.ds(*CUTS[c])

        @pl.when(g >= NP)
        def _():
            drain(send_ref.at[chunk, pl.ds(0, NP)], hsend.at[c])

        @pl.when(g < NP)
        def _():
            drain(send_ref.at[chunk, pl.ds(0, NP - 1)], hsend.at[c])

    def hop1(c):
        chunk = pl.ds(*CUTS[c])

        @pl.loop(1, GROUPS)
        def _(d):
            to = lax.rem(g + d, GROUPS)

            @pl.when(to < NP)
            def _():
                pltpu.make_async_remote_copy(
                    src_ref=send_ref.at[chunk, to],
                    dst_ref=h1[c].at[:, g],
                    send_sem=hsend.at[c],
                    recv_sem=hrecv.at[c],
                    device_id={"grp": to},
                    device_id_type=MESH,
                ).start()

        pending["hop1_sent", c] = functools.partial(hop1_sent, c)

    hop1(0)
    hop1(1)

    place, group = iota((GROUPS, 128), 1), iota((GROUPS, 128), 0)
    inv_vec[...] = jnp.zeros((8, 128), jnp.int32)
    columns = reads_vec[...].T
    for k in range(4):
        asked_here = columns[:, k : k + 1] == place
        inv_vec[k : k + 1, :] = jnp.max(
            jnp.where(asked_here, group, 0), axis=0, keepdims=True
        )
    askers = pltpu.make_async_copy(inv_vec, inv_ref, wsem.at[6])
    askers.start()
    offset = iota((1, 128), 1)
    for j in range(48):
        pos_ref[j // 6, :, (j % 6) * 128 : (j % 6 + 1) * 128] = (
            table_ref[g, j] * 128 + offset
        ).astype(F32)
    askers.wait()

    to_right = pltpu.make_async_remote_copy(
        src_ref=pool_ref,
        dst_ref=kbuf.at[x],
        send_sem=ksend.at[0],
        recv_sem=krecv.at[0],
        device_id={"tp": right_t},
        device_id_type=MESH,
    )
    to_left = pltpu.make_async_remote_copy(
        src_ref=pool_ref,
        dst_ref=kbuf.at[x],
        send_sem=ksend.at[1],
        recv_sem=krecv.at[1],
        device_id={"tp": left_t},
        device_id_type=MESH,
    )
    to_right.start()
    to_left.start()
    pending["right_sent"] = to_right.wait_send
    pending["left_sent"] = to_left.wait_send
    pending["from_left"] = to_right.wait_recv
    pending["from_right"] = to_left.wait_recv

    def hop2_sent(c):
        @pl.when(g < NP)
        def _():
            drain(s2.at[pl.ds(*CUTS[c]), pl.ds(0, GROUPS - 1)], hsend.at[3 + c])

    near = lax.rem(plane + turn + 4, 4)
    far = lax.rem(plane + 2, 4)

    def hop2_arrived(c):
        chunk = pl.ds(*CUTS[c])
        count = jnp.int32(NP)
        if c < 2:
            count = GROUPS - 2 * jnp.where((plane == 3) | (far == 3), 1, 0)
            count = count - 4 * jnp.where(near == 3, 1, 0)
        count = count - jnp.where(g < NP, 1, 0)
        for n in range(GROUPS - 5, GROUPS + 1):

            @pl.when(count == n)
            def _():
                drain(q1.at[chunk, pl.ds(0, n)], hrecv.at[3 + c])

    def route(c):

        @pl.when(g < NP)
        def _():
            chunk = pl.ds(*CUTS[c])
            tiles = range(CUTS[c][0], CUTS[c][0] + CUTS[c][1])
            drain(h1[c].at[:, pl.ds(0, GROUPS - 1)], hrecv.at[c])
            kp = (0, 1, lax.rem(g // TILES, 2))[c]
            upper = iota((16, 128), 0) < 8

            def picked(w, to):
                first = h1[c][w % 2, inv_ref[2 * kp, to]]
                second = h1[c][w % 2, inv_ref[2 * kp + 1, to]]
                return jnp.where(upper, first, second)

            @pl.loop(1, GROUPS)
            def _(d):
                to = lax.rem(g + d, GROUPS)
                for w in tiles:
                    s2[w, to] = picked(w, to)
                away = lax.rem(lax.rem(to // 2, 4) - plane + 4, 4)
                crossing = (away == 2) | (away == 2 - turn)

                def hop2(dst, device):
                    pltpu.make_async_remote_copy(
                        src_ref=s2.at[chunk, to],
                        dst_ref=dst.at[chunk, g],
                        send_sem=hsend.at[3 + c],
                        recv_sem=hrecv.at[3 + c],
                        device_id=device,
                        device_id_type=MESH,
                    ).start()

                if c == 2:
                    hop2(q1, {"grp": to})
                else:
                    pl.when(crossing)(lambda: hop2(q2, {"grp": to, "tp": peer_t}))
                    pl.when(jnp.logical_not(crossing))(lambda: hop2(q1, {"grp": to}))

            for w in tiles:
                q1[w, g] = picked(w, g)

        pending["hop2_sent", c] = functools.partial(hop2_sent, c)
        pending["hop2", c] = functools.partial(hop2_arrived, c)

    route(0)
    route(1)

    def swap_arrived(c):
        drain(q2.at[pl.ds(*CUTS[c])], zrecv.at[c])

    def swap_sent(c):
        drain(q2.at[pl.ds(*CUTS[c])], zsend.at[c])

    def swap(c):
        finish(("hop2", c))
        for src, dst, at in ((q1, q2, plane), (q1, q2, near), (q2, q1, near), (q2, q1, far)):
            for y in range(4):
                part = pl.ds(8 * y + 2 * at, 2)
                pltpu.make_async_remote_copy(
                    src_ref=src.at[pl.ds(*CUTS[c]), part],
                    dst_ref=dst.at[pl.ds(*CUTS[c]), part],
                    send_sem=zsend.at[c],
                    recv_sem=zrecv.at[c],
                    device_id={"tp": peer_t},
                    device_id_type=MESH,
                ).start()
        pending["swap_sent", c] = functools.partial(swap_sent, c)
        pending["swap", c] = functools.partial(swap_arrived, c)

    finish("from_left")
    on_right = pltpu.make_async_remote_copy(
        src_ref=kbuf.at[left, pl.ds(0, 3)],
        dst_ref=kbuf.at[left, pl.ds(0, 3)],
        send_sem=ksend.at[2],
        recv_sem=krecv.at[2],
        device_id={"tp": right_t},
        device_id_type=MESH,
    )
    on_right.start()
    finish("from_right")
    on_left = pltpu.make_async_remote_copy(
        src_ref=kbuf.at[right, pl.ds(3, 3)],
        dst_ref=kbuf.at[right, pl.ds(3, 3)],
        send_sem=ksend.at[3],
        recv_sem=krecv.at[3],
        device_id={"tp": left_t},
        device_id_type=MESH,
    )
    on_left.start()
    pending["on_right_sent"] = on_right.wait_send
    pending["on_left_sent"] = on_left.wait_send
    pending["across_1"] = on_right.wait_recv
    pending["across_2"] = on_left.wait_recv
    swap(0)
    hop1(2)
    swap(1)
    finish("own_keys")

    nq = QP * 16
    nt = EP * 16

    def lines(ref, slot, step, count):
        pieces = []
        for i in range(count):
            units = [i * TILES + w for w in range(TILES)]
            pieces.append(
                jnp.concatenate([ref[slot + u % step, u // step] for u in units], axis=1)
            )
        return jnp.concatenate(pieces, axis=0)

    def keys_of(b, width):
        return jnp.concatenate([kbuf[b, j, :width] for j in range(6)], axis=1)

    def attend(rows, buf, tail=None):
        count = rows.shape[0]
        lengths = rows[:, 576:577].astype(F32) * 64.0 + rows[:, 608:609].astype(F32)
        top = jnp.full((count, 1), NEGATIVE, F32)
        if tail is not None:
            top = jnp.max(tail, axis=1, keepdims=True)
        for i, b in enumerate((x, left, right, across)):
            if i == 3 and "across_1" in pending:
                finish("across_1", "across_2")
            scores = jnp.dot(rows[:, :576], keys_of(b, 576), preferred_element_type=F32)
            scores = jnp.where(pos_ref[b * 2 + z] < lengths, scores * SCALE2, NEGATIVE)
            buf[i] = scores
            top = jnp.maximum(top, jnp.max(scores, axis=1, keepdims=True))
        den = jnp.zeros((count, 1), F32)
        acc = jnp.zeros((count, LATENT), F32)
        if tail is not None:
            weight = jnp.exp2(tail - top).astype(BF16)
            den = jnp.sum(weight.astype(F32), axis=1, keepdims=True)
            acc = jnp.dot(weight, extra[:, :LATENT], preferred_element_type=F32)
        for i, b in enumerate((x, left, right, across)):
            weight = jnp.exp2(buf[i] - top).astype(BF16)
            den = den + jnp.sum(weight.astype(F32), axis=1, keepdims=True)
            acc = acc + lax.dot_general(
                weight, keys_of(b, LATENT), NT, preferred_element_type=F32
            )
        return top, den, acc

    diagonal = iota((HALF, HALF), 0) == iota((HALF, HALF), 1)
    n, m = iota((HALF, nt), 0), iota((HALF, nt), 1)
    line = (m // 32) * 8 + m % 8
    in_place = (line // 4 == n // 64) & (line % 4 <= (n // 16) % 4)
    own_top, own_den = [], []
    for c in range(2):
        finish(("swap", c))
        top, den, acc = attend(lines(q2, 2 * c, 2, 12), sbuf.at[0])
        numer_out[c] = (acc / den).astype(BF16)
        lse = top + jnp.log2(den)
        lse_out[c] = jnp.broadcast_to(
            jnp.sum(jnp.where(diagonal, lse, 0.0), axis=0, keepdims=True), (8, HALF)
        )
        for s, (src, dst) in enumerate([(numer_out, numer_in), (lse_out, lse_in)]):
            copy = pltpu.make_async_remote_copy(
                src_ref=src.at[c],
                dst_ref=dst.at[c],
                send_sem=zsend.at[2 + 2 * c + s],
                recv_sem=zrecv.at[2 + 2 * c + s],
                device_id={"tp": peer_t},
                device_id_type=MESH,
            )
            copy.start()
            pending["back_sent", c, s] = copy.wait_send
            pending["back", c, s] = copy.wait_recv
        if c == 0:
            route(2)
    finish(("hop2", 2))
    extra = lines(q1, 4, 1, EP)
    for c in range(2):
        rows = lines(q1, 2 * c, 2, 12)
        tail = lax.dot_general(
            rows[:, :576], extra[:, :576], NT, preferred_element_type=F32
        )
        seen = in_place & ((m // 8) % 4 == 2 * c + (n // 8) % 2)
        tail = jnp.where(seen, tail * SCALE2, NEGATIVE)
        top, den, acc = attend(rows, sbuf.at[1], tail)
        own_top.append(top)
        own_den.append(den)
        acc_own[HALF * c : HALF * (c + 1)] = acc
    finish("weights")
    for c in range(2):
        finish(("back", c, 0), ("back", c, 1))
        at = slice(HALF * c, HALF * (c + 1))
        lse = jnp.sum(jnp.where(diagonal, lse_in[c, 0:1, :], 0.0), axis=1, keepdims=True)
        both = jnp.maximum(own_top[c], lse)
        mine = jnp.exp2(own_top[c] - both)
        theirs = jnp.exp2(lse - both)
        scaled = 1.0 / (own_den[c] * mine + theirs)
        latent[at] = (
            acc_own[at] * (mine * scaled) + numer_in[c].astype(F32) * (theirs * scaled)
        ).astype(BF16)

    head_of = iota((nq, 128), 0) % 8
    for h in range(8):
        value = jnp.dot(latent[...], wuv[h], preferred_element_type=F32)
        flatm[:, h * 128 : (h + 1) * 128] = jnp.where(head_of == h, value, 0.0).astype(BF16)
    o, n = iota((ROWS, nq), 0), iota((ROWS, nq), 1)
    chosen = (n % HALF) // 16 == o % 12
    chosen = chosen & ((n // HALF) * 2 + (n // 8) % 2 == o // 12)
    flat = jnp.dot(
        jnp.where(chosen, 1.0, 0.0).astype(BF16), flatm[...], preferred_element_type=F32
    ).astype(BF16)

    def spread(part, dst, s):
        for d in range(1, 8):
            to = lax.rem(t + d, 8)
            pltpu.make_async_remote_copy(
                src_ref=part(to),
                dst_ref=dst.at[t],
                send_sem=tsend.at[s],
                recv_sem=trecv.at[s],
                device_id={"tp": to},
                device_id_type=MESH,
            ).start()
        pending["spread_sent", s] = lambda: drain(rs1.at[pl.ds(0, 7)], tsend.at[s])
        pending["spread", s] = lambda: drain(dst.at[pl.ds(0, 7)], trecv.at[s])

    def slabs(left_side, weight, dst):
        for j in range(4):
            wide = jnp.dot(
                left_side, weight[:, 896 * j : 896 * (j + 1)], preferred_element_type=F32
            ).astype(BF16)
            dst[2 * j, :, :SLAB] = wide[:, :SLAB]
            dst[2 * j + 1, :, :SLAB] = wide[:, SLAB:]

    mix[0, :, :, SLAB:] = jnp.zeros((8, ROWS, SLABW - SLAB), BF16)
    mix[1, :, :, SLAB:] = jnp.zeros((8, ROWS, SLABW - SLAB), BF16)
    slabs(flat, wout, mix.at[0])
    spread(lambda to: mix.at[0, to], rs1, 0)
    rs1[t] = mix[0, t]
    o, m = iota((ROWS, nt), 0), iota((ROWS, nt), 1)
    line = (m // 32) * 8 + m % 8
    chosen = (line - 12 == o % 12) & ((m // 8) % 4 == o // 12)
    hidden = jnp.dot(
        jnp.where(chosen, 1.0, 0.0).astype(BF16),
        extra[:, :SLABW],
        preferred_element_type=F32,
    )
    finish(("spread", 0))
    for j in range(8):
        hidden = hidden + rs1[j].astype(F32)
    lane = iota((ROWS, SLABW), 1)
    hidden = jnp.where(lane < SLAB, hidden, 0.0)
    square = jnp.sum(hidden * hidden, axis=1, keepdims=True)
    high = square.astype(BF16).astype(F32)
    low = square - high
    packed = jnp.where(
        lane < SLAB, hidden * gain_slab[...], jnp.where(lane < SLAB + 32, high, low)
    ).astype(BF16)
    agout[...] = packed
    spread(lambda to: agout, ag, 1)
    ag[t] = packed

    o, m = iota((64, ROWS), 0), iota((64, ROWS), 1)

    def placed(chosen, columns):
        return jnp.dot(
            jnp.where((o // 16 == m // 12) & chosen, 1.0, 0.0).astype(BF16),
            columns,
            preferred_element_type=F32,
        )

    rounded = hidden.astype(BF16)
    wide = placed(o % 16 == m % 12, rounded[:, :RET])
    rest = [
        placed(o % 16 - 12 + 4 * r == m % 12, rounded[:, RET:SLAB]) for r in range(3)
    ]
    rest = jnp.concatenate(rest + [jnp.zeros((64, RET - 192), F32)], axis=1)
    lower = iota((64, RET), 0) % 16 >= 12
    block = jnp.where(lower, rest, wide).astype(BF16)
    for i in range(12):
        home_out[i] = block[16 * (i // 3) : 16 * (i // 3) + 16, 128 * (i % 3) : 128 * (i % 3 + 1)]
        copy = pltpu.make_async_remote_copy(
            src_ref=home_out.at[i],
            dst_ref=home_mid.at[g],
            send_sem=bsend.at[i],
            recv_sem=brecv.at[0],
            device_id={"grp": i},
            device_id_type=MESH,
        )

        @pl.when(g != i)
        def _():
            copy.start()

        @pl.when(g == i)
        def _():
            home_mid[g] = home_out[i]

    def home_sent():
        for i in range(12):

            @pl.when(g != i)
            def _():
                drain(home_out.at[i], bsend.at[i])

        @pl.when(g < 12)
        def _():
            drain(home_next.at[pl.ds(0, GROUPS - 1)], bsend.at[12])

    def home_arrived():
        @pl.when(g < 12)
        def _():
            drain(home_in.at[pl.ds(0, 11)], brecv.at[1])

        @pl.when(g >= 12)
        def _():
            drain(home_in.at[pl.ds(0, 12)], brecv.at[1])

    finish(("spread", 1))
    total = jnp.zeros((ROWS, 1), F32)
    gate = jnp.zeros((ROWS, 128), F32)
    upward = jnp.zeros((ROWS, 128), F32)
    for j in range(8):
        block = ag[j]
        total = total + (
            block[:, SLAB : SLAB + 1].astype(F32) + block[:, SLAB + 32 : SLAB + 33].astype(F32)
        )
        at = slice(SLAB * j, SLAB * (j + 1))
        gate = gate + jnp.dot(block[:, :SLAB], wgate[at], preferred_element_type=F32)
        upward = upward + jnp.dot(block[:, :SLAB], wup[at], preferred_element_type=F32)
    factor = lax.rsqrt(total * (1.0 / 3584.0) + EPSILON)
    gate = gate * factor
    upward = upward * factor
    active = (gate / (1.0 + jnp.exp(-gate)) * upward).astype(BF16)

    fin[...] = placed(o % 16 == m % 12, active).astype(BF16).reshape(4, 16, 128)

    def answer(to):
        slot = jnp.where(reads_ref[3, to] == g, 3, 0)
        slot = jnp.where(reads_ref[2, to] == g, 2, slot)
        slot = jnp.where(reads_ref[1, to] == g, 1, slot)
        return fin[slot]

    @pl.loop(1, GROUPS)
    def _(d):
        to = lax.rem(g + d, GROUPS)
        sback[to] = answer(to)
        pltpu.make_async_remote_copy(
            src_ref=sback.at[to],
            dst_ref=rback.at[g],
            send_sem=hsend.at[6],
            recv_sem=hrecv.at[6],
            device_id={"grp": to},
            device_id_type=MESH,
        ).start()

    rback[g] = answer(g)
    pending["return_sent"] = lambda: drain(sback.at[pl.ds(0, GROUPS - 1)], hsend.at[6])
    pending["return"] = lambda: drain(rback.at[pl.ds(0, GROUPS - 1)], hrecv.at[6])

    @pl.when(g < 12)
    def _():
        drain(home_mid.at[pl.ds(0, GROUPS - 1)], brecv.at[0])
        k = g // 3

        @pl.loop(1, GROUPS)
        def _(d):
            to = lax.rem(g + d, GROUPS)
            home_next[to] = home_mid[reads_ref[k, to]]
            pltpu.make_async_remote_copy(
                src_ref=home_next.at[to],
                dst_ref=home_in.at[g],
                send_sem=bsend.at[12],
                recv_sem=brecv.at[1],
                device_id={"grp": to},
                device_id_type=MESH,
            ).start()

        home_in[g] = home_mid[reads_ref[k, g]]

    pending["home_sent"] = home_sent
    pending["home"] = home_arrived
    finish("return")
    o, m = iota((ROWS, 64), 0), iota((ROWS, 64), 1)
    blocks = jnp.concatenate([rback[reads_ref[k, g]] for k in range(4)], axis=0)
    active = jnp.dot(
        jnp.where((o // 12 == m // 16) & (o % 12 == m % 16), 1.0, 0.0).astype(BF16),
        blocks,
        preferred_element_type=F32,
    ).astype(BF16)
    slabs(active, wdown, mix.at[1])
    spread(lambda to: mix.at[1, to], rs2, 2)
    rs2[t] = mix[1, t]
    finish("home")
    finish(("spread", 2))
    summed = rs2[0].astype(F32)
    for j in range(1, 8):
        summed = summed + rs2[j].astype(F32)
    for k in range(4):
        block = jnp.concatenate([home_in[3 * k + j] for j in range(3)], axis=1).astype(F32)
        for r in range(3):
            at = slice(12 * k + 4 * r, 12 * k + 4 * r + 4)
            out_ref[3 * k + r, :, :RET] = (
                summed[at, :RET] + block[4 * r : 4 * r + 4]
            ).astype(BF16)
            out_ref[3 * k + r, :, RET:] = (
                summed[at, RET:SLAB] + block[12:, 64 * r : 64 * r + 64]
            ).astype(BF16)

    finish()


def on_device(
    pool_pages,
    page_table,
    read_list,
    context,
    queries,
    tail_keys,
    residual,
    w_uv,
    w_out,
    norm_gain,
    w_gate,
    w_up,
    w_down,
):
    smem = pl.BlockSpec(memory_space=pltpu.SMEM)
    vmem = pl.BlockSpec(memory_space=pltpu.VMEM)
    anym = pl.BlockSpec(memory_space=pl.ANY)
    dma = pltpu.SemaphoreType.DMA
    nq = QP * 16
    return pl.pallas_call(
        kernel,
        out_shape=jax.ShapeDtypeStruct((12, 4, SLAB), BF16),
        in_specs=[smem] * 3 + [vmem] * 5 + [anym] * 6,
        out_specs=vmem,
        scratch_shapes=[
            pltpu.VMEM((TILES, NP, 16, 128), BF16),
            pltpu.VMEM((8, 128), jnp.int32),
            pltpu.SMEM((8, 128), jnp.int32),
            pltpu.VMEM((8, 1, 768), F32),
            pltpu.VMEM((1, SLABW), F32),
            pltpu.VMEM((2, GROUPS, 16, 128), BF16),
            pltpu.VMEM((2, GROUPS, 16, 128), BF16),
            pltpu.VMEM((1, GROUPS, 16, 128), BF16),
            pltpu.VMEM((TILES, GROUPS, 16, 128), BF16),
            pltpu.VMEM((TILES, GROUPS, 16, 128), BF16),
            pltpu.VMEM((4, GROUPS, 16, 128), BF16),
            pltpu.VMEM((4, 6, 576, 128), BF16),
            pltpu.VMEM((nq, LATENT), F32),
            pltpu.VMEM((2, 4, HALF, 768), F32),
            pltpu.VMEM((2, HALF, LATENT), BF16),
            pltpu.VMEM((2, HALF, LATENT), BF16),
            pltpu.VMEM((2, 8, HALF), F32),
            pltpu.VMEM((2, 8, HALF), F32),
            pltpu.VMEM((nq, LATENT), BF16),
            pltpu.VMEM((nq, 1024), BF16),
            pltpu.VMEM((8, 512, 128), BF16),
            pltpu.VMEM((1024, 3584), BF16),
            pltpu.VMEM((3584, 128), BF16),
            pltpu.VMEM((3584, 128), BF16),
            pltpu.VMEM((128, 3584), BF16),
            pltpu.VMEM((2, 8, ROWS, SLABW), BF16),
            pltpu.VMEM((8, ROWS, SLABW), BF16),
            pltpu.VMEM((ROWS, SLABW), BF16),
            pltpu.VMEM((8, ROWS, SLABW), BF16),
            pltpu.VMEM((8, ROWS, SLABW), BF16),
            pltpu.VMEM((4, 16, 128), BF16),
            pltpu.VMEM((GROUPS, 16, 128), BF16),
            pltpu.VMEM((GROUPS, 16, 128), BF16),
            pltpu.VMEM((12, 16, 128), BF16),
            pltpu.VMEM((GROUPS, 16, 128), BF16),
            pltpu.VMEM((GROUPS, 16, 128), BF16),
            pltpu.VMEM((12, 16, 128), BF16),
            dma((7,)),
            dma((4,)),
            dma((4,)),
            dma((7,)),
            dma((7,)),
            dma((6,)),
            dma((6,)),
            dma((3,)),
            dma((3,)),
            dma((13,)),
            dma((2,)),
        ],
        compiler_params=pltpu.CompilerParams(
            collective_id=0, has_side_effects=True, vmem_limit_bytes=56 * 1024 * 1024
        ),
    )(
        read_list.T,
        page_table,
        context,
        read_list.T,
        queries,
        tail_keys,
        residual,
        norm_gain,
        pool_pages.reshape(6, 128, 576).transpose(0, 2, 1),
        w_uv,
        w_out,
        w_gate,
        w_up,
        w_down,
    )


def solution(mesh):
    placed = (
        P("grp", "tp", None, None),
        P(),
        P(),
        P("grp"),
        P("grp", None, "tp", None),
        P("grp", None, None),
        P("grp", None, None),
        P("tp", None, None),
        P("tp", None),
        P(),
        P(None, "tp"),
        P(None, "tp"),
        P("tp", None),
    )
    return jax.shard_map(
        on_device, mesh=mesh, in_specs=placed, out_specs=P("grp", None, "tp"), check_vma=False
    )
```

```python
import functools

import jax
import jax.numpy as jnp
import numpy as np
from jax import lax
from jax.experimental import pallas as pl
from jax.experimental.pallas import tpu as pltpu
from jax.sharding import PartitionSpec as P

LATENT = 512
SCALE = 192.0 ** (-0.5)
SCALE2 = SCALE * 1.4426950408889634
NEGATIVE = -1e30
EPSILON = 1e-06
MESH = pl.DeviceIdType.MESH
F32 = jnp.float32
BF16 = jnp.bfloat16

GROUPS = 32
QP = 24
EP = 6
NP = QP + EP
WIDE = 640
SLAB = 448
SLABW = 512
ROWS = 48
RET = 384
TILES = WIDE // 128
CUTS = ((0, 2), (2, 2), (4, 1))
HALF = 192
NT = (((1,), (1,)), ((), ()))


def drain(ref, sem):
    pltpu.make_async_copy(ref, ref, sem).wait()


def iota(shape, dim):
    return lax.broadcasted_iota(jnp.int32, shape, dim)


def kernel(
    reads_ref,
    table_ref,
    context_ref,
    reads_vec,
    queries_ref,
    tail_ref,
    resid_ref,
    gain_ref,
    pool_ref,
    wuv_hbm,
    wout_hbm,
    wgate_hbm,
    wup_hbm,
    wdown_hbm,
    out_ref,
    send_ref,
    inv_vec,
    inv_ref,
    pos_ref,
    gain_slab,
    h1_0,
    h1_1,
    h1_2,
    s2,
    q1,
    q2,
    kbuf,
    acc_own,
    sbuf,
    numer_out,
    numer_in,
    lse_out,
    lse_in,
    latent,
    flatm,
    wuv,
    wout,
    wgate,
    wup,
    wdown,
    mix,
    rs1,
    agout,
    ag,
    rs2,
    fin,
    sback,
    rback,
    home_out,
    home_mid,
    home_next,
    home_in,
    wsem,
    ksend,
    krecv,
    hsend,
    hrecv,
    zsend,
    zrecv,
    tsend,
    trecv,
    bsend,
    brecv,
):
    g = lax.axis_index("grp")
    t = lax.axis_index("tp")
    x, z = t // 2, t % 2
    right = lax.rem(x + 1, 4)
    left = lax.rem(x + 3, 4)
    across = lax.rem(x + 2, 4)
    right_t = right * 2 + z
    left_t = left * 2 + z
    peer_t = x * 2 + (1 - z)

    pending = {}
    h1 = (h1_0, h1_1, h1_2)

    def finish(*names):
        for name in names or list(pending):
            pending.pop(name)()

    barrier = pltpu.get_barrier_semaphore()

    @pl.loop(1, GROUPS)
    def _(d):
        pl.semaphore_signal(
            barrier, inc=1, device_id={"grp": lax.rem(g + d, GROUPS)}, device_id_type=MESH
        )

    @pl.loop(1, 8)
    def _(d):
        pl.semaphore_signal(
            barrier, inc=1, device_id={"tp": lax.rem(t + d, 8)}, device_id_type=MESH
        )

    plane = lax.rem(g // 2, 4)
    turn = 2 * z - 1

    @pl.loop(0, 16)
    def _(d):
        far = lax.rem(plane + 2 - (d % 2) * turn, 4)
        to = (d // 4) * 8 + far * 2 + (d // 2) % 2
        pl.semaphore_signal(
            barrier, inc=1, device_id={"grp": to, "tp": peer_t}, device_id_type=MESH
        )

    own_keys = pltpu.make_async_copy(pool_ref, kbuf.at[x], wsem.at[0])
    own_keys.start()
    weights = [
        pltpu.make_async_copy(wuv_hbm, wuv, wsem.at[1]),
        pltpu.make_async_copy(wout_hbm, wout, wsem.at[2]),
        pltpu.make_async_copy(wgate_hbm, wgate, wsem.at[3]),
        pltpu.make_async_copy(wup_hbm, wup, wsem.at[4]),
        pltpu.make_async_copy(wdown_hbm, wdown, wsem.at[5]),
    ]
    for copy in weights:
        copy.start()
    pending["own_keys"] = own_keys.wait
    pending["weights"] = lambda: [copy.wait() for copy in weights]

    half = iota((8, 64), 1) < 32
    for k in range(0, 4, 2):
        for r in range(3):
            marks = []
            for n in (k * 3 + r, (k + 1) * 3 + r):
                length = context_ref[n]
                marks.append(
                    jnp.where(half, length // 64, length % 64).astype(F32).astype(BF16)
                )
            for s in range(4):
                for h in range(2):
                    row = jnp.concatenate([queries_ref[(k + h) * 3 + r, s], marks[h]], axis=1)
                    for w in range(TILES):
                        u = (r * 4 + s) * TILES + w
                        send_ref[k + u % 2, u // 2, 8 * h : 8 * h + 8] = row[
                            :, 128 * w : 128 * (w + 1)
                        ]
    for j in range(8):

        @pl.when(t == j)
        def _():
            at = slice(SLAB * j, SLAB * (j + 1))
            gain_slab[0, :SLAB] = gain_ref[at]
            gain_slab[:, SLAB:] = jnp.zeros((1, SLABW - SLAB), F32)
            for k in range(0, 4, 2):

                def line(n, b):
                    if b < 3:
                        block = tail_ref[n * 3 + b].astype(F32)
                    else:
                        block = resid_ref[n * 3 + b - 3, :, at].astype(F32)
                    return jnp.pad(block, ((0, 0), (0, WIDE - block.shape[1])))

                for e in range(3):
                    block = jnp.concatenate(
                        [line(k, 2 * e), line(k, 2 * e + 1), line(k + 1, 2 * e), line(k + 1, 2 * e + 1)],
                        axis=0,
                    ).astype(BF16)
                    for w in range(TILES):
                        send_ref[4, (e * 2 + k // 2) * TILES + w] = block[
                            :, 128 * w : 128 * (w + 1)
                        ]

    @pl.when(g < NP)
    def _():
        for w in range(TILES):
            h1[w // 2][w % 2, g] = send_ref[w, g]

    pl.semaphore_wait(barrier, GROUPS - 1 + 7 + 16)

    def hop1_sent(c):
        chunk = pl.ds(*CUTS[c])

        @pl.when(g >= NP)
        def _():
            drain(send_ref.at[chunk, pl.ds(0, NP)], hsend.at[c])

        @pl.when(g < NP)
        def _():
            drain(send_ref.at[chunk, pl.ds(0, NP - 1)], hsend.at[c])

    def hop1(c):
        chunk = pl.ds(*CUTS[c])

        @pl.loop(1, GROUPS)
        def _(d):
            to = lax.rem(g + d, GROUPS)

            @pl.when(to < NP)
            def _():
                pltpu.make_async_remote_copy(
                    src_ref=send_ref.at[chunk, to],
                    dst_ref=h1[c].at[:, g],
                    send_sem=hsend.at[c],
                    recv_sem=hrecv.at[c],
                    device_id={"grp": to},
                    device_id_type=MESH,
                ).start()

        pending["hop1_sent", c] = functools.partial(hop1_sent, c)

    hop1(0)
    hop1(1)
    hop1(2)

    place, group = iota((GROUPS, 128), 1), iota((GROUPS, 128), 0)
    inv_vec[...] = jnp.zeros((8, 128), jnp.int32)
    columns = reads_vec[...].T
    for k in range(4):
        asked_here = columns[:, k : k + 1] == place
        inv_vec[k : k + 1, :] = jnp.max(
            jnp.where(asked_here, group, 0), axis=0, keepdims=True
        )
    askers = pltpu.make_async_copy(inv_vec, inv_ref, wsem.at[6])
    askers.start()
    offset = iota((1, 128), 1)
    for j in range(48):
        pos_ref[j // 6, :, (j % 6) * 128 : (j % 6 + 1) * 128] = (
            table_ref[g, j] * 128 + offset
        ).astype(F32)
    askers.wait()

    to_right = pltpu.make_async_remote_copy(
        src_ref=pool_ref,
        dst_ref=kbuf.at[x],
        send_sem=ksend.at[0],
        recv_sem=krecv.at[0],
        device_id={"tp": right_t},
        device_id_type=MESH,
    )
    to_left = pltpu.make_async_remote_copy(
        src_ref=pool_ref,
        dst_ref=kbuf.at[x],
        send_sem=ksend.at[1],
        recv_sem=krecv.at[1],
        device_id={"tp": left_t},
        device_id_type=MESH,
    )
    to_right.start()
    to_left.start()
    pending["right_sent"] = to_right.wait_send
    pending["left_sent"] = to_left.wait_send
    pending["from_left"] = to_right.wait_recv
    pending["from_right"] = to_left.wait_recv

    def hop2_sent(c):
        @pl.when(g < NP)
        def _():
            drain(s2.at[pl.ds(*CUTS[c]), pl.ds(0, GROUPS - 1)], hsend.at[3 + c])

    near = lax.rem(plane + turn + 4, 4)
    far = lax.rem(plane + 2, 4)

    def hop2_arrived(c):
        chunk = pl.ds(*CUTS[c])
        count = jnp.int32(NP)
        if c < 2:
            count = GROUPS - 2 * jnp.where((plane == 3) | (far == 3), 1, 0)
            count = count - 4 * jnp.where(near == 3, 1, 0)
        count = count - jnp.where(g < NP, 1, 0)
        for n in range(GROUPS - 5, GROUPS + 1):

            @pl.when(count == n)
            def _():
                drain(q1.at[chunk, pl.ds(0, n)], hrecv.at[3 + c])

    def route(c):

        @pl.when(g < NP)
        def _():
            chunk = pl.ds(*CUTS[c])
            tiles = range(CUTS[c][0], CUTS[c][0] + CUTS[c][1])
            drain(h1[c].at[:, pl.ds(0, GROUPS - 1)], hrecv.at[c])
            kp = (0, 1, lax.rem(g // TILES, 2))[c]
            upper = iota((16, 128), 0) < 8

            def picked(w, to):
                first = h1[c][w % 2, inv_ref[2 * kp, to]]
                second = h1[c][w % 2, inv_ref[2 * kp + 1, to]]
                return jnp.where(upper, first, second)

            @pl.loop(1, GROUPS)
            def _(d):
                to = lax.rem(g + d, GROUPS)
                for w in tiles:
                    s2[w, to] = picked(w, to)
                away = lax.rem(lax.rem(to // 2, 4) - plane + 4, 4)
                crossing = (away == 2) | (away == 2 - turn)

                def hop2(dst, device):
                    pltpu.make_async_remote_copy(
                        src_ref=s2.at[chunk, to],
                        dst_ref=dst.at[chunk, g],
                        send_sem=hsend.at[3 + c],
                        recv_sem=hrecv.at[3 + c],
                        device_id=device,
                        device_id_type=MESH,
                    ).start()

                if c == 2:
                    hop2(q1, {"grp": to})
                else:
                    pl.when(crossing)(lambda: hop2(q2, {"grp": to, "tp": peer_t}))
                    pl.when(jnp.logical_not(crossing))(lambda: hop2(q1, {"grp": to}))

            for w in tiles:
                q1[w, g] = picked(w, g)

        pending["hop2_sent", c] = functools.partial(hop2_sent, c)
        pending["hop2", c] = functools.partial(hop2_arrived, c)

    route(0)
    route(1)
    route(2)

    def swap_arrived(c):
        drain(q2.at[pl.ds(*CUTS[c])], zrecv.at[c])

    def swap_sent(c):
        drain(q2.at[pl.ds(*CUTS[c])], zsend.at[c])

    def swap(c):
        finish(("hop2", c))
        for src, dst, at in ((q1, q2, plane), (q1, q2, near), (q2, q1, near), (q2, q1, far)):
            for y in range(4):
                part = pl.ds(8 * y + 2 * at, 2)
                pltpu.make_async_remote_copy(
                    src_ref=src.at[pl.ds(*CUTS[c]), part],
                    dst_ref=dst.at[pl.ds(*CUTS[c]), part],
                    send_sem=zsend.at[c],
                    recv_sem=zrecv.at[c],
                    device_id={"tp": peer_t},
                    device_id_type=MESH,
                ).start()
        pending["swap_sent", c] = functools.partial(swap_sent, c)
        pending["swap", c] = functools.partial(swap_arrived, c)

    finish("from_left")
    on_right = pltpu.make_async_remote_copy(
        src_ref=kbuf.at[left, pl.ds(0, 3)],
        dst_ref=kbuf.at[left, pl.ds(0, 3)],
        send_sem=ksend.at[2],
        recv_sem=krecv.at[2],
        device_id={"tp": right_t},
        device_id_type=MESH,
    )
    on_right.start()
    finish("from_right")
    on_left = pltpu.make_async_remote_copy(
        src_ref=kbuf.at[right, pl.ds(3, 3)],
        dst_ref=kbuf.at[right, pl.ds(3, 3)],
        send_sem=ksend.at[3],
        recv_sem=krecv.at[3],
        device_id={"tp": left_t},
        device_id_type=MESH,
    )
    on_left.start()
    pending["on_right_sent"] = on_right.wait_send
    pending["on_left_sent"] = on_left.wait_send
    pending["across_1"] = on_right.wait_recv
    pending["across_2"] = on_left.wait_recv
    swap(0)
    swap(1)
    finish("own_keys")

    nq = QP * 16
    nt = EP * 16

    def lines(ref, slot, step, count):
        pieces = []
        for i in range(count):
            units = [i * TILES + w for w in range(TILES)]
            pieces.append(
                jnp.concatenate([ref[slot + u % step, u // step] for u in units], axis=1)
            )
        return jnp.concatenate(pieces, axis=0)

    def keys_of(b, width):
        return jnp.concatenate([kbuf[b, j, :width] for j in range(6)], axis=1)

    def attend(rows, buf, tail=None):
        count = rows.shape[0]
        lengths = rows[:, 576:577].astype(F32) * 64.0 + rows[:, 608:609].astype(F32)
        top = jnp.full((count, 1), NEGATIVE, F32)
        if tail is not None:
            top = jnp.max(tail, axis=1, keepdims=True)
        for i, b in enumerate((x, left, right, across)):
            if i == 3 and "across_1" in pending:
                finish("across_1", "across_2")
            scores = jnp.dot(rows[:, :576], keys_of(b, 576), preferred_element_type=F32)
            scores = jnp.where(pos_ref[b * 2 + z] < lengths, scores * SCALE2, NEGATIVE)
            buf[i] = scores
            top = jnp.maximum(top, jnp.max(scores, axis=1, keepdims=True))
        den = jnp.zeros((count, 1), F32)
        acc = jnp.zeros((count, LATENT), F32)
        if tail is not None:
            weight = jnp.exp2(tail - top).astype(BF16)
            den = jnp.sum(weight.astype(F32), axis=1, keepdims=True)
            acc = jnp.dot(weight, extra[:, :LATENT], preferred_element_type=F32)
        for i, b in enumerate((x, left, right, across)):
            weight = jnp.exp2(buf[i] - top).astype(BF16)
            den = den + jnp.sum(weight.astype(F32), axis=1, keepdims=True)
            acc = acc + lax.dot_general(
                weight, keys_of(b, LATENT), NT, preferred_element_type=F32
            )
        return top, den, acc

    diagonal = iota((HALF, HALF), 0) == iota((HALF, HALF), 1)
    n, m = iota((HALF, nt), 0), iota((HALF, nt), 1)
    line = (m // 32) * 8 + m % 8
    in_place = (line // 4 == n // 64) & (line % 4 <= (n // 16) % 4)
    own_top, own_den = [], []
    for c in range(2):
        finish(("swap", c))
        top, den, acc = attend(lines(q2, 2 * c, 2, 12), sbuf.at[0])
        numer_out[c] = (acc / den).astype(BF16)
        lse = top + jnp.log2(den)
        lse_out[c] = jnp.broadcast_to(
            jnp.sum(jnp.where(diagonal, lse, 0.0), axis=0, keepdims=True), (8, HALF)
        )
        for s, (src, dst) in enumerate([(numer_out, numer_in), (lse_out, lse_in)]):
            copy = pltpu.make_async_remote_copy(
                src_ref=src.at[c],
                dst_ref=dst.at[c],
                send_sem=zsend.at[2 + 2 * c + s],
                recv_sem=zrecv.at[2 + 2 * c + s],
                device_id={"tp": peer_t},
                device_id_type=MESH,
            )
            copy.start()
            pending["back_sent", c, s] = copy.wait_send
            pending["back", c, s] = copy.wait_recv
    finish(("hop2", 2))
    extra = lines(q1, 4, 1, EP)
    for c in range(2):
        rows = lines(q1, 2 * c, 2, 12)
        tail = lax.dot_general(
            rows[:, :576], extra[:, :576], NT, preferred_element_type=F32
        )
        seen = in_place & ((m // 8) % 4 == 2 * c + (n // 8) % 2)
        tail = jnp.where(seen, tail * SCALE2, NEGATIVE)
        top, den, acc = attend(rows, sbuf.at[1], tail)
        own_top.append(top)
        own_den.append(den)
        acc_own[HALF * c : HALF * (c + 1)] = acc
    finish("weights")
    head_of = iota((HALF, 128), 0) % 8
    for c in range(2):
        finish(("back", c, 0), ("back", c, 1))
        at = slice(HALF * c, HALF * (c + 1))
        lse = jnp.sum(jnp.where(diagonal, lse_in[c, 0:1, :], 0.0), axis=1, keepdims=True)
        both = jnp.maximum(own_top[c], lse)
        mine = jnp.exp2(own_top[c] - both)
        theirs = jnp.exp2(lse - both)
        scaled = 1.0 / (own_den[c] * mine + theirs)
        latent[at] = (
            acc_own[at] * (mine * scaled) + numer_in[c].astype(F32) * (theirs * scaled)
        ).astype(BF16)
        for h in range(8):
            value = jnp.dot(latent[at], wuv[h], preferred_element_type=F32)
            flatm[at, h * 128 : (h + 1) * 128] = jnp.where(head_of == h, value, 0.0).astype(
                BF16
            )

    o, n = iota((ROWS, nq), 0), iota((ROWS, nq), 1)
    chosen = (n % HALF) // 16 == o % 12
    chosen = chosen & ((n // HALF) * 2 + (n // 8) % 2 == o // 12)
    flat = jnp.dot(
        jnp.where(chosen, 1.0, 0.0).astype(BF16), flatm[...], preferred_element_type=F32
    ).astype(BF16)

    def spread(part, dst, s):
        for d in range(1, 8):
            to = lax.rem(t + d, 8)
            pltpu.make_async_remote_copy(
                src_ref=part(to),
                dst_ref=dst.at[t],
                send_sem=tsend.at[s],
                recv_sem=trecv.at[s],
                device_id={"tp": to},
                device_id_type=MESH,
            ).start()
        pending["spread_sent", s] = lambda: drain(rs1.at[pl.ds(0, 7)], tsend.at[s])
        pending["spread", s] = lambda: drain(dst.at[pl.ds(0, 7)], trecv.at[s])

    def slabs(left_side, weight, part, dst, s):
        for dx in (2, 1, 3, 0):
            pair = lax.rem(x + dx, 4)
            columns = pl.ds(pl.multiple_of(pair * 2 * SLAB, 128), 2 * SLAB)
            wide = jnp.dot(
                left_side, weight[:, columns], preferred_element_type=F32
            ).astype(BF16)
            part[2 * pair, :, :SLAB] = wide[:, :SLAB]
            part[2 * pair + 1, :, :SLAB] = wide[:, SLAB:]
            for to in (pair * 2 + z, peer_t) if dx == 0 else (pair * 2, pair * 2 + 1):
                if dx == 0 and to is not peer_t:
                    dst[t] = part[t]
                    continue
                pltpu.make_async_remote_copy(
                    src_ref=part.at[to],
                    dst_ref=dst.at[t],
                    send_sem=tsend.at[s],
                    recv_sem=trecv.at[s],
                    device_id={"tp": to},
                    device_id_type=MESH,
                ).start()
        pending["spread_sent", s] = lambda: drain(rs1.at[pl.ds(0, 7)], tsend.at[s])
        pending["spread", s] = lambda: drain(dst.at[pl.ds(0, 7)], trecv.at[s])

    mix[0, :, :, SLAB:] = jnp.zeros((8, ROWS, SLABW - SLAB), BF16)
    mix[1, :, :, SLAB:] = jnp.zeros((8, ROWS, SLABW - SLAB), BF16)
    slabs(flat, wout, mix.at[0], rs1, 0)
    o, m = iota((ROWS, nt), 0), iota((ROWS, nt), 1)
    line = (m // 32) * 8 + m % 8
    chosen = (line - 12 == o % 12) & ((m // 8) % 4 == o // 12)
    hidden = jnp.dot(
        jnp.where(chosen, 1.0, 0.0).astype(BF16),
        extra[:, :SLABW],
        preferred_element_type=F32,
    )
    finish(("spread", 0))
    for j in range(8):
        hidden = hidden + rs1[j].astype(F32)
    lane = iota((ROWS, SLABW), 1)
    hidden = jnp.where(lane < SLAB, hidden, 0.0)
    square = jnp.sum(hidden * hidden, axis=1, keepdims=True)
    high = square.astype(BF16).astype(F32)
    low = square - high
    packed = jnp.where(
        lane < SLAB, hidden * gain_slab[...], jnp.where(lane < SLAB + 32, high, low)
    ).astype(BF16)
    agout[...] = packed
    spread(lambda to: agout, ag, 1)
    ag[t] = packed

    o, m = iota((64, ROWS), 0), iota((64, ROWS), 1)

    def placed(chosen, columns):
        return jnp.dot(
            jnp.where((o // 16 == m // 12) & chosen, 1.0, 0.0).astype(BF16),
            columns,
            preferred_element_type=F32,
        )

    rounded = hidden.astype(BF16)
    wide = placed(o % 16 == m % 12, rounded[:, :RET])
    rest = [
        placed(o % 16 - 12 + 4 * r == m % 12, rounded[:, RET:SLAB]) for r in range(3)
    ]
    rest = jnp.concatenate(rest + [jnp.zeros((64, RET - 192), F32)], axis=1)
    lower = iota((64, RET), 0) % 16 >= 12
    block = jnp.where(lower, rest, wide).astype(BF16)
    for i in range(12):
        home_out[i] = block[16 * (i // 3) : 16 * (i // 3) + 16, 128 * (i % 3) : 128 * (i % 3 + 1)]
        copy = pltpu.make_async_remote_copy(
            src_ref=home_out.at[i],
            dst_ref=home_mid.at[g],
            send_sem=bsend.at[i],
            recv_sem=brecv.at[0],
            device_id={"grp": i},
            device_id_type=MESH,
        )

        @pl.when(g != i)
        def _():
            copy.start()

        @pl.when(g == i)
        def _():
            home_mid[g] = home_out[i]

    def home_sent():
        for i in range(12):

            @pl.when(g != i)
            def _():
                drain(home_out.at[i], bsend.at[i])

        @pl.when(g < 12)
        def _():
            drain(home_next.at[pl.ds(0, GROUPS - 1)], bsend.at[12])

    def home_arrived():
        @pl.when(g < 12)
        def _():
            drain(home_in.at[pl.ds(0, 11)], brecv.at[1])

        @pl.when(g >= 12)
        def _():
            drain(home_in.at[pl.ds(0, 12)], brecv.at[1])

    finish(("spread", 1))
    total = jnp.zeros((ROWS, 1), F32)
    gate = jnp.zeros((ROWS, 128), F32)
    upward = jnp.zeros((ROWS, 128), F32)
    for j in range(8):
        block = ag[j]
        total = total + (
            block[:, SLAB : SLAB + 1].astype(F32) + block[:, SLAB + 32 : SLAB + 33].astype(F32)
        )
        at = slice(SLAB * j, SLAB * (j + 1))
        gate = gate + jnp.dot(block[:, :SLAB], wgate[at], preferred_element_type=F32)
        upward = upward + jnp.dot(block[:, :SLAB], wup[at], preferred_element_type=F32)
    factor = lax.rsqrt(total * (1.0 / 3584.0) + EPSILON)
    gate = gate * factor
    upward = upward * factor
    active = (gate / (1.0 + jnp.exp(-gate)) * upward).astype(BF16)

    fin[...] = placed(o % 16 == m % 12, active).astype(BF16).reshape(4, 16, 128)

    def answer(to):
        slot = jnp.where(reads_ref[3, to] == g, 3, 0)
        slot = jnp.where(reads_ref[2, to] == g, 2, slot)
        slot = jnp.where(reads_ref[1, to] == g, 1, slot)
        return fin[slot]

    @pl.loop(1, GROUPS)
    def _(d):
        to = lax.rem(g + d, GROUPS)
        sback[to] = answer(to)
        pltpu.make_async_remote_copy(
            src_ref=sback.at[to],
            dst_ref=rback.at[g],
            send_sem=hsend.at[6],
            recv_sem=hrecv.at[6],
            device_id={"grp": to},
            device_id_type=MESH,
        ).start()

    rback[g] = answer(g)
    pending["return_sent"] = lambda: drain(sback.at[pl.ds(0, GROUPS - 1)], hsend.at[6])
    pending["return"] = lambda: drain(rback.at[pl.ds(0, GROUPS - 1)], hrecv.at[6])

    @pl.when(g < 12)
    def _():
        drain(home_mid.at[pl.ds(0, GROUPS - 1)], brecv.at[0])
        k = g // 3

        @pl.loop(1, GROUPS)
        def _(d):
            to = lax.rem(g + d, GROUPS)
            home_next[to] = home_mid[reads_ref[k, to]]
            pltpu.make_async_remote_copy(
                src_ref=home_next.at[to],
                dst_ref=home_in.at[g],
                send_sem=bsend.at[12],
                recv_sem=brecv.at[1],
                device_id={"grp": to},
                device_id_type=MESH,
            ).start()

        home_in[g] = home_mid[reads_ref[k, g]]

    pending["home_sent"] = home_sent
    pending["home"] = home_arrived
    finish("return")
    o, m = iota((ROWS, 64), 0), iota((ROWS, 64), 1)
    blocks = jnp.concatenate([rback[reads_ref[k, g]] for k in range(4)], axis=0)
    active = jnp.dot(
        jnp.where((o // 12 == m // 16) & (o % 12 == m % 16), 1.0, 0.0).astype(BF16),
        blocks,
        preferred_element_type=F32,
    ).astype(BF16)
    slabs(active, wdown, mix.at[1], rs2, 2)
    finish("home")
    finish(("spread", 2))
    summed = rs2[0].astype(F32)
    for j in range(1, 8):
        summed = summed + rs2[j].astype(F32)
    for k in range(4):
        block = jnp.concatenate([home_in[3 * k + j] for j in range(3)], axis=1).astype(F32)
        for r in range(3):
            at = slice(12 * k + 4 * r, 12 * k + 4 * r + 4)
            out_ref[3 * k + r, :, :RET] = (
                summed[at, :RET] + block[4 * r : 4 * r + 4]
            ).astype(BF16)
            out_ref[3 * k + r, :, RET:] = (
                summed[at, RET:SLAB] + block[12:, 64 * r : 64 * r + 64]
            ).astype(BF16)

    finish()


def on_device(
    pool_pages,
    page_table,
    read_list,
    context,
    queries,
    tail_keys,
    residual,
    w_uv,
    w_out,
    norm_gain,
    w_gate,
    w_up,
    w_down,
):
    smem = pl.BlockSpec(memory_space=pltpu.SMEM)
    vmem = pl.BlockSpec(memory_space=pltpu.VMEM)
    anym = pl.BlockSpec(memory_space=pl.ANY)
    dma = pltpu.SemaphoreType.DMA
    nq = QP * 16
    return pl.pallas_call(
        kernel,
        out_shape=jax.ShapeDtypeStruct((12, 4, SLAB), BF16),
        in_specs=[smem] * 3 + [vmem] * 5 + [anym] * 6,
        out_specs=vmem,
        scratch_shapes=[
            pltpu.VMEM((TILES, NP, 16, 128), BF16),
            pltpu.VMEM((8, 128), jnp.int32),
            pltpu.SMEM((8, 128), jnp.int32),
            pltpu.VMEM((8, 1, 768), F32),
            pltpu.VMEM((1, SLABW), F32),
            pltpu.VMEM((2, GROUPS, 16, 128), BF16),
            pltpu.VMEM((2, GROUPS, 16, 128), BF16),
            pltpu.VMEM((1, GROUPS, 16, 128), BF16),
            pltpu.VMEM((TILES, GROUPS, 16, 128), BF16),
            pltpu.VMEM((TILES, GROUPS, 16, 128), BF16),
            pltpu.VMEM((4, GROUPS, 16, 128), BF16),
            pltpu.VMEM((4, 6, 576, 128), BF16),
            pltpu.VMEM((nq, LATENT), F32),
            pltpu.VMEM((2, 4, HALF, 768), F32),
            pltpu.VMEM((2, HALF, LATENT), BF16),
            pltpu.VMEM((2, HALF, LATENT), BF16),
            pltpu.VMEM((2, 8, HALF), F32),
            pltpu.VMEM((2, 8, HALF), F32),
            pltpu.VMEM((nq, LATENT), BF16),
            pltpu.VMEM((nq, 1024), BF16),
            pltpu.VMEM((8, 512, 128), BF16),
            pltpu.VMEM((1024, 3584), BF16),
            pltpu.VMEM((3584, 128), BF16),
            pltpu.VMEM((3584, 128), BF16),
            pltpu.VMEM((128, 3584), BF16),
            pltpu.VMEM((2, 8, ROWS, SLABW), BF16),
            pltpu.VMEM((8, ROWS, SLABW), BF16),
            pltpu.VMEM((ROWS, SLABW), BF16),
            pltpu.VMEM((8, ROWS, SLABW), BF16),
            pltpu.VMEM((8, ROWS, SLABW), BF16),
            pltpu.VMEM((4, 16, 128), BF16),
            pltpu.VMEM((GROUPS, 16, 128), BF16),
            pltpu.VMEM((GROUPS, 16, 128), BF16),
            pltpu.VMEM((12, 16, 128), BF16),
            pltpu.VMEM((GROUPS, 16, 128), BF16),
            pltpu.VMEM((GROUPS, 16, 128), BF16),
            pltpu.VMEM((12, 16, 128), BF16),
            dma((7,)),
            dma((4,)),
            dma((4,)),
            dma((7,)),
            dma((7,)),
            dma((6,)),
            dma((6,)),
            dma((3,)),
            dma((3,)),
            dma((13,)),
            dma((2,)),
        ],
        compiler_params=pltpu.CompilerParams(
            collective_id=0, has_side_effects=True, vmem_limit_bytes=56 * 1024 * 1024
        ),
    )(
        read_list.T,
        page_table,
        context,
        read_list.T,
        queries,
        tail_keys,
        residual,
        norm_gain,
        pool_pages.reshape(6, 128, 576).transpose(0, 2, 1),
        w_uv,
        w_out,
        w_gate,
        w_up,
        w_down,
    )


def solution(mesh):
    placed = (
        P("grp", "tp", None, None),
        P(),
        P(),
        P("grp"),
        P("grp", None, "tp", None),
        P("grp", None, None),
        P("grp", None, None),
        P("tp", None, None),
        P("tp", None),
        P(),
        P(None, "tp"),
        P(None, "tp"),
        P("tp", None),
    )
    return jax.shard_map(
        on_device, mesh=mesh, in_specs=placed, out_specs=P("grp", None, "tp"), check_vma=False
    )
```

```python
import functools

import jax
import jax.numpy as jnp
import numpy as np
from jax import lax
from jax.experimental import pallas as pl
from jax.experimental.pallas import tpu as pltpu
from jax.sharding import PartitionSpec as P

LATENT = 512
SCALE = 192.0 ** (-0.5)
SCALE2 = SCALE * 1.4426950408889634
NEGATIVE = -1e30
EPSILON = 1e-06
MESH = pl.DeviceIdType.MESH
F32 = jnp.float32
BF16 = jnp.bfloat16

GROUPS = 32
QP = 24
EP = 6
NP = QP + EP
WIDE = 640
SLAB = 448
SLABW = 512
ROWS = 48
RET = 384
TILES = WIDE // 128
CUTS = ((0, 2), (2, 2), (4, 1))
HALF = 192
NT = (((1,), (1,)), ((), ()))


def drain(ref, sem):
    pltpu.make_async_copy(ref, ref, sem).wait()


def iota(shape, dim):
    return lax.broadcasted_iota(jnp.int32, shape, dim)


def kernel(
    reads_ref,
    table_ref,
    context_ref,
    reads_vec,
    queries_ref,
    tail_ref,
    resid_ref,
    gain_ref,
    pool_ref,
    wuv_hbm,
    wout_hbm,
    wgate_hbm,
    wup_hbm,
    wdown_hbm,
    out_ref,
    send_ref,
    inv_vec,
    inv_ref,
    pos_ref,
    gain_slab,
    h1_0,
    h1_1,
    h1_2,
    s2,
    q1,
    q2,
    kbuf,
    acc_own,
    sbuf,
    numer_out,
    numer_in,
    lse_out,
    lse_in,
    latent,
    flatm,
    wuv,
    wout,
    wgate,
    wup,
    wdown,
    mix,
    rs1,
    agout,
    ag,
    rs2,
    fin,
    sback,
    rback,
    home_out,
    home_mid,
    home_next,
    home_in,
    wsem,
    ksend,
    krecv,
    hsend,
    hrecv,
    zsend,
    zrecv,
    tsend,
    trecv,
    bsend,
    brecv,
):
    g = lax.axis_index("grp")
    t = lax.axis_index("tp")
    x, z = t // 2, t % 2
    right = lax.rem(x + 1, 4)
    left = lax.rem(x + 3, 4)
    across = lax.rem(x + 2, 4)
    right_t = right * 2 + z
    left_t = left * 2 + z
    peer_t = x * 2 + (1 - z)

    pending = {}
    h1 = (h1_0, h1_1, h1_2)

    def finish(*names):
        for name in names or list(pending):
            pending.pop(name)()

    barrier = pltpu.get_barrier_semaphore()

    @pl.loop(1, GROUPS)
    def _(d):
        pl.semaphore_signal(
            barrier, inc=1, device_id={"grp": lax.rem(g + d, GROUPS)}, device_id_type=MESH
        )

    @pl.loop(1, 8)
    def _(d):
        pl.semaphore_signal(
            barrier, inc=1, device_id={"tp": lax.rem(t + d, 8)}, device_id_type=MESH
        )

    plane = lax.rem(g // 2, 4)
    turn = 2 * z - 1

    @pl.loop(0, 16)
    def _(d):
        far = lax.rem(plane + 2 - (d % 2) * turn, 4)
        to = (d // 4) * 8 + far * 2 + (d // 2) % 2
        pl.semaphore_signal(
            barrier, inc=1, device_id={"grp": to, "tp": peer_t}, device_id_type=MESH
        )

    own_keys = pltpu.make_async_copy(pool_ref, kbuf.at[x], wsem.at[0])
    own_keys.start()
    weights = [
        pltpu.make_async_copy(wuv_hbm, wuv, wsem.at[1]),
        pltpu.make_async_copy(wout_hbm, wout, wsem.at[2]),
        pltpu.make_async_copy(wgate_hbm, wgate, wsem.at[3]),
        pltpu.make_async_copy(wup_hbm, wup, wsem.at[4]),
        pltpu.make_async_copy(wdown_hbm, wdown, wsem.at[5]),
    ]
    for copy in weights:
        copy.start()
    pending["own_keys"] = own_keys.wait
    pending["weights"] = lambda: [copy.wait() for copy in weights]

    half = iota((8, 64), 1) < 32
    for k in range(0, 4, 2):
        for r in range(3):
            marks = []
            for n in (k * 3 + r, (k + 1) * 3 + r):
                length = context_ref[n]
                marks.append(
                    jnp.where(half, length // 64, length % 64).astype(F32).astype(BF16)
                )
            for s in range(4):
                for h in range(2):
                    row = jnp.concatenate([queries_ref[(k + h) * 3 + r, s], marks[h]], axis=1)
                    for w in range(TILES):
                        u = (r * 4 + s) * TILES + w
                        send_ref[k + u % 2, u // 2, 8 * h : 8 * h + 8] = row[
                            :, 128 * w : 128 * (w + 1)
                        ]
    for j in range(8):

        @pl.when(t == j)
        def _():
            at = slice(SLAB * j, SLAB * (j + 1))
            gain_slab[0, :SLAB] = gain_ref[at]
            gain_slab[:, SLAB:] = jnp.zeros((1, SLABW - SLAB), F32)
            for k in range(0, 4, 2):

                def line(n, b):
                    if b < 3:
                        block = tail_ref[n * 3 + b].astype(F32)
                    else:
                        block = resid_ref[n * 3 + b - 3, :, at].astype(F32)
                    return jnp.pad(block, ((0, 0), (0, WIDE - block.shape[1])))

                for e in range(3):
                    block = jnp.concatenate(
                        [line(k, 2 * e), line(k, 2 * e + 1), line(k + 1, 2 * e), line(k + 1, 2 * e + 1)],
                        axis=0,
                    ).astype(BF16)
                    for w in range(TILES):
                        send_ref[4, (e * 2 + k // 2) * TILES + w] = block[
                            :, 128 * w : 128 * (w + 1)
                        ]

    @pl.when(g < NP)
    def _():
        for w in range(TILES):
            h1[w // 2][w % 2, g] = send_ref[w, g]

    pl.semaphore_wait(barrier, GROUPS - 1 + 7 + 16)

    to_right = pltpu.make_async_remote_copy(
        src_ref=pool_ref,
        dst_ref=kbuf.at[x],
        send_sem=ksend.at[0],
        recv_sem=krecv.at[0],
        device_id={"tp": right_t},
        device_id_type=MESH,
    )
    to_left = pltpu.make_async_remote_copy(
        src_ref=pool_ref,
        dst_ref=kbuf.at[x],
        send_sem=ksend.at[1],
        recv_sem=krecv.at[1],
        device_id={"tp": left_t},
        device_id_type=MESH,
    )
    to_right.start()
    to_left.start()
    pending["right_sent"] = to_right.wait_send
    pending["left_sent"] = to_left.wait_send
    pending["from_left"] = to_right.wait_recv
    pending["from_right"] = to_left.wait_recv

    def hop1_sent(c):
        chunk = pl.ds(*CUTS[c])

        @pl.when(g >= NP)
        def _():
            drain(send_ref.at[chunk, pl.ds(0, NP)], hsend.at[c])

        @pl.when(g < NP)
        def _():
            drain(send_ref.at[chunk, pl.ds(0, NP - 1)], hsend.at[c])

    def hop1(c):
        chunk = pl.ds(*CUTS[c])

        @pl.loop(1, GROUPS)
        def _(d):
            to = lax.rem(g + d, GROUPS)

            @pl.when(to < NP)
            def _():
                pltpu.make_async_remote_copy(
                    src_ref=send_ref.at[chunk, to],
                    dst_ref=h1[c].at[:, g],
                    send_sem=hsend.at[c],
                    recv_sem=hrecv.at[c],
                    device_id={"grp": to},
                    device_id_type=MESH,
                ).start()

        pending["hop1_sent", c] = functools.partial(hop1_sent, c)

    hop1(0)
    hop1(1)
    hop1(2)

    place, group = iota((GROUPS, 128), 1), iota((GROUPS, 128), 0)
    inv_vec[...] = jnp.zeros((8, 128), jnp.int32)
    columns = reads_vec[...].T
    for k in range(4):
        asked_here = columns[:, k : k + 1] == place
        inv_vec[k : k + 1, :] = jnp.max(
            jnp.where(asked_here, group, 0), axis=0, keepdims=True
        )
    askers = pltpu.make_async_copy(inv_vec, inv_ref, wsem.at[6])
    askers.start()
    offset = iota((1, 128), 1)
    for j in range(48):
        pos_ref[j // 6, :, (j % 6) * 128 : (j % 6 + 1) * 128] = (
            table_ref[g, j] * 128 + offset
        ).astype(F32)
    askers.wait()

    def hop2_sent(c):
        @pl.when(g < NP)
        def _():
            drain(s2.at[pl.ds(*CUTS[c]), pl.ds(0, GROUPS - 1)], hsend.at[3 + c])

    near = lax.rem(plane + turn + 4, 4)
    far = lax.rem(plane + 2, 4)

    def hop2_arrived(c):
        chunk = pl.ds(*CUTS[c])
        count = jnp.int32(NP)
        if c < 2:
            count = GROUPS - 2 * jnp.where((plane == 3) | (far == 3), 1, 0)
            count = count - 4 * jnp.where(near == 3, 1, 0)
        count = count - jnp.where(g < NP, 1, 0)
        for n in range(GROUPS - 5, GROUPS + 1):

            @pl.when(count == n)
            def _():
                drain(q1.at[chunk, pl.ds(0, n)], hrecv.at[3 + c])

    def route(c):

        @pl.when(g < NP)
        def _():
            chunk = pl.ds(*CUTS[c])
            tiles = range(CUTS[c][0], CUTS[c][0] + CUTS[c][1])
            drain(h1[c].at[:, pl.ds(0, GROUPS - 1)], hrecv.at[c])
            kp = (0, 1, lax.rem(g // TILES, 2))[c]
            upper = iota((16, 128), 0) < 8

            def picked(w, to):
                first = h1[c][w % 2, inv_ref[2 * kp, to]]
                second = h1[c][w % 2, inv_ref[2 * kp + 1, to]]
                return jnp.where(upper, first, second)

            @pl.loop(1, GROUPS)
            def _(d):
                to = lax.rem(g + d, GROUPS)
                for w in tiles:
                    s2[w, to] = picked(w, to)
                away = lax.rem(lax.rem(to // 2, 4) - plane + 4, 4)
                crossing = (away == 2) | (away == 2 - turn)

                def hop2(dst, device):
                    pltpu.make_async_remote_copy(
                        src_ref=s2.at[chunk, to],
                        dst_ref=dst.at[chunk, g],
                        send_sem=hsend.at[3 + c],
                        recv_sem=hrecv.at[3 + c],
                        device_id=device,
                        device_id_type=MESH,
                    ).start()

                if c == 2:
                    hop2(q1, {"grp": to})
                else:
                    pl.when(crossing)(lambda: hop2(q2, {"grp": to, "tp": peer_t}))
                    pl.when(jnp.logical_not(crossing))(lambda: hop2(q1, {"grp": to}))

            for w in tiles:
                q1[w, g] = picked(w, g)

        pending["hop2_sent", c] = functools.partial(hop2_sent, c)
        pending["hop2", c] = functools.partial(hop2_arrived, c)

    route(0)
    route(1)
    route(2)

    def swap_arrived(c):
        drain(q2.at[pl.ds(*CUTS[c])], zrecv.at[c])

    def swap_sent(c):
        drain(q2.at[pl.ds(*CUTS[c])], zsend.at[c])

    def swap(c):
        finish(("hop2", c))
        for src, dst, at in ((q1, q2, plane), (q1, q2, near), (q2, q1, near), (q2, q1, far)):
            for y in range(4):
                part = pl.ds(8 * y + 2 * at, 2)
                pltpu.make_async_remote_copy(
                    src_ref=src.at[pl.ds(*CUTS[c]), part],
                    dst_ref=dst.at[pl.ds(*CUTS[c]), part],
                    send_sem=zsend.at[c],
                    recv_sem=zrecv.at[c],
                    device_id={"tp": peer_t},
                    device_id_type=MESH,
                ).start()
        pending["swap_sent", c] = functools.partial(swap_sent, c)
        pending["swap", c] = functools.partial(swap_arrived, c)

    finish("from_left")
    on_right = pltpu.make_async_remote_copy(
        src_ref=kbuf.at[left, pl.ds(0, 3)],
        dst_ref=kbuf.at[left, pl.ds(0, 3)],
        send_sem=ksend.at[2],
        recv_sem=krecv.at[2],
        device_id={"tp": right_t},
        device_id_type=MESH,
    )
    on_right.start()
    finish("from_right")
    on_left = pltpu.make_async_remote_copy(
        src_ref=kbuf.at[right, pl.ds(3, 3)],
        dst_ref=kbuf.at[right, pl.ds(3, 3)],
        send_sem=ksend.at[3],
        recv_sem=krecv.at[3],
        device_id={"tp": left_t},
        device_id_type=MESH,
    )
    on_left.start()
    pending["on_right_sent"] = on_right.wait_send
    pending["on_left_sent"] = on_left.wait_send
    pending["across_1"] = on_right.wait_recv
    pending["across_2"] = on_left.wait_recv
    swap(0)
    swap(1)
    finish("own_keys")

    nq = QP * 16
    nt = EP * 16

    def lines(ref, slot, step, count):
        pieces = []
        for i in range(count):
            units = [i * TILES + w for w in range(TILES)]
            pieces.append(
                jnp.concatenate([ref[slot + u % step, u // step] for u in units], axis=1)
            )
        return jnp.concatenate(pieces, axis=0)

    def keys_of(b, width):
        return jnp.concatenate([kbuf[b, j, :width] for j in range(6)], axis=1)

    def attend(rows, buf, tail=None):
        count = rows.shape[0]
        lengths = rows[:, 576:577].astype(F32) * 64.0 + rows[:, 608:609].astype(F32)
        top = jnp.full((count, 1), NEGATIVE, F32)
        if tail is not None:
            top = jnp.max(tail, axis=1, keepdims=True)
        for i, b in enumerate((x, left, right, across)):
            if i == 3 and "across_1" in pending:
                finish("across_1", "across_2")
            scores = jnp.dot(rows[:, :576], keys_of(b, 576), preferred_element_type=F32)
            scores = jnp.where(pos_ref[b * 2 + z] < lengths, scores * SCALE2, NEGATIVE)
            buf[i] = scores
            top = jnp.maximum(top, jnp.max(scores, axis=1, keepdims=True))
        den = jnp.zeros((count, 1), F32)
        acc = jnp.zeros((count, LATENT), F32)
        if tail is not None:
            weight = jnp.exp2(tail - top).astype(BF16)
            den = jnp.sum(weight.astype(F32), axis=1, keepdims=True)
            acc = jnp.dot(weight, extra[:, :LATENT], preferred_element_type=F32)
        for i, b in enumerate((x, left, right, across)):
            weight = jnp.exp2(buf[i] - top).astype(BF16)
            den = den + jnp.sum(weight.astype(F32), axis=1, keepdims=True)
            acc = acc + lax.dot_general(
                weight, keys_of(b, LATENT), NT, preferred_element_type=F32
            )
        return top, den, acc

    diagonal = iota((HALF, HALF), 0) == iota((HALF, HALF), 1)
    n, m = iota((HALF, nt), 0), iota((HALF, nt), 1)
    line = (m // 32) * 8 + m % 8
    in_place = (line // 4 == n // 64) & (line % 4 <= (n // 16) % 4)
    own_top, own_den = [], []
    for c in range(2):
        finish(("swap", c))
        top, den, acc = attend(lines(q2, 2 * c, 2, 12), sbuf.at[0])
        numer_out[c] = (acc / den).astype(BF16)
        lse = top + jnp.log2(den)
        lse_out[c] = jnp.broadcast_to(
            jnp.sum(jnp.where(diagonal, lse, 0.0), axis=0, keepdims=True), (8, HALF)
        )
        for s, (src, dst) in enumerate([(numer_out, numer_in), (lse_out, lse_in)]):
            copy = pltpu.make_async_remote_copy(
                src_ref=src.at[c],
                dst_ref=dst.at[c],
                send_sem=zsend.at[2 + 2 * c + s],
                recv_sem=zrecv.at[2 + 2 * c + s],
                device_id={"tp": peer_t},
                device_id_type=MESH,
            )
            copy.start()
            pending["back_sent", c, s] = copy.wait_send
            pending["back", c, s] = copy.wait_recv
    finish(("hop2", 2))
    extra = lines(q1, 4, 1, EP)
    for c in range(2):
        rows = lines(q1, 2 * c, 2, 12)
        tail = lax.dot_general(
            rows[:, :576], extra[:, :576], NT, preferred_element_type=F32
        )
        seen = in_place & ((m // 8) % 4 == 2 * c + (n // 8) % 2)
        tail = jnp.where(seen, tail * SCALE2, NEGATIVE)
        top, den, acc = attend(rows, sbuf.at[1], tail)
        own_top.append(top)
        own_den.append(den)
        acc_own[HALF * c : HALF * (c + 1)] = acc
    finish("weights")
    head_of = iota((HALF, 128), 0) % 8
    for c in range(2):
        finish(("back", c, 0), ("back", c, 1))
        at = slice(HALF * c, HALF * (c + 1))
        lse = jnp.sum(jnp.where(diagonal, lse_in[c, 0:1, :], 0.0), axis=1, keepdims=True)
        both = jnp.maximum(own_top[c], lse)
        mine = jnp.exp2(own_top[c] - both)
        theirs = jnp.exp2(lse - both)
        scaled = 1.0 / (own_den[c] * mine + theirs)
        latent[at] = (
            acc_own[at] * (mine * scaled) + numer_in[c].astype(F32) * (theirs * scaled)
        ).astype(BF16)
        for h in range(8):
            value = jnp.dot(latent[at], wuv[h], preferred_element_type=F32)
            flatm[at, h * 128 : (h + 1) * 128] = jnp.where(head_of == h, value, 0.0).astype(
                BF16
            )

    o, n = iota((ROWS, nq), 0), iota((ROWS, nq), 1)
    chosen = (n % HALF) // 16 == o % 12
    chosen = chosen & ((n // HALF) * 2 + (n // 8) % 2 == o // 12)
    flat = jnp.dot(
        jnp.where(chosen, 1.0, 0.0).astype(BF16), flatm[...], preferred_element_type=F32
    ).astype(BF16)

    def spread(part, dst, s):
        for dx, dz in ((2, 1), (1, 1), (3, 1), (2, 0), (0, 1), (1, 0), (3, 0)):
            to = lax.rem(x + dx, 4) * 2 + lax.rem(z + dz, 2)
            pltpu.make_async_remote_copy(
                src_ref=part(to),
                dst_ref=dst.at[t],
                send_sem=tsend.at[s],
                recv_sem=trecv.at[s],
                device_id={"tp": to},
                device_id_type=MESH,
            ).start()
        pending["spread_sent", s] = lambda: drain(rs1.at[pl.ds(0, 7)], tsend.at[s])
        pending["spread", s] = lambda: drain(dst.at[pl.ds(0, 7)], trecv.at[s])

    def slabs(left_side, weight, part, dst, s):
        for dx in (2, 1, 3, 0):
            pair = lax.rem(x + dx, 4)
            columns = pl.ds(pl.multiple_of(pair * 2 * SLAB, 128), 2 * SLAB)
            wide = jnp.dot(
                left_side, weight[:, columns], preferred_element_type=F32
            ).astype(BF16)
            part[2 * pair, :, :SLAB] = wide[:, :SLAB]
            part[2 * pair + 1, :, :SLAB] = wide[:, SLAB:]
            for to in (pair * 2 + z, peer_t) if dx == 0 else (pair * 2, pair * 2 + 1):
                if dx == 0 and to is not peer_t:
                    dst[t] = part[t]
                    continue
                pltpu.make_async_remote_copy(
                    src_ref=part.at[to],
                    dst_ref=dst.at[t],
                    send_sem=tsend.at[s],
                    recv_sem=trecv.at[s],
                    device_id={"tp": to},
                    device_id_type=MESH,
                ).start()
        pending["spread_sent", s] = lambda: drain(rs1.at[pl.ds(0, 7)], tsend.at[s])
        pending["spread", s] = lambda: drain(dst.at[pl.ds(0, 7)], trecv.at[s])

    mix[0, :, :, SLAB:] = jnp.zeros((8, ROWS, SLABW - SLAB), BF16)
    mix[1, :, :, SLAB:] = jnp.zeros((8, ROWS, SLABW - SLAB), BF16)
    slabs(flat, wout, mix.at[0], rs1, 0)
    o, m = iota((ROWS, nt), 0), iota((ROWS, nt), 1)
    line = (m // 32) * 8 + m % 8
    chosen = (line - 12 == o % 12) & ((m // 8) % 4 == o // 12)
    hidden = jnp.dot(
        jnp.where(chosen, 1.0, 0.0).astype(BF16),
        extra[:, :SLABW],
        preferred_element_type=F32,
    )
    finish(("spread", 0))
    for j in range(8):
        hidden = hidden + rs1[j].astype(F32)
    lane = iota((ROWS, SLABW), 1)
    hidden = jnp.where(lane < SLAB, hidden, 0.0)
    square = jnp.sum(hidden * hidden, axis=1, keepdims=True)
    high = square.astype(BF16).astype(F32)
    low = square - high
    packed = jnp.where(
        lane < SLAB, hidden * gain_slab[...], jnp.where(lane < SLAB + 32, high, low)
    ).astype(BF16)
    agout[...] = packed
    spread(lambda to: agout, ag, 1)
    ag[t] = packed

    o, m = iota((64, ROWS), 0), iota((64, ROWS), 1)

    def placed(chosen, columns):
        return jnp.dot(
            jnp.where((o // 16 == m // 12) & chosen, 1.0, 0.0).astype(BF16),
            columns,
            preferred_element_type=F32,
        )

    rounded = hidden.astype(BF16)
    wide = placed(o % 16 == m % 12, rounded[:, :RET])
    rest = [
        placed(o % 16 - 12 + 4 * r == m % 12, rounded[:, RET:SLAB]) for r in range(3)
    ]
    rest = jnp.concatenate(rest + [jnp.zeros((64, RET - 192), F32)], axis=1)
    lower = iota((64, RET), 0) % 16 >= 12
    block = jnp.where(lower, rest, wide).astype(BF16)
    for i in range(12):
        home_out[i] = block[16 * (i // 3) : 16 * (i // 3) + 16, 128 * (i % 3) : 128 * (i % 3 + 1)]
        copy = pltpu.make_async_remote_copy(
            src_ref=home_out.at[i],
            dst_ref=home_mid.at[g],
            send_sem=bsend.at[i],
            recv_sem=brecv.at[0],
            device_id={"grp": i},
            device_id_type=MESH,
        )

        @pl.when(g != i)
        def _():
            copy.start()

        @pl.when(g == i)
        def _():
            home_mid[g] = home_out[i]

    def home_sent():
        for i in range(12):

            @pl.when(g != i)
            def _():
                drain(home_out.at[i], bsend.at[i])

        @pl.when(g < 12)
        def _():
            drain(home_next.at[pl.ds(0, GROUPS - 1)], bsend.at[12])

    def home_arrived():
        @pl.when(g < 12)
        def _():
            drain(home_in.at[pl.ds(0, 11)], brecv.at[1])

        @pl.when(g >= 12)
        def _():
            drain(home_in.at[pl.ds(0, 12)], brecv.at[1])

    finish(("spread", 1))
    total = jnp.zeros((ROWS, 1), F32)
    gate = jnp.zeros((ROWS, 128), F32)
    upward = jnp.zeros((ROWS, 128), F32)
    for j in range(8):
        block = ag[j]
        total = total + (
            block[:, SLAB : SLAB + 1].astype(F32) + block[:, SLAB + 32 : SLAB + 33].astype(F32)
        )
        at = slice(SLAB * j, SLAB * (j + 1))
        gate = gate + jnp.dot(block[:, :SLAB], wgate[at], preferred_element_type=F32)
        upward = upward + jnp.dot(block[:, :SLAB], wup[at], preferred_element_type=F32)
    factor = lax.rsqrt(total * (1.0 / 3584.0) + EPSILON)
    gate = gate * factor
    upward = upward * factor
    active = (gate / (1.0 + jnp.exp(-gate)) * upward).astype(BF16)

    fin[...] = placed(o % 16 == m % 12, active).astype(BF16).reshape(4, 16, 128)

    def answer(to):
        slot = jnp.where(reads_ref[3, to] == g, 3, 0)
        slot = jnp.where(reads_ref[2, to] == g, 2, slot)
        slot = jnp.where(reads_ref[1, to] == g, 1, slot)
        return fin[slot]

    @pl.loop(1, GROUPS)
    def _(d):
        to = lax.rem(g + d, GROUPS)
        sback[to] = answer(to)
        pltpu.make_async_remote_copy(
            src_ref=sback.at[to],
            dst_ref=rback.at[g],
            send_sem=hsend.at[6],
            recv_sem=hrecv.at[6],
            device_id={"grp": to},
            device_id_type=MESH,
        ).start()

    rback[g] = answer(g)
    pending["return_sent"] = lambda: drain(sback.at[pl.ds(0, GROUPS - 1)], hsend.at[6])
    pending["return"] = lambda: drain(rback.at[pl.ds(0, GROUPS - 1)], hrecv.at[6])

    @pl.when(g < 12)
    def _():
        drain(home_mid.at[pl.ds(0, GROUPS - 1)], brecv.at[0])
        k = g // 3

        @pl.loop(1, GROUPS)
        def _(d):
            to = lax.rem(g + d, GROUPS)
            home_next[to] = home_mid[reads_ref[k, to]]
            pltpu.make_async_remote_copy(
                src_ref=home_next.at[to],
                dst_ref=home_in.at[g],
                send_sem=bsend.at[12],
                recv_sem=brecv.at[1],
                device_id={"grp": to},
                device_id_type=MESH,
            ).start()

        home_in[g] = home_mid[reads_ref[k, g]]

    pending["home_sent"] = home_sent
    pending["home"] = home_arrived
    finish("return")
    o, m = iota((ROWS, 64), 0), iota((ROWS, 64), 1)
    blocks = jnp.concatenate([rback[reads_ref[k, g]] for k in range(4)], axis=0)
    active = jnp.dot(
        jnp.where((o // 12 == m // 16) & (o % 12 == m % 16), 1.0, 0.0).astype(BF16),
        blocks,
        preferred_element_type=F32,
    ).astype(BF16)
    slabs(active, wdown, mix.at[1], rs2, 2)
    finish("home")
    finish(("spread", 2))
    summed = rs2[0].astype(F32)
    for j in range(1, 8):
        summed = summed + rs2[j].astype(F32)
    for k in range(4):
        block = jnp.concatenate([home_in[3 * k + j] for j in range(3)], axis=1).astype(F32)
        for r in range(3):
            at = slice(12 * k + 4 * r, 12 * k + 4 * r + 4)
            out_ref[3 * k + r, :, :RET] = (
                summed[at, :RET] + block[4 * r : 4 * r + 4]
            ).astype(BF16)
            out_ref[3 * k + r, :, RET:] = (
                summed[at, RET:SLAB] + block[12:, 64 * r : 64 * r + 64]
            ).astype(BF16)

    finish()


def on_device(
    pool_pages,
    page_table,
    read_list,
    context,
    queries,
    tail_keys,
    residual,
    w_uv,
    w_out,
    norm_gain,
    w_gate,
    w_up,
    w_down,
):
    smem = pl.BlockSpec(memory_space=pltpu.SMEM)
    vmem = pl.BlockSpec(memory_space=pltpu.VMEM)
    anym = pl.BlockSpec(memory_space=pl.ANY)
    dma = pltpu.SemaphoreType.DMA
    nq = QP * 16
    return pl.pallas_call(
        kernel,
        out_shape=jax.ShapeDtypeStruct((12, 4, SLAB), BF16),
        in_specs=[smem] * 3 + [vmem] * 5 + [anym] * 6,
        out_specs=vmem,
        scratch_shapes=[
            pltpu.VMEM((TILES, NP, 16, 128), BF16),
            pltpu.VMEM((8, 128), jnp.int32),
            pltpu.SMEM((8, 128), jnp.int32),
            pltpu.VMEM((8, 1, 768), F32),
            pltpu.VMEM((1, SLABW), F32),
            pltpu.VMEM((2, GROUPS, 16, 128), BF16),
            pltpu.VMEM((2, GROUPS, 16, 128), BF16),
            pltpu.VMEM((1, GROUPS, 16, 128), BF16),
            pltpu.VMEM((TILES, GROUPS, 16, 128), BF16),
            pltpu.VMEM((TILES, GROUPS, 16, 128), BF16),
            pltpu.VMEM((4, GROUPS, 16, 128), BF16),
            pltpu.VMEM((4, 6, 576, 128), BF16),
            pltpu.VMEM((nq, LATENT), F32),
            pltpu.VMEM((2, 4, HALF, 768), F32),
            pltpu.VMEM((2, HALF, LATENT), BF16),
            pltpu.VMEM((2, HALF, LATENT), BF16),
            pltpu.VMEM((2, 8, HALF), F32),
            pltpu.VMEM((2, 8, HALF), F32),
            pltpu.VMEM((nq, LATENT), BF16),
            pltpu.VMEM((nq, 1024), BF16),
            pltpu.VMEM((8, 512, 128), BF16),
            pltpu.VMEM((1024, 3584), BF16),
            pltpu.VMEM((3584, 128), BF16),
            pltpu.VMEM((3584, 128), BF16),
            pltpu.VMEM((128, 3584), BF16),
            pltpu.VMEM((2, 8, ROWS, SLABW), BF16),
            pltpu.VMEM((8, ROWS, SLABW), BF16),
            pltpu.VMEM((ROWS, SLABW), BF16),
            pltpu.VMEM((8, ROWS, SLABW), BF16),
            pltpu.VMEM((8, ROWS, SLABW), BF16),
            pltpu.VMEM((4, 16, 128), BF16),
            pltpu.VMEM((GROUPS, 16, 128), BF16),
            pltpu.VMEM((GROUPS, 16, 128), BF16),
            pltpu.VMEM((12, 16, 128), BF16),
            pltpu.VMEM((GROUPS, 16, 128), BF16),
            pltpu.VMEM((GROUPS, 16, 128), BF16),
            pltpu.VMEM((12, 16, 128), BF16),
            dma((7,)),
            dma((4,)),
            dma((4,)),
            dma((7,)),
            dma((7,)),
            dma((6,)),
            dma((6,)),
            dma((3,)),
            dma((3,)),
            dma((13,)),
            dma((2,)),
        ],
        compiler_params=pltpu.CompilerParams(
            collective_id=0, has_side_effects=True, vmem_limit_bytes=56 * 1024 * 1024
        ),
    )(
        read_list.T,
        page_table,
        context,
        read_list.T,
        queries,
        tail_keys,
        residual,
        norm_gain,
        pool_pages.reshape(6, 128, 576).transpose(0, 2, 1),
        w_uv,
        w_out,
        w_gate,
        w_up,
        w_down,
    )


def solution(mesh):
    placed = (
        P("grp", "tp", None, None),
        P(),
        P(),
        P("grp"),
        P("grp", None, "tp", None),
        P("grp", None, None),
        P("grp", None, None),
        P("tp", None, None),
        P("tp", None),
        P(),
        P(None, "tp"),
        P(None, "tp"),
        P("tp", None),
    )
    return jax.shard_map(
        on_device, mesh=mesh, in_specs=placed, out_specs=P("grp", None, "tp"), check_vma=False
    )
```
